32 devices in a mesh: dp: 16 (over z, x, core), tensor: 2 (over y).
Axes of the slice: x: 2, y: 2, z: 4, core: 2. Of those that a mesh axis runs over, the one named last changes fastest.
Arguments:
- tokens: bfloat16 [18912, 768], P(('dp', 'tensor')), may hold values from -6 to 6
- patch_mask: int32 [18912], P(('dp', 'tensor')), may hold values from 0 to 1, as said below
- mask_token: float32 [768], replicated, may hold values from -5 to 5
- norm1_gain: float32 [768], replicated, may hold values from 0.1 to 1.9
- norm1_shift: float32 [768], replicated, may hold values from -3 to 3
- w_qkv: bfloat16 [3, 768, 768], P(None, None, 'tensor'), may hold values from -0.21875 to 0.21875
- qv_bias: float32 [2, 768], P(None, 'tensor'), may hold values from -3 to 3
- w_proj: bfloat16 [768, 768], P('tensor'), may hold values from -0.875 to 0.875
- proj_bias: float32 [768], replicated, may hold values from -3 to 3
- layer_scales: float32 [2, 768], replicated, may hold values from 0.5 to 1.5
- norm2_gain: float32 [768], replicated, may hold values from 0.1 to 1.9
- norm2_shift: float32 [768], replicated, may hold values from -3 to 3
- w_up: bfloat16 [768, 3072], P(None, 'tensor'), may hold values from -0.21875 to 0.21875
- up_bias: float32 [3072], P('tensor'), may hold values from -3 to 3
- w_down: bfloat16 [3072, 768], P('tensor'), may hold values from -0.109375 to 0.109375
- down_bias: float32 [768], replicated, may hold values from -3 to 3
- cotangent: bfloat16 [18912, 768], P(('dp', 'tensor')), may hold values from -6 to 6
Outputs:
- output: bfloat16 [18912, 768], P(('dp', 'tensor'))
- grad_tokens: bfloat16 [18912, 768], P(('dp', 'tensor'))
- grad_mask_token: float32 [768], replicated
- grad_norm1_gain: float32 [768], replicated
- grad_norm1_shift: float32 [768], replicated
- grad_w_qkv: float32 [3, 768, 768], P(None, None, 'tensor')
- grad_qv_bias: float32 [2, 768], P(None, 'tensor')
- grad_w_proj: float32 [768, 768], P('tensor')
- grad_proj_bias: float32 [768], replicated
- grad_layer_scales: float32 [2, 768], replicated
- grad_norm2_gain: float32 [768], replicated
- grad_norm2_shift: float32 [768], replicated
- grad_w_up: float32 [768, 3072], P(None, 'tensor')
- grad_up_bias: float32 [3072], P('tensor')
- grad_w_down: float32 [3072, 768], P('tensor')
- grad_down_bias: float32 [768], replicated
The draws below stay inside these ranges and needn't reach their ends.
Inputs may be any that keep to these rules, and one draw needn't show every extreme that they name: `patch_mask`: row 0 of each image (its class row) is 0; of the other 196 rows of an image, between (392) // 5 + 1 and (784) // 5 are 1.
All inputs are finite; a program needn't handle non-finite values.
Results may differ from the reference program's by a relative error of at most 0.017.
Values may be sent and summed in bfloat16 or wider, within the bound.
A program may use at most 192 MiB of HBM per device.

```python
import math
import jax
import jax.numpy as jnp
from jax import lax

D = 768
HEADS = 12
HD = 64
FF = 3072
L = 197
IMAGES = 96
TOKENS = 18912


def draw_patch_mask(key, part):
    image_keys = jax.random.split(key, IMAGES)
    lowest = 2 * (L - 1) // 5 + 1
    highest = 4 * (L - 1) // 5

    def one_image(image_key):
        count_key, order_key = jax.random.split(image_key)
        masked_count = jax.random.randint(count_key, (), lowest, highest + 1)
        order = jax.random.permutation(order_key, L - 1)
        patches = (order < masked_count).astype(jnp.int32)
        return jnp.concatenate([jnp.zeros((1,), jnp.int32), patches])
    return jax.vmap(one_image)(image_keys).reshape(-1)


def level_of(rng, extent, cuts, smallest, high):
    loudness, own = 1.0, jax.random.fold_in(rng, 6)
    for axis_at, shards_of in cuts:
        heights = jnp.exp(jax.random.uniform(jax.random.fold_in(own, axis_at), (shards_of,), jnp.float32, smallest / len(cuts), high / len(cuts)))
        loudness = loudness * jnp.repeat(heights, extent[axis_at] // shards_of).reshape([-1 if axis == axis_at else 1 for axis in range(len(extent))])
    return loudness


def bell_draw(own_key, shape, spread, limit, cuts=(), kind=jnp.bfloat16):
    values = spread * jax.random.normal(own_key, shape, jnp.float32)
    if cuts:
        values = values * level_of(own_key, shape, cuts, -0.22, 0.18)
    return jnp.clip(values, -limit, limit).astype(kind)


def setup_inputs(seed: int = 0) -> dict:
    key_list = jax.random.split(jax.random.key(seed), 18)
    return {
        "tokens": bell_draw(key_list[0], (TOKENS, D), 1.0, 6.0, ((0, 32),)),
        "patch_mask": draw_patch_mask(jax.random.fold_in(key_list[17], 71), 0),
        "mask_token": bell_draw(key_list[2], (D,), 1.0, 5.0, (), jnp.float32),
        "norm1_gain": jnp.clip(1.0 + 0.18 * jax.random.normal(key_list[3], (D,), jnp.float32), 0.1, 1.9),
        "norm1_shift": bell_draw(key_list[4], (D,), 0.5, 3.0, (), jnp.float32),
        "w_qkv": bell_draw(key_list[5], (3, D, D), D ** -0.5, 0.21875, ((2, 2),)),
        "qv_bias": bell_draw(key_list[6], (2, D), 0.5, 3.0, ((1, 2),), jnp.float32),
        "w_proj": bell_draw(key_list[7], (D, D), (D // 16) ** -0.5, 0.875, ((0, 2),)),
        "proj_bias": bell_draw(key_list[8], (D,), 0.5, 3.0, (), jnp.float32),
        "layer_scales": jnp.clip(jax.random.uniform(key_list[9], (2, D), jnp.float32, 0.5, 1.5), 0.5, 1.5),
        "norm2_gain": jnp.clip(1.0 + 0.18 * jax.random.normal(key_list[10], (D,), jnp.float32), 0.1, 1.9),
        "norm2_shift": bell_draw(key_list[11], (D,), 0.5, 3.0, (), jnp.float32),
        "w_up": bell_draw(key_list[12], (D, FF), D ** -0.5, 0.21875, ((1, 2),)),
        "up_bias": bell_draw(key_list[13], (FF,), 0.5, 3.0, ((0, 2),), jnp.float32),
        "w_down": bell_draw(key_list[14], (FF, D), FF ** -0.5, 0.109375, ((0, 2),)),
        "down_bias": bell_draw(key_list[15], (D,), 0.5, 3.0, (), jnp.float32),
        "cotangent": bell_draw(key_list[16], (TOKENS, D), 1.0, 6.0, ((0, 32),)),
    }


@jax.custom_vjp
def low(v):
    return lax.optimization_barrier(v.astype(jnp.bfloat16)).astype(jnp.float32)

@jax.custom_vjp
def low_back(v):
    return v

def low_keep(v):
    return (low(v), None)

def low_pass(kept, grad):
    return (grad,)

def back_keep(v):
    return (v, None)

def back_low(kept, grad):
    return (low(grad),)
low.defvjp(low_keep, low_pass)
low_back.defvjp(back_keep, back_low)
EPS = 1e-06
HIGH = lax.Precision.HIGHEST
INV_ROOT2 = 0.7071067811865476

def layer_norm(rows, gain, shift):
    row_mean = lax.optimization_barrier(jnp.mean(rows, axis=-1, keepdims=True))
    centred = rows - row_mean
    variance = lax.optimization_barrier(jnp.mean(centred * centred, axis=-1, keepdims=True))
    return centred * lax.rsqrt(variance + EPS) * gain + shift

def gelu_exact(values_in):
    return 0.5 * values_in * (1.0 + lax.erf(values_in * INV_ROOT2))

def group_forward(params, rows_in, mask_rows):
    mask_token, norm1_gain, norm1_shift, w_qkv, qv_bias, w_proj, proj_bias, layer_scales, norm2_gain, norm2_shift, w_up, up_bias, w_down, down_bias = params
    images = rows_in.shape[0] // L
    mixed = jnp.where((mask_rows == 1)[:, None], mask_token[None, :], rows_in)
    normed1 = low(layer_norm(mixed, norm1_gain, norm1_shift))
    project = jnp.einsum('rd,pde->pre', normed1, w_qkv, precision=HIGH)
    queries = low_back(low((project[0] + qv_bias[0]) * 0.125))
    keys_all = low_back(low(project[1]))
    values = low_back(low(project[2] + qv_bias[1]))
    shape_four = (images, L, HEADS, HD)
    scores = low_back(jnp.einsum('bqhe,bkhe->bhqk', queries.reshape(shape_four), keys_all.reshape(shape_four), precision=HIGH))
    top_score = lax.optimization_barrier(jnp.max(scores, axis=-1, keepdims=True))
    exponent = jnp.exp(scores - top_score)
    probs = low(exponent / lax.optimization_barrier(jnp.sum(exponent, axis=-1, keepdims=True)))
    heads_mix = jnp.einsum('bhqk,bkhe->bqhe', probs, values.reshape(shape_four), precision=HIGH)
    heads_out = low_back(low(heads_mix.reshape(-1, D)))
    branch1 = low_back(jnp.dot(heads_out, w_proj, precision=HIGH) + proj_bias)
    middle = mixed + layer_scales[0] * branch1
    normed2 = low(layer_norm(middle, norm2_gain, norm2_shift))
    hidden_pre = low_back(jnp.dot(normed2, w_up, precision=HIGH) + up_bias)
    hidden_act = low(gelu_exact(hidden_pre))
    branch2 = low_back(jnp.dot(hidden_act, w_down, precision=HIGH) + down_bias)
    return middle + layer_scales[1] * branch2

def reference(tokens, patch_mask, mask_token, norm1_gain, norm1_shift, w_qkv, qv_bias, w_proj, proj_bias, layer_scales, norm2_gain, norm2_shift, w_up, up_bias, w_down, down_bias, cotangent):
    batch_images = math.gcd(IMAGES, 16)
    params = (mask_token, norm1_gain, norm1_shift, w_qkv.astype(jnp.float32), qv_bias, w_proj.astype(jnp.float32), proj_bias, layer_scales, norm2_gain, norm2_shift, w_up.astype(jnp.float32), up_bias, w_down.astype(jnp.float32), down_bias)
    rows_in = tokens.astype(jnp.float32)
    mask_groups = patch_mask.reshape(-1, batch_images * L)

    def forward(rows_all, weights):
        grouped = rows_all.reshape(-1, batch_images * L, D)

        def one_group(pair):
            return group_forward(weights, pair[0], pair[1])
        return lax.map(jax.checkpoint(one_group), (grouped, mask_groups)).reshape(-1, D)
    output, pullback = jax.vjp(forward, rows_in, params)
    weighted = cotangent.astype(jnp.float32) * patch_mask[:, None].astype(jnp.float32)
    grad_rows, grads = pullback(weighted)
    return (output.astype(jnp.bfloat16), grad_rows.astype(jnp.bfloat16), grads[0], grads[1], grads[2], grads[3], grads[4], grads[5], grads[6], grads[7], grads[8], grads[9], grads[10], grads[11], grads[12], grads[13])
```

```python
import functools

import jax
import jax.numpy as jnp
from jax import lax
from jax.experimental import pallas as pl
from jax.experimental.pallas import tpu as pltpu
from jax.sharding import PartitionSpec as P

MESH = pl.DeviceIdType.MESH
F32 = jnp.float32
BF16 = jnp.bfloat16
L = 197
LP = 208
D = 768
EPS = 1e-06
INV_ROOT2 = 0.7071067811865476
INV_ROOT2PI = 0.3989422804014327

MTOK, N1G, N1S, PB, LS0, LS1, N2G, N2S, DB, QVO, UPO, QVX, UPX = (
    0, 1, 2, 3, 4, 5, 6, 7, 8, 9, 10, 12, 13)
NSUM = 9
NVEC = 16


def dot(a, b):
    return lax.dot_general(a, b, (((1,), (0,)), ((), ())), preferred_element_type=F32)


def dot_nt(a, b):
    return lax.dot_general(a, b, (((1,), (1,)), ((), ())), preferred_element_type=F32)


def fold(x):
    return jnp.sum(x.reshape(x.shape[0] // 8, 8, x.shape[1]), axis=0)


def normed(rows):
    centred = rows - jnp.mean(rows, axis=-1, keepdims=True)
    inverse = lax.rsqrt(jnp.mean(centred * centred, axis=-1, keepdims=True) + EPS)
    return centred * inverse, inverse


def norm_back(grad, gain, scaled, inverse):
    weighted = grad * gain
    inner = (
        weighted
        - jnp.mean(weighted, axis=-1, keepdims=True)
        - scaled * jnp.mean(weighted * scaled, axis=-1, keepdims=True)
    )
    return inverse * inner


def wide(column):
    return jnp.concatenate([column] * (D // 128), axis=1)


BLOCKS = ((0, 48), (48, 48), (96, 48), (144, 48), (192, 16))


VECTORS = ("mtok", "n1g", "n1s", "pb", "n2g", "n2s", "db")


class Layer:
    def __init__(self, r, rows):
        self.__dict__.update(r)
        self.rows = rows
        self.images = rows // L
        self.padded = self.images * LP

    def widen(self, src):
        n = self.rows // 16

        @pl.loop(0, n)
        def _(b):
            at = pl.ds(pl.multiple_of(b * 16, 16), 16)
            self.t32[at, :] = src[at, :].astype(F32)

        left = self.rows - n * 16
        if left:
            self.t32[n * 16 : self.rows, :] = src[n * 16 : self.rows, :].astype(F32)

    def narrow(self, src, dst):
        for i in range(self.images):
            for r, n in BLOCKS:
                n = min(n, L - r)
                self.t32[pl.ds(L * i + r, n), :] = src[pl.ds(LP * i + r, n), :].astype(F32)
        n = self.rows // 16

        @pl.loop(0, n)
        def _(b):
            at = pl.ds(pl.multiple_of(b * 16, 16), 16)
            dst[at, :] = self.t32[at, :].astype(BF16)

        left = self.rows - n * 16
        if left:
            dst[n * 16 : self.rows, :] = self.t32[n * 16 : self.rows, :].astype(BF16)

    def row_loop(self, body):
        @pl.loop(0, self.padded // 48)
        def _(b):
            body(pl.ds(pl.multiple_of(b * 48, 48), 48))

    def acc(self, at, x):
        self.vacc[pl.ds(at * 8, 8), :] += fold(x)

    def vectors(self):
        for name in ("mtok", "n1g", "n1s", "pb", "n2g", "n2s", "db"):
            self.__dict__[name] = self.rows8.at[pl.ds(VECTORS.index(name), 1), :]
            self.rows8[VECTORS.index(name), :] = self.__dict__["in_" + name][...]

    def start(self):
        self.vacc[...] = jnp.zeros_like(self.vacc)
        rows = self.rows
        self.mrow[...] = jnp.zeros_like(self.mrow)
        flags = jnp.where(self.mask[...] == 1, 1.0, 0.0).astype(F32)[None, :]
        self.mrow[:, pl.ds(0, rows)] = jnp.broadcast_to(flags, (128, rows))
        self.mcol[...] = jnp.transpose(self.mrow[...])
        self.t32[pl.ds(rows, self.t32.shape[0] - rows), :] = jnp.zeros(
            (self.t32.shape[0] - rows, D), F32)
        self.widen(self.tok)
        for i in range(self.images):
            for r, n in BLOCKS:
                at = pl.ds(L * i + r, n)
                to = pl.ds(LP * i + r, n)
                x = self.t32[at, :]
                mk = self.mcol[at, :]
                mx = jnp.where(wide(mk) > 0.5, self.mtok[...], x)
                if r + n > L:
                    keep = lax.broadcasted_iota(jnp.int32, (n, 128), 0) < L - r
                    mk = jnp.where(keep, mk, 0.0)
                    mx = jnp.where(wide(keep), mx, 0.0)
                self.maskp[to, :] = mk
                self.mixed[to, :] = mx
                sc, _ = normed(mx)
                self.n1[to, :] = (sc * self.n1g[...] + self.n1s[...]).astype(BF16)

    def start2(self):
        self.n1t[...] = jnp.transpose(self.n1[...])
        self.widen(self.cot)
        for i in range(self.images):
            for r, n in BLOCKS:
                at = pl.ds(L * i + r, n)
                to = pl.ds(LP * i + r, n)
                go = self.t32[at, :] * wide(self.maskp[to, :])
                self.gout[to, :] = go.astype(BF16)
                self.gb[to, :] = (self.ls[1:2, :] * go).astype(BF16)

    def w_pair(self, j, h):
        return jnp.concatenate(
            [self.g_at[j, h, pl.ds(p * D, D), :] for p in range(3)], axis=1)

    def qkv(self, j, h):
        t = h * 3 + j
        proj = dot(self.n1[...], self.w_pair(j, h))
        qb = self.qb[pl.ds(t, 1), :]
        vb = self.qb[pl.ds(8 + t, 1), :]
        self.q[t] = ((proj[:, 0:128] + qb) * 0.125).astype(BF16)
        self.k[t] = proj[:, 128:256].astype(BF16)
        self.v[t] = (proj[:, 256:384] + vb).astype(BF16)

    def two(self, x):
        low = lax.broadcasted_iota(jnp.int32, x.shape, 1) < 64
        zero = jnp.zeros_like(x)
        return jnp.where(low, x, zero), jnp.where(low, zero, x)

    def attend(self, t):
        for i in range(self.images):
            at = pl.ds(i * LP, LP)
            q0, q1 = self.two(self.q[t, at, :])
            k = self.k[t, at, :]
            vt = jnp.transpose(self.v[t, at, :])
            outs = []
            for e, qe in enumerate((q0, q1)):
                s = dot_nt(k, qe)
                s = jnp.where(lax.broadcasted_iota(jnp.int32, s.shape, 0) < L, s, -1e30)
                x = jnp.exp(s - jnp.max(s, axis=0, keepdims=True))
                p = (x * (1.0 / jnp.sum(x, axis=0, keepdims=True))).astype(BF16)
                self.pt[(t * self.images + i) * 2 + e] = p
                outs.append(dot(vt[e * 64 : e * 64 + 64, :], p))
            ot = jnp.concatenate(outs, axis=0).astype(BF16)
            self.hot[i, pl.ds(pl.multiple_of(t * 128, 128), 128), :] = ot
            self.ho[t, at, :] = jnp.transpose(ot)

    def w_proj(self):
        return jnp.concatenate(
            [
                jnp.concatenate(
                    [self.g_at[3, h, pl.ds(b * 384, 384), :] for b in range(6)], axis=1)
                for h in range(2)
            ],
            axis=0,
        )

    def project(self):
        @pl.loop(0, self.images)
        def _(i):
            at = pl.ds(pl.multiple_of(i * LP, 16), LP)
            o = jnp.concatenate([self.ho[t, at, :] for t in range(6)], axis=1)
            self.br1[at, :] = dot(o, self.w_proj()) + self.pb[...]

    def second_norm(self):
        def body(at):
            middle = self.mixed[at, :] + self.ls[0:1, :] * self.br1[at, :]
            sc, _ = normed(middle)
            self.n2[at, :] = (sc * self.n2g[...] + self.n2s[...]).astype(BF16)
            self.br2[at, :] = jnp.zeros((48, D), F32)
            self.gn2[at, :] = jnp.zeros((48, D), F32)

        self.row_loop(body)
        self.n2t[...] = jnp.transpose(self.n2[...])

    def feed(self, j, h):
        wd = jnp.concatenate(
            [self.g_ff[j, h, pl.ds(b * 256, 256), :] for b in range(6)], axis=1)
        wu = jnp.concatenate(
            [self.g_ff[j, h, pl.ds(1536 + b * D, D), :] for b in range(2)], axis=1)
        row = h * 6 + j
        pre = dot(self.n2[...], wu) + self.ub[pl.ds(row, 1), :]
        cdf = 0.5 * (1.0 + lax.erf(pre * INV_ROOT2))
        act = (pre * cdf).astype(BF16)
        slope = cdf + pre * jnp.exp(-0.5 * pre * pre) * INV_ROOT2PI
        gp32 = dot_nt(self.gb[...], wd) * slope
        gp = gp32.astype(BF16)
        self.uba[row] = fold(gp.astype(F32))
        self.br2[...] += dot(act, wd)
        self.gn2[...] += dot_nt(gp, wu)
        gwd = dot(jnp.transpose(act), self.gb[...]).astype(BF16)
        gwu = dot(self.n2t[...], gp).astype(BF16)
        for b in range(6):
            self.g_ff[j, h, pl.ds(b * 256, 256), :] = gwd[:, b * 128 : b * 128 + 128]
        for b in range(2):
            self.g_ff[j, h, pl.ds(1536 + b * D, D), :] = gwu[:, b * 128 : b * 128 + 128]

    def middle_back(self):
        ls0, ls1 = self.ls[0:1, :], self.ls[1:2, :]

        def body(at):
            b1 = self.br1[at, :]
            middle = self.mixed[at, :] + ls0 * b1
            sc, inv = normed(middle)
            b2 = self.br2[at, :] + self.db[...]
            self.outp[at, :] = (middle + ls1 * b2).astype(BF16)
            self.br2[at, :] = jnp.zeros((48, D), F32)
            go = self.gout[at, :].astype(F32)
            self.acc(LS1, go * b2)
            self.acc(DB, self.gb[at, :].astype(F32))
            g = self.gn2[at, :]
            self.acc(N2G, g * sc)
            self.acc(N2S, g)
            gm = go + norm_back(g, self.n2g[...], sc, inv)
            self.acc(LS0, gm * b1)
            gb1 = (ls0 * gm).astype(BF16)
            self.gb[at, :] = gb1
            self.acc(PB, gb1.astype(F32))
            self.gn2[at, :] = gm

        self.row_loop(body)

    def output(self):
        self.narrow(self.outp, self.out)

    def proj_back(self):
        @pl.loop(0, self.images)
        def _(i):
            at = pl.ds(pl.multiple_of(i * LP, 16), LP)
            gh = dot_nt(self.gb[at, :], self.w_proj()).astype(BF16)
            for t in range(6):
                self.ho[t, at, :] = gh[:, t * 128 : t * 128 + 128]

    def proj_grad(self, h):
        total = sum(
            dot(self.hot[i, pl.ds(h * 384, 384), :], self.gb[pl.ds(i * LP, LP), :])
            for i in range(self.images))
        for b in range(6):
            self.g_at[3, h, pl.ds(b * 384, 384), :] = total[
                :, b * 128 : b * 128 + 128].astype(BF16)

    def attend_back(self, t):
        for i in range(self.images):
            at = pl.ds(i * LP, LP)
            q0, q1 = self.two(self.q[t, at, :])
            d0, d1 = self.two(self.ho[t, at, :])
            k = self.k[t, at, :]
            v = self.v[t, at, :]
            kt = jnp.transpose(k)
            dq, dk, dv = [], 0.0, 0.0
            for e, (qe, de) in enumerate(((q0, d0), (q1, d1))):
                pb = self.pt[(t * self.images + i) * 2 + e]
                p = pb.astype(F32)
                gp = dot_nt(v, de)
                gs = (p * (gp - jnp.sum(gp * p, axis=0, keepdims=True))).astype(BF16)
                dv = dv + dot(pb, de)
                dk = dk + dot(gs, qe)
                dq.append(dot(kt[e * 64 : e * 64 + 64, :], gs))
            dq = jnp.transpose(jnp.concatenate(dq, axis=0)) * 0.125
            self.dqkv[at, 0:128] = dq.astype(BF16)
            self.dqkv[at, 128:256] = dk.astype(BF16)
            self.dqkv[at, 256:384] = dv.astype(BF16)
        self.qa[t] = fold(self.dqkv[:, 0:128].astype(F32))
        self.qa[8 + t] = fold(self.dqkv[:, 256:384].astype(F32))

    def qkv_back(self, j, h):
        self.br2[...] += dot_nt(self.dqkv[...], self.w_pair(j, h))
        grad = dot(self.n1t[...], self.dqkv[...])
        for p in range(3):
            self.g_at[j, h, pl.ds(p * D, D), :] = grad[
                :, p * 128 : p * 128 + 128].astype(BF16)

    def first_back(self):
        def body(at):
            sc, inv = normed(self.mixed[at, :])
            g = self.br2[at, :]
            self.acc(N1G, g * sc)
            self.acc(N1S, g)
            gx = self.gn2[at, :] + norm_back(g, self.n1g[...], sc, inv)
            mk = wide(self.maskp[at, :]) > 0.5
            self.acc(MTOK, jnp.where(mk, gx, 0.0))
            self.br2[at, :] = jnp.where(mk, 0.0, gx)

        self.row_loop(body)

    def sums(self, vec):
        vec[...] = jnp.zeros_like(vec)
        for s in range(NSUM):
            vec[s : s + 1, :] = jnp.sum(
                self.vacc[pl.ds(s * 8, 8), :], axis=0, keepdims=True)
        for h, (qv, up) in enumerate(((QVO, UPO), (QVX, UPX))):
            for w in range(2):
                for j in range(3):
                    c = w * 384 + j * 128
                    vec[qv : qv + 1, c : c + 128] = jnp.sum(
                        self.qa[8 * w + h * 3 + j], axis=0, keepdims=True)
            for j in range(6):
                c = j % 3 * 256
                vec[up + j // 3 : up + j // 3 + 1, c : c + 256] = jnp.sum(
                    self.uba[h * 6 + j], axis=0, keepdims=True)


def layer_scratch(rows):
    n = rows // L
    padded = n * LP
    v = pltpu.VMEM
    return dict(
        t32=v(((rows + 11 + 15) // 16 * 16 + 0, D), F32),
        mrow=v((128, (rows + 127) // 128 * 128), F32),
        mcol=v(((rows + 127) // 128 * 128, 128), F32),
        maskp=v((padded, 128), F32),
        mixed=v((padded, D), F32),
        gout=v((padded, D), BF16),
        n1=v((padded, D), BF16),
        n1t=v((D, padded), BF16),
        q=v((6, padded, 128), BF16),
        k=v((6, padded, 128), BF16),
        v=v((6, padded, 128), BF16),
        pt=v((6 * n * 2, LP, LP), BF16),
        ho=v((6, padded, 128), BF16),
        hot=v((n, D, LP), BF16),
        br1=v((padded, D), F32),
        n2=v((padded, D), BF16),
        n2t=v((D, padded), BF16),
        gb=v((padded, D), BF16),
        outp=v((padded, D), BF16),
        br2=v((padded, D), F32),
        gn2=v((padded, D), F32),
        dqkv=v((padded, 384), BF16),
        rows8=v((8, D), F32),
        vacc=v((NSUM * 8, D), F32),
        qb=v((16, 128), F32),
        ub=v((12, 256), F32),
        qa=v((16, 8, 128), F32),
        uba=v((12, 8, 256), F32),
    )


FF_ROWS, AT_ROWS = 3072, 2304
CHUNKS = tuple([("g_ff", j, FF_ROWS) for j in range(6)] + [("g_at", j, AT_ROWS) for j in range(4)])


def plan_of(n, bits):
    rows, steps = n // 2, []
    for b in range(1, bits):
        if rows // 2 % 16 == 0:
            rows //= 2
            steps.append((b, rows, True))
        else:
            steps.append((b, rows, False))
    return steps


def land_offsets(bits):
    at, table = 0, {}
    for k, (_, _, n) in enumerate(CHUNKS):
        table[k, "y"] = at
        at += n // 2
        for b, rows, _ in plan_of(n, bits):
            table[k, b] = at
            at += rows
    return table, at


class Links:
    def __init__(self, r, bits):
        self.__dict__.update(r)
        self.bits = bits
        self.dp = lax.axis_index("dp")
        self.half = lax.axis_index("tensor")
        self.bit = [(self.dp // (1 << b)) % 2 for b in range(bits)]
        self.offsets, _ = land_offsets(bits)

    def peer(self, way):
        if way == "y":
            return (self.dp, 1 - self.half)
        return (self.dp + (1 << way) * (1 - 2 * self.bit[way]), self.half)

    def greet(self):
        barrier = pltpu.get_barrier_semaphore()
        ways = ["y"] + list(range(self.bits))
        for way in ways:
            pl.semaphore_signal(barrier, inc=1, device_id=self.peer(way), device_id_type=MESH)
        pl.semaphore_wait(barrier, len(ways))

    def copy(self, src, dst, send, recv, way):
        return pltpu.make_async_remote_copy(
            src_ref=src, dst_ref=dst, send_sem=send, recv_sem=recv,
            device_id=self.peer(way), device_id_type=MESH)

    def load(self, k):
        name, j, n = CHUNKS[k]
        sem = self.load_sem.at[k]
        if name == "g_ff":
            for b in range(6):
                pltpu.make_async_copy(
                    self.w_dn.at[pl.ds(j * 256, 256), pl.ds(b * 128, 128)],
                    self.g_ff.at[j, 0, pl.ds(b * 256, 256)], sem).start()
            for b in range(2):
                pltpu.make_async_copy(
                    self.w_up.at[:, pl.ds(j * 256 + b * 128, 128)],
                    self.g_ff.at[j, 0, pl.ds(1536 + b * D, D)], sem).start()
        elif j < 3:
            for p in range(3):
                pltpu.make_async_copy(
                    self.w_qkv.at[p, :, pl.ds(j * 128, 128)],
                    self.g_at.at[j, 0, pl.ds(p * D, D)], sem).start()
        else:
            for b in range(6):
                pltpu.make_async_copy(
                    self.w_pr.at[:, pl.ds(b * 128, 128)],
                    self.g_at.at[3, 0, pl.ds(b * 384, 384)], sem).start()

    def loaded(self, k):
        name, j, n = CHUNKS[k]
        ref = getattr(self, name).at[j, 0]
        pltpu.make_async_copy(ref, ref, self.load_sem.at[k]).wait()

    def bias(self, stage):
        a = self.copy(self.qvb, self.qvbx, self.b_send.at[0], self.b_recv.at[0], "y")
        b = self.copy(self.upb, self.upbx, self.b_send.at[1], self.b_recv.at[1], "y")
        if stage == 0:
            a.start()
            b.start()
            return
        a.wait()
        b.wait()
        for h, (qv, up) in enumerate(((self.qvb, self.upb), (self.qvbx, self.upbx))):
            for j in range(3):
                for w in range(2):
                    row = 8 * w + h * 3 + j
                    self.qb[row : row + 1, :] = qv[w : w + 1, j * 128 : j * 128 + 128]
            for j in range(6):
                row = h * 6 + j
                self.ub[row : row + 1, :] = up[pl.ds(j * 256, 256)][None, :]

    def gather_copies(self, k):
        name, j, n = CHUNKS[k]
        ref = getattr(self, name)
        piece = n // 16
        core, b1, b2 = self.bit[0], self.bit[1], self.bit[2]
        base = core * (n // 2)

        def make(i, half, off, rows, way):
            def build():
                at = pl.ds(pl.multiple_of(off, 16), rows)
                return self.copy(
                    ref.at[j, half, at], ref.at[j, 1, at],
                    self.w_send.at[k, i], self.w_recv.at[k, i], way)

            return build

        p0 = base + (b2 * 2 + b1) * piece
        p1 = base + n // 4 + (b1 * 2 + b2) * piece
        return [
            make(0, 0, p0, piece, "y"),
            make(1, 0, p1, piece, "y"),
            make(2, 1, p0, piece, 1),
            make(3, 1, p1, piece, 2),
            make(4, 1, base + b2 * 2 * piece, 2 * piece, 2),
            make(5, 1, base + n // 4 + b1 * 2 * piece, 2 * piece, 1),
            make(6, 1, base, n // 2, 0),
        ]

    def gather(self, k, stage):
        c = self.gather_copies(k)
        if stage == 0:
            self.loaded(k)
            c[0]().start()
            c[1]().start()
        elif stage == 1:
            c[0]().wait_recv()
            c[2]().start()
            c[1]().wait_recv()
            c[3]().start()
        elif stage == 2:
            c[2]().wait_recv()
            c[4]().start()
            c[3]().wait_recv()
            c[5]().start()
        elif stage == 3:
            c[4]().wait_recv()
            c[5]().wait_recv()
            c[6]().start()
        elif stage == 4:
            c[6]().wait_recv()
        else:
            for one in c:
                one().wait_send()

    def add(self, dst, dst_at, src, src_at, rows):
        size = next(s for s in (256, 192, 144, 128, 112, 96, 80, 64, 48, 32, 16) if rows % s == 0)

        @pl.loop(0, rows // size)
        def _(b):
            to = pl.ds(pl.multiple_of(dst_at + b * size, 16), size)
            of = pl.ds(pl.multiple_of(src_at + b * size, 16), size)
            total = dst[to, :].astype(F32) + src[of, :].astype(F32)
            dst[to, :] = total.astype(BF16)

    def reduce_copies(self, k):
        name, j, n = CHUNKS[k]
        ref = getattr(self, name)
        land1 = self.land_ff if name == "g_ff" else self.land_at
        own, mine = ref.at[j, 0], self.bit[0] * (n // 2)
        out = []

        def add(src, dst, way, adds):
            i = len(out)

            def build():
                return self.copy(src(), dst(), self.r_send.at[k, i], self.r_recv.at[k, i], way)

            out.append((build, adds))

        def rows_of(r, at, rows):
            return lambda: r.at[pl.ds(pl.multiple_of(at, 16), rows)]

        theirs = (1 - self.bit[0]) * (n // 2)
        add(lambda: ref.at[j, :, pl.ds(pl.multiple_of(theirs, 16), n // 2), :],
            lambda: land1.at[j], 0,
            [(ref.at[j, h], mine, land1.at[j, h], 0, n // 2) for h in range(2)])
        o = self.offsets[k, "y"]
        add(rows_of(ref.at[j, 1], mine, n // 2), rows_of(self.land, o, n // 2), "y",
            [(own, mine, self.land, o, n // 2)])
        back = [(0, mine, n // 2)]
        for b, rows, halves in plan_of(n, self.bits):
            o = self.offsets[k, b]
            if halves:
                away = mine + (1 - self.bit[b]) * rows
                mine = mine + self.bit[b] * rows
                back.append((b, mine, rows))
            else:
                away = mine
            add(rows_of(own, away, rows), rows_of(self.land, o, rows), b,
                [(own, mine, self.land, o, rows)])
        for b, at, rows in back[::-1]:
            add(rows_of(own, at, rows), rows_of(own, at, rows), b, [])
        return out

    def result_copy(self, k):
        name, j, n = CHUNKS[k]
        out = self.o_ff if name == "g_ff" else self.o_at
        return pltpu.make_async_copy(
            getattr(self, name).at[j, 0], out.at[j], self.out_sem.at[k])

    def reduce(self, k, stage):
        steps = self.reduce_copies(k)
        if stage > 0:
            build, adds = steps[stage - 1]
            copy = build()
            copy.wait_recv()
            if adds:
                copy.wait_send()
                way = self.way(stage - 1)
                if way != "y" and self.halving(k, stage - 1):
                    pl.semaphore_signal(
                        self.credit.at[k, way], inc=1, device_id=self.peer(way),
                        device_id_type=MESH)
            for dst, dst_at, src, src_at, rows in adds:
                self.add(dst, dst_at, src, src_at, rows)
        if stage < len(steps):
            if not steps[stage][1]:
                pl.semaphore_wait(self.credit.at[k, self.back_way(k, stage)], 1)
            steps[stage][0]().start()
        else:
            self.result_copy(k).start()

    def way(self, step):
        return (0, "y")[step] if step < 2 else step - 1

    def back_way(self, k, step):
        ways = [0] + [b for b, _, halves in plan_of(CHUNKS[k][2], self.bits) if halves]
        return ways[::-1][step - self.bits - 1]

    def halving(self, k, step):
        plan = plan_of(CHUNKS[k][2], self.bits)
        return step < 2 or step - 2 >= len(plan) or plan[step - 2][2]

    def finish(self, k):
        for i, (build, adds) in enumerate(self.reduce_copies(k)):
            if not adds:
                build().wait_send()
        self.result_copy(k).wait()

    def vec_copy(self, s):
        way = self.way(s)
        return self.copy(self.vb.at[s], self.vr.at[s], self.v_send.at[s], self.v_recv.at[s], way)

    def vec(self, stage):
        if stage > 0:
            s = stage - 1
            self.vec_copy(s).wait_recv()
            if s == 1:
                self.vb[2, 0:NSUM, :] = self.vb[1, 0:NSUM, :] + self.vr[1, 0:NSUM, :]
                self.vb[2, QVO:QVX, :] = self.vb[1, QVO:QVX, :] + self.vr[1, QVX : QVX + 3, :]
                self.vb[2, QVX:NVEC, :] = jnp.zeros((NVEC - QVX, D), F32)
            else:
                self.vb[stage] = self.vb[s] + self.vr[s]
        if stage < self.bits + 1:
            self.vec_copy(stage).start()

    def vec_end(self):
        for s in range(self.bits + 1):
            self.vec_copy(s).wait_send()
        self.o_vec[...] = self.vb[self.bits + 1]


def link_scratch(bits):
    v, dma = pltpu.VMEM, pltpu.SemaphoreType.DMA
    steps = 2 * bits + 1
    return dict(
        g_ff=v((6, 2, FF_ROWS, 128), BF16),
        g_at=v((4, 2, AT_ROWS, 128), BF16),
        land_ff=v((6, 2, FF_ROWS // 2, 128), BF16),
        land_at=v((4, 2, AT_ROWS // 2, 128), BF16),
        land=v((land_offsets(bits)[1], 128), BF16),
        qvbx=v((2, 384), F32),
        upbx=v((1536,), F32),
        vb=v((bits + 2, NVEC, D), F32),
        vr=v((bits + 1, NVEC, D), F32),
        load_sem=dma((10,)),
        out_sem=dma((10,)),
        b_send=dma((2,)),
        b_recv=dma((2,)),
        w_send=dma((10, 7)),
        w_recv=dma((10, 7)),
        r_send=dma((10, steps)),
        r_recv=dma((10, steps)),
        credit=pltpu.SemaphoreType.REGULAR((10, bits)),
        v_send=dma((bits + 1,)),
        v_recv=dma((bits + 1,)),
    )


GATHER_ORDER = (6, 7, 8, 9, 0, 1, 2, 3, 4, 5)


def timeline(bits):
    pieces = [("start", 2.2, None)]
    pieces += [(("qa", t, s), (0.6, 1.5)[s], 6 + t - 3 if s == 0 and t >= 3 else None)
               for t in range(3) for s in range(2)]
    pieces += [("start2", 1.5, None)]
    pieces += [(("qa", t, s), (0.6, 1.5)[s], 6 + t - 3 if s == 0 else None)
               for t in range(3, 6) for s in range(2)]
    pieces += [("project", 1.2, 9), ("second_norm", 4.0, None)]
    pieces += [(("feed", u, 0), 1.95, u // 2 if u % 2 == 0 else None) for u in range(12)]
    pieces += [("middle_back", 4.0, None), ("proj_back", 1.0, None),
               ("proj_grad", 1.6, None)]
    pieces += [(("back", u, s), (1.65, 1.4)[s], None) for u in range(6) for s in range(2)]
    pieces += [("first_back", 2.5, None), ("sums", 1.0, None), ("output", 1.5, None), ("tokens", 1.5, None)]
    after = {("feed", 2 * j + 1, 0): j for j in range(6)}
    after["proj_grad"] = 9
    after.update({("back", 2 * j + 1, 1): 6 + j for j in range(3)})

    rate = 91e3 / 2
    free = {}

    def send(now, way, nbytes):
        if way == 0:
            line, took = "c", nbytes / 480e3
        elif way == "y" or way == 1:
            line, took = way, nbytes / rate
        else:
            line, took = "z", nbytes / rate * (2 if way > 2 else 1)
        begin = max(now, free.get(line, 0.0))
        free[line] = begin + took
        return begin + took + 1.7

    steps = 2 * bits + 1
    order, now = [], 3.0
    w_stage, w_ready = {}, {}
    r_stage, r_ready = {}, {}
    v_stage, v_ready = None, 0.0

    def reduce_bytes(k, stage):
        n = CHUNKS[k][2]
        plan = plan_of(n, bits)
        ways = [(0, n * 256), ("y", n * 128)] + [(b, rows * 256) for b, rows, _ in plan]
        ways += [(b, rows * 256) for b, rows, halves in plan[::-1] if halves] + [(0, n * 128)]
        return ways, ways[stage] if stage < len(ways) else None

    def gather_step(k):
        nonlocal now
        s = w_stage[k]
        n = CHUNKS[k][2]
        piece = n // 16 * 256
        order.append(("w", k, s))
        now = max(now, w_ready[k]) + 0.25
        if s == 0:
            w_ready[k] = send(now, "y", 2 * piece)
        elif s == 1:
            w_ready[k] = max(send(now, 1, piece), send(now, 2, piece))
        elif s == 2:
            w_ready[k] = max(send(now, 2, 2 * piece), send(now, 1, 2 * piece))
        elif s == 3:
            w_ready[k] = send(now, 0, n // 2 * 256)
        else:
            w_ready[k] = now
        w_stage[k] = s + 1

    def reduce_step(k):
        nonlocal now
        s = r_stage[k]
        ways, this = reduce_bytes(k, s)
        order.append(("r", k, s))
        now = max(now, r_ready[k]) + 0.2
        if 1 <= s <= 2 + len(plan_of(CHUNKS[k][2], bits)):
            now += ways[s - 1][1] / 2e6
        if this is None:
            del r_stage[k]
            return
        r_ready[k] = send(now, *this)
        r_stage[k] = s + 1

    def vec_step():
        nonlocal now, v_stage, v_ready
        order.append(("v", v_stage))
        now = max(now, v_ready) + 0.2
        if v_stage == bits + 1:
            v_stage = None
            return
        way = (0, "y")[v_stage] if v_stage < 2 else v_stage - 1
        v_ready = send(now, way, NVEC * D * 4)
        v_stage += 1

    def poll():
        again = True
        while again:
            again = False
            for k in sorted(r_stage, key=lambda k: (min(r_stage[k], 2), r_ready[k])):
                if r_ready[k] + SLACK <= now:
                    reduce_step(k)
                    again = True
                    break
            if again:
                continue
            for k in GATHER_ORDER:
                if k in w_stage and w_stage[k] <= 4 and w_ready[k] + SLACK <= now:
                    gather_step(k)
                    again = True
                    break
            if not again and v_stage is not None and v_ready + SLACK <= now:
                vec_step()
                again = True

    for k in GATHER_ORDER:
        w_stage[k], w_ready[k] = 0, 0.0
        gather_step(k)
    for piece, took, needs in pieces:
        poll()
        if needs is not None:
            while w_stage[needs] <= 4:
                first = min((k for k in w_stage if w_stage[k] <= 4),
                            key=lambda k: (w_ready[k], GATHER_ORDER.index(k)))
                if w_ready[first] > w_ready[needs]:
                    first = needs
                gather_step(first)
            order.append(("w", needs, 5))
        order.append(("c", piece))
        now += took
        if piece in after:
            k = after[piece]
            r_stage[k], r_ready[k] = 0, now
        if piece == "sums":
            v_stage, v_ready = 0, now
    while r_stage or v_stage is not None:
        k = min(r_stage, key=lambda k: r_ready[k]) if r_stage else None
        if v_stage is not None and (k is None or v_ready <= r_ready[k]):
            vec_step()
        else:
            reduce_step(k)
    return order, now


SLACK = 0.3


def layer_kernel(bits, rows, names, *refs):
    r = dict(zip(names, refs))
    y = Layer(r, rows)
    links = Links(r, bits)
    order, _ = timeline(bits)
    for k in GATHER_ORDER:
        links.load(k)
    y.vectors()
    links.greet()
    links.bias(0)

    def link_step(op):
        if op[0] == "w":
            links.gather(op[1], op[2])
        elif op[0] == "r":
            links.reduce(op[1], op[2])
        else:
            links.vec(op[1])

    def attend(t, s):
        if s == 0:
            y.qkv(lax.rem(t, 3), t // 3)
        else:
            y.attend(t)

    def feed(u, s):
        y.feed(u // 2, 1 - lax.rem(u, 2))

    def back(u, s):
        j, h = u // 2, 1 - lax.rem(u, 2)
        if s == 0:
            y.attend_back(h * 3 + j)
        else:
            y.qkv_back(j, h)

    loops = {"qa": (attend, 2), "feed": (feed, 1), "back": (back, 2)}

    def proj_grad():
        y.proj_grad(1)
        y.proj_grad(0)

    single = {
        "start": y.start,
        "start2": y.start2,
        "project": y.project,
        "second_norm": y.second_norm,
        "middle_back": y.middle_back,
        "proj_back": y.proj_back,
        "proj_grad": proj_grad,
        "first_back": y.first_back,
        "sums": lambda: y.sums(links.vb.at[0]),
        "output": y.output,
        "tokens": lambda: y.narrow(y.br2, y.gtok),
    }

    at = 0
    first_pass = True
    while at < len(order):
        op = order[at]
        if op[0] != "c":
            link_step(op)
            at += 1
            continue
        if isinstance(op[1], str):
            if op[1] == "start":
                single["start"]()
                links.bias(1)
            else:
                single[op[1]]()
            at += 1
            continue
        kind = op[1][0]
        body, slots = loops[kind]
        end, last = at, at
        while end < len(order):
            o = order[end]
            if o[0] == "c":
                if isinstance(o[1], str) or o[1][0] != kind:
                    break
                last = end
            end += 1
        before = {}
        pending = []
        for o in order[at : last + 1]:
            if o[0] == "c":
                before[o[1][1], o[1][2]] = pending
                pending = []
            else:
                pending.append(o)
        low = op[1][1]
        high = order[last][1][1] + 1

        @pl.loop(low, high)
        def _(t):
            for s in range(slots):
                for u in range(low, high):
                    if before[u, s]:
                        @pl.when(t == u)
                        def _(ops=before[u, s]):
                            for o in ops:
                                link_step(o)
                body(t, s)

        at = last + 1
    for k in range(10):
        links.finish(k)
    links.vec_end()


INPUTS = ("tok", "mask", "in_mtok", "in_n1g", "in_n1s", "qvb", "in_pb", "ls", "in_n2g", "in_n2s",
          "upb", "in_db", "cot", "w_qkv", "w_pr", "w_up", "w_dn")
OUTPUTS = ("out", "gtok", "o_ff", "o_at", "o_vec")


def finish_kernel(ff, at, vec, o1, o2, p1, p2, wu, wd, wq, wp, mt, g1, s1, qv, pb, ls, g2, s2, ub, db):
    j = pl.program_id(0)
    for b in range(6):
        wd[:, b * 128 : b * 128 + 128] = ff[0, b * 256 : b * 256 + 256, :].astype(F32)
    for b in range(2):
        wu[:, b * 128 : b * 128 + 128] = ff[
            0, 1536 + b * D : 1536 + b * D + D, :].astype(F32)

    @pl.when(j < 3)
    def _():
        for p in range(3):
            wq[p] = at[0, p * D : p * D + D, :].astype(F32)

    @pl.when(j == 3)
    def _():
        for b in range(6):
            wp[:, b * 128 : b * 128 + 128] = at[0, b * 384 : b * 384 + 384, :].astype(F32)

    @pl.when(j == 4)
    def _():
        p1[...] = o1[...]
        p2[...] = o2[...]

    @pl.when(j == 0)
    def _():
        for ref, row in ((mt, MTOK), (g1, N1G), (s1, N1S), (pb, PB), (g2, N2G), (s2, N2S),
                         (db, DB)):
            ref[...] = vec[row, :]
        ls[...] = vec[LS0 : LS1 + 1, :]
        for w in range(2):
            qv[w : w + 1, :] = vec[QVO : QVO + 1, w * 384 : w * 384 + 384]
            ub[pl.ds(w * D, D)] = vec[UPO + w, :]


def local(dp, tokens, patch_mask, mask_token, norm1_gain, norm1_shift, w_qkv, qv_bias, w_proj,
          proj_bias, layer_scales, norm2_gain, norm2_shift, w_up, up_bias, w_down, down_bias,
          cotangent):
    bits = dp.bit_length() - 1
    rows = tokens.shape[0]
    scratch = {**layer_scratch(rows), **link_scratch(bits)}
    vmem, hbm = pl.BlockSpec(memory_space=pltpu.VMEM), pl.BlockSpec(memory_space=pl.ANY)
    shape = jax.ShapeDtypeStruct
    out, gtok, ff, at, vec = pl.pallas_call(
        functools.partial(layer_kernel, bits, rows, INPUTS + OUTPUTS + tuple(scratch)),
        name="layer",
        in_specs=[vmem] * 13 + [hbm] * 4,
        out_specs=[vmem, vmem, hbm, hbm, vmem],
        out_shape=[
            shape((rows, D), BF16),
            shape((rows, D), BF16),
            shape((6, FF_ROWS, 128), BF16),
            shape((4, AT_ROWS, 128), BF16),
            shape((NVEC, D), F32),
        ],
        scratch_shapes=list(scratch.values()),
        compiler_params=pltpu.CompilerParams(
            collective_id=0, has_side_effects=True, vmem_limit_bytes=63 * 2**20),
        cost_estimate=pl.CostEstimate(
            flops=27 * 10**9, bytes_accessed=20 * 10**6, transcendentals=10**7),
    )(
        tokens, patch_mask, mask_token, norm1_gain, norm1_shift, qv_bias, proj_bias,
        layer_scales, norm2_gain, norm2_shift, up_bias, down_bias, cotangent, w_qkv, w_proj,
        w_up, w_down,
    )
    one = shape((D,), F32)
    flat = pl.BlockSpec((D,), lambda j: (0,))
    whole = pl.BlockSpec((rows, D), lambda j: (0, 0))
    out, gtok, wu, wd, wq, wp, mt, g1, s1, qv, pb, ls, g2, s2, ub, db = pl.pallas_call(
        finish_kernel,
        name="finish",
        grid=(6,),
        in_specs=[
            pl.BlockSpec((1, FF_ROWS, 128), lambda j: (j, 0, 0)),
            pl.BlockSpec((1, AT_ROWS, 128), lambda j: (jnp.minimum(j, 3), 0, 0)),
            pl.BlockSpec((NVEC, D), lambda j: (0, 0)),
            whole, whole,
        ],
        out_specs=[
            whole, whole,
            pl.BlockSpec((D, 256), lambda j: (0, j)),
            pl.BlockSpec((256, D), lambda j: (j, 0)),
            pl.BlockSpec((3, D, 128), lambda j: (0, 0, jnp.minimum(j, 2))),
            pl.BlockSpec((384, D), lambda j: (0, 0)),
            flat, flat, flat,
            pl.BlockSpec((2, 384), lambda j: (0, 0)),
            flat,
            pl.BlockSpec((2, D), lambda j: (0, 0)),
            flat, flat,
            pl.BlockSpec((2 * D,), lambda j: (0,)),
            flat,
        ],
        out_shape=[
            shape((rows, D), BF16), shape((rows, D), BF16),
            shape((D, 1536), F32), shape((1536, D), F32), shape((3, D, 384), F32),
            shape((384, D), F32), one, one, one, shape((2, 384), F32), one, shape((2, D), F32),
            one, one, shape((2 * D,), F32), one,
        ],
    )(ff, at, vec, out, gtok)
    return out, gtok, mt, g1, s1, wq, qv, wp, pb, ls, g2, s2, wu, ub, wd, db


def solution(mesh):
    rows2, both = P(("dp", "tensor"), None), P(("dp", "tensor"))
    return jax.shard_map(
        functools.partial(local, mesh.shape["dp"]),
        mesh=mesh,
        in_specs=(
            rows2, both, P(), P(), P(), P(None, None, "tensor"), P(None, "tensor"),
            P("tensor", None), P(), P(), P(), P(), P(None, "tensor"), P("tensor"),
            P("tensor", None), P(), rows2,
        ),
        out_specs=(
            rows2, rows2, P(), P(), P(), P(None, None, "tensor"), P(None, "tensor"),
            P("tensor", None), P(), P(), P(), P(), P(None, "tensor"), P("tensor"),
            P("tensor", None), P(),
        ),
        check_vma=False,
    )
```

```python
import functools

import jax
import jax.numpy as jnp
from jax import lax
from jax.experimental import pallas as pl
from jax.experimental.pallas import tpu as pltpu
from jax.sharding import PartitionSpec as P

MESH = pl.DeviceIdType.MESH
F32 = jnp.float32
BF16 = jnp.bfloat16
L = 197
LP = 208
D = 768
EPS = 1e-06
INV_ROOT2 = 0.7071067811865476
INV_ROOT2PI = 0.3989422804014327

MTOK, N1G, N1S, PB, LS0, LS1, N2G, N2S, DB, QVO, UPO, QVX, UPX = (
    0, 1, 2, 3, 4, 5, 6, 7, 8, 9, 10, 12, 13)
NSUM = 9
NVEC = 16


def dot(a, b):
    return lax.dot_general(a, b, (((1,), (0,)), ((), ())), preferred_element_type=F32)


def dot_nt(a, b):
    return lax.dot_general(a, b, (((1,), (1,)), ((), ())), preferred_element_type=F32)


def fold(x):
    return jnp.sum(x.reshape(x.shape[0] // 8, 8, x.shape[1]), axis=0)


def normed(rows):
    centred = rows - jnp.mean(rows, axis=-1, keepdims=True)
    inverse = lax.rsqrt(jnp.mean(centred * centred, axis=-1, keepdims=True) + EPS)
    return centred * inverse, inverse


def norm_back(grad, gain, scaled, inverse):
    weighted = grad * gain
    inner = (
        weighted
        - jnp.mean(weighted, axis=-1, keepdims=True)
        - scaled * jnp.mean(weighted * scaled, axis=-1, keepdims=True)
    )
    return inverse * inner


def wide(column):
    return jnp.concatenate([column] * (D // 128), axis=1)


BLOCKS = ((0, 48), (48, 48), (96, 48), (144, 48), (192, 16))


VECTORS = ("mtok", "n1g", "n1s", "pb", "n2g", "n2s", "db")


class Layer:
    def __init__(self, r, rows):
        self.__dict__.update(r)
        self.rows = rows
        self.images = rows // L
        self.padded = self.images * LP

    def widen(self, src):
        n = self.rows // 16

        @pl.loop(0, n)
        def _(b):
            at = pl.ds(pl.multiple_of(b * 16, 16), 16)
            self.t32[at, :] = src[at, :].astype(F32)

        left = self.rows - n * 16
        if left:
            self.t32[n * 16 : self.rows, :] = src[n * 16 : self.rows, :].astype(F32)

    def narrow(self, src, dst):
        for i in range(self.images):
            for r, n in BLOCKS:
                n = min(n, L - r)
                self.t32[pl.ds(L * i + r, n), :] = src[pl.ds(LP * i + r, n), :].astype(F32)
        n = self.rows // 16

        @pl.loop(0, n)
        def _(b):
            at = pl.ds(pl.multiple_of(b * 16, 16), 16)
            dst[at, :] = self.t32[at, :].astype(BF16)

        left = self.rows - n * 16
        if left:
            dst[n * 16 : self.rows, :] = self.t32[n * 16 : self.rows, :].astype(BF16)

    def bands(self, i):
        for r, n in BLOCKS:
            yield pl.ds(pl.multiple_of(i * LP + r, 16), n), n

    def acc(self, at, x):
        self.vacc[pl.ds(at * 8, 8), :] += fold(x)

    def vectors(self):
        for name in ("mtok", "n1g", "n1s", "pb", "n2g", "n2s", "db"):
            self.__dict__[name] = self.rows8.at[pl.ds(VECTORS.index(name), 1), :]
            self.rows8[VECTORS.index(name), :] = self.__dict__["in_" + name][...]

    def start(self):
        self.vacc[...] = jnp.zeros_like(self.vacc)
        rows = self.rows
        self.mrow[...] = jnp.zeros_like(self.mrow)
        flags = jnp.where(self.mask[...] == 1, 1.0, 0.0).astype(F32)[None, :]
        self.mrow[:, pl.ds(0, rows)] = jnp.broadcast_to(flags, (128, rows))
        self.mcol[...] = jnp.transpose(self.mrow[...])
        self.t32[pl.ds(rows, self.t32.shape[0] - rows), :] = jnp.zeros(
            (self.t32.shape[0] - rows, D), F32)
        self.io_copy(0).wait()
        self.widen(self.tok)
        for i in range(self.images):
            for r, n in BLOCKS:
                at = pl.ds(L * i + r, n)
                to = pl.ds(LP * i + r, n)
                x = self.t32[at, :]
                mk = self.mcol[at, :]
                mx = jnp.where(wide(mk) > 0.5, self.mtok[...], x)
                if r + n > L:
                    keep = lax.broadcasted_iota(jnp.int32, (n, 128), 0) < L - r
                    mk = jnp.where(keep, mk, 0.0)
                    mx = jnp.where(wide(keep), mx, 0.0)
                self.maskp[to, :] = mk
                self.mixed[to, :] = mx
                sc, _ = normed(mx)
                self.n1[to, :] = (sc * self.n1g[...] + self.n1s[...]).astype(BF16)

    def start2(self):
        self.n1t[...] = jnp.transpose(self.n1[...])
        self.io_copy(1).wait()
        self.clear()
        self.widen(self.cot)
        for i in range(self.images):
            for r, n in BLOCKS:
                at = pl.ds(L * i + r, n)
                to = pl.ds(LP * i + r, n)
                go = self.t32[at, :] * wide(self.maskp[to, :])
                self.gout[to, :] = go.astype(BF16)
                self.gb[to, :] = (self.ls[1:2, :] * go).astype(BF16)

    def w_pair(self, j, h):
        return jnp.concatenate(
            [self.g_at[j, h, pl.ds(p * D, D), :] for p in range(3)], axis=1)

    def qkv(self, j, h):
        t = h * 3 + j
        proj = dot(self.n1[...], self.w_pair(j, h))
        qb = self.qb[pl.ds(t, 1), :]
        vb = self.qb[pl.ds(8 + t, 1), :]
        self.q[t] = ((proj[:, 0:128] + qb) * 0.125).astype(BF16)
        self.k[t] = proj[:, 128:256].astype(BF16)
        self.v[t] = (proj[:, 256:384] + vb).astype(BF16)

    def two(self, x):
        low = lax.broadcasted_iota(jnp.int32, x.shape, 1) < 64
        zero = jnp.zeros_like(x)
        return jnp.where(low, x, zero), jnp.where(low, zero, x)

    def attend(self, t):
        for i in range(self.images):
            at = pl.ds(i * LP, LP)
            q0, q1 = self.two(self.q[t, at, :])
            k = self.k[t, at, :]
            vt = jnp.transpose(self.v[t, at, :])
            outs = []
            for e, qe in enumerate((q0, q1)):
                s = dot_nt(k, qe)
                tail = s[LP - 16 :]
                keep = lax.broadcasted_iota(jnp.int32, tail.shape, 0) < L - (LP - 16)
                s = jnp.concatenate([s[: LP - 16], jnp.where(keep, tail, -1e30)], axis=0)
                x = jnp.exp(s - jnp.max(s, axis=0, keepdims=True))
                p = (x * (1.0 / jnp.sum(x, axis=0, keepdims=True))).astype(BF16)
                self.pt[(t * self.images + i) * 2 + e] = p
                outs.append(dot(vt[e * 64 : e * 64 + 64, :], p))
            ot = jnp.concatenate(outs, axis=0).astype(BF16)
            self.hot[i, pl.ds(pl.multiple_of(t * 128, 128), 128), :] = ot
            self.ho[t, at, :] = jnp.transpose(ot)

    def w_proj(self):
        return jnp.concatenate(
            [
                jnp.concatenate(
                    [self.g_at[3, h, pl.ds(b * 384, 384), :] for b in range(6)], axis=1)
                for h in range(2)
            ],
            axis=0,
        )

    def project(self):
        o = jnp.concatenate([self.ho[t] for t in range(6)], axis=1)
        self.br1[...] = dot(o, self.w_proj()) + self.pb[...]

    def second_norm(self):
        for i in range(self.images):
            for at, rows in self.bands(i):
                middle = self.mixed[at, :] + self.ls[0:1, :] * self.br1[at, :]
                sc, _ = normed(middle)
                self.n2[at, :] = (sc * self.n2g[...] + self.n2s[...]).astype(BF16)

    def clear(self):
        self.br2[...] = jnp.zeros_like(self.br2)
        self.gn2[...] = jnp.zeros_like(self.gn2)

    def turn(self):
        self.n2t[...] = jnp.transpose(self.n2[...])

    def feed(self, j, h):
        wd = jnp.concatenate(
            [self.g_ff[j, h, pl.ds(b * 256, 256), :] for b in range(6)], axis=1)
        wu = jnp.concatenate(
            [self.g_ff[j, h, pl.ds(1536 + b * D, D), :] for b in range(2)], axis=1)
        row = h * 6 + j
        pre = dot(self.n2[...], wu) + self.ub[pl.ds(row, 1), :]
        cdf = 0.5 * (1.0 + lax.erf(pre * INV_ROOT2))
        act = (pre * cdf).astype(BF16)
        slope = cdf + pre * jnp.exp(-0.5 * pre * pre) * INV_ROOT2PI
        gp32 = dot_nt(self.gb[...], wd) * slope
        gp = gp32.astype(BF16)
        self.uba[row] = fold(gp.astype(F32))
        self.br2[...] += dot(act, wd)
        self.gn2[...] += dot_nt(gp, wu)
        gwd = dot(jnp.transpose(act), self.gb[...]).astype(BF16)
        gwu = dot(self.n2t[...], gp).astype(BF16)
        for b in range(6):
            self.g_ff[j, h, pl.ds(b * 256, 256), :] = gwd[:, b * 128 : b * 128 + 128]
        for b in range(2):
            self.g_ff[j, h, pl.ds(1536 + b * D, D), :] = gwu[:, b * 128 : b * 128 + 128]

    def middle_back(self, i):
        ls0, ls1 = self.ls[0:1, :], self.ls[1:2, :]
        for at, rows in self.bands(i):
            b1 = self.br1[at, :]
            middle = self.mixed[at, :] + ls0 * b1
            sc, inv = normed(middle)
            b2 = self.br2[at, :] + self.db[...]
            self.outp[at, :] = (middle + ls1 * b2).astype(BF16)
            self.br2[at, :] = jnp.zeros((rows, D), F32)
            go = self.gout[at, :].astype(F32)
            self.acc(LS1, go * b2)
            self.acc(DB, self.gb[at, :].astype(F32))
            g = self.gn2[at, :]
            self.acc(N2G, g * sc)
            self.acc(N2S, g)
            gm = go + norm_back(g, self.n2g[...], sc, inv)
            self.acc(LS0, gm * b1)
            gb1 = (ls0 * gm).astype(BF16)
            self.gb[at, :] = gb1
            self.acc(PB, gb1.astype(F32))
            self.gn2[at, :] = gm

    def io_copy(self, i):
        src, dst = ((self.h_tok, self.tok), (self.h_cot, self.cot), (self.tok, self.h_out),
                    (self.cot, self.h_gtok))[i]
        return pltpu.make_async_copy(src, dst, self.io_sem.at[i])

    def output(self):
        self.narrow(self.outp, self.tok)
        self.io_copy(2).start()

    def tokens(self):
        self.narrow(self.br2, self.cot)
        self.io_copy(3).start()

    def proj_back(self):
        gh = dot_nt(self.gb[...], self.w_proj()).astype(BF16)
        for t in range(6):
            self.ho[t] = gh[:, t * 128 : t * 128 + 128]

    def proj_grad(self, h):
        total = sum(
            dot(self.hot[i, pl.ds(h * 384, 384), :], self.gb[pl.ds(i * LP, LP), :])
            for i in range(self.images))
        for b in range(6):
            self.g_at[3, h, pl.ds(b * 384, 384), :] = total[
                :, b * 128 : b * 128 + 128].astype(BF16)

    def attend_back(self, t):
        for i in range(self.images):
            at = pl.ds(i * LP, LP)
            q0, q1 = self.two(self.q[t, at, :])
            d0, d1 = self.two(self.ho[t, at, :])
            k = self.k[t, at, :]
            v = self.v[t, at, :]
            kt = jnp.transpose(k)
            dq, dk, dv = [], 0.0, 0.0
            for e, (qe, de) in enumerate(((q0, d0), (q1, d1))):
                pb = self.pt[(t * self.images + i) * 2 + e]
                p = pb.astype(F32)
                gp = dot_nt(v, de)
                gs = (p * (gp - jnp.sum(gp * p, axis=0, keepdims=True))).astype(BF16)
                dv = dv + dot(pb, de)
                dk = dk + dot(gs, qe)
                dq.append(dot(kt[e * 64 : e * 64 + 64, :], gs))
            dq = jnp.transpose(jnp.concatenate(dq, axis=0)) * 0.125
            self.dqkv[at, 0:128] = dq.astype(BF16)
            self.dqkv[at, 128:256] = dk.astype(BF16)
            self.dqkv[at, 256:384] = dv.astype(BF16)
        self.qa[t] = fold(self.dqkv[:, 0:128].astype(F32))
        self.qa[8 + t] = fold(self.dqkv[:, 256:384].astype(F32))

    def qkv_back(self, j, h):
        self.br2[...] += dot_nt(self.dqkv[...], self.w_pair(j, h))
        grad = dot(self.n1t[...], self.dqkv[...])
        for p in range(3):
            self.g_at[j, h, pl.ds(p * D, D), :] = grad[
                :, p * 128 : p * 128 + 128].astype(BF16)

    def first_back(self, i):
        for at, _ in self.bands(i):
            sc, inv = normed(self.mixed[at, :])
            g = self.br2[at, :]
            self.acc(N1G, g * sc)
            self.acc(N1S, g)
            gx = self.gn2[at, :] + norm_back(g, self.n1g[...], sc, inv)
            mk = wide(self.maskp[at, :]) > 0.5
            self.acc(MTOK, jnp.where(mk, gx, 0.0))
            self.br2[at, :] = jnp.where(mk, 0.0, gx)

    def sums(self, vec):
        vec[...] = jnp.zeros_like(vec)
        for s in range(NSUM):
            vec[s : s + 1, :] = jnp.sum(
                self.vacc[pl.ds(s * 8, 8), :], axis=0, keepdims=True)
        for h, (qv, up) in enumerate(((QVO, UPO), (QVX, UPX))):
            for w in range(2):
                for j in range(3):
                    c = w * 384 + j * 128
                    vec[qv : qv + 1, c : c + 128] = jnp.sum(
                        self.qa[8 * w + h * 3 + j], axis=0, keepdims=True)
            for j in range(6):
                c = j % 3 * 256
                vec[up + j // 3 : up + j // 3 + 1, c : c + 256] = jnp.sum(
                    self.uba[h * 6 + j], axis=0, keepdims=True)


def layer_scratch(rows):
    n = rows // L
    padded = n * LP
    v = pltpu.VMEM
    return dict(
        tok=v((rows, D), BF16),
        cot=v((rows, D), BF16),
        io_sem=pltpu.SemaphoreType.DMA((4,)),
        t32=v(((rows + 11 + 15) // 16 * 16 + 0, D), F32),
        mrow=v((128, (rows + 127) // 128 * 128), F32),
        mcol=v(((rows + 127) // 128 * 128, 128), F32),
        maskp=v((padded, 128), F32),
        mixed=v((padded, D), F32),
        gout=v((padded, D), BF16),
        n1=v((padded, D), BF16),
        n1t=v((D, padded), BF16),
        q=v((6, padded, 128), BF16),
        k=v((6, padded, 128), BF16),
        v=v((6, padded, 128), BF16),
        pt=v((6 * n * 2, LP, LP), BF16),
        ho=v((6, padded, 128), BF16),
        hot=v((n, D, LP), BF16),
        br1=v((padded, D), F32),
        n2=v((padded, D), BF16),
        n2t=v((D, padded), BF16),
        gb=v((padded, D), BF16),
        outp=v((padded, D), BF16),
        br2=v((padded, D), F32),
        gn2=v((padded, D), F32),
        dqkv=v((padded, 384), BF16),
        rows8=v((8, D), F32),
        vacc=v((NSUM * 8, D), F32),
        qb=v((16, 128), F32),
        ub=v((12, 256), F32),
        qa=v((16, 8, 128), F32),
        uba=v((12, 8, 256), F32),
    )


FF_ROWS, AT_ROWS = 3072, 2304
CHUNKS = tuple([("g_ff", j, FF_ROWS) for j in range(6)] + [("g_at", j, AT_ROWS) for j in range(4)])


Y_FIRST, Z_FIRST = (0, "y", 1, 2, 3), (0, 2, "y", 1, 3)
CUTS = {
    0: ((5, (0, 'y', 1, 13, 12), -31), (6, (0, 1, 2, 'y', 13), -60), (1, (0, 'y', 1, 12, 13), -41),),
    1: ((3, (0, 2, 1, 3, 'y'), -2), (3, (0, 'y', 1, 2, 13), 4), (6, (0, 'y', 1, 2, 13), 50),),
    2: ((6, (0, 1, 'y', 2, 13), 40), (6, (0, 'y', 1, 2, 13), 47),),
    3: ((4, (0, 2, 1, 13, 'y'), -10), (8, (0, 'y', 2, 1, 13), -49),),
    4: ((10, (0, 'y', 1, 2, 13), 27), (2, (0, 'y', 2, 1, 13), -42),),
    5: ((1, (0, 1, 2, 13, 'y'), 14), (11, (0, 1, 'y', 2, 13), -38),),
    9: ((2, (0, 2, 1, 'y', 3), -16), (7, (0, 'y', 1, 2, 13), -24),),
    6: ((9, (0, 'y', 1, 2, 13), 23),),
    7: ((9, (0, 'y', 1, 2, 13), 6),),
    8: ((4, (0, 1, 'y', 2, 13), 5), (5, (0, 'y', 2, 1, 13), 2),),
}


def parts_of():
    out = []
    for k, cuts in CUTS.items():
        at = 0
        for units, order, weight in cuts:
            out.append((k, at, units * 256, order, weight))
            at += units * 256
    return tuple(out)


PARTS = parts_of()


def steps_of(part, bits):
    _, _, rows, order, _ = part
    order = [w for w in order if w == "y" or w % 10 < bits] + list(range(4, bits))
    both, out = True, []
    for way in order:
        if way == "y":
            both = False
            out.append((way, False, rows, False))
        elif way < 10 and rows // 2 % 16 == 0:
            rows //= 2
            out.append((way, both, rows, True))
        else:
            out.append((way % 10, both, rows, False))
    return out


def land_offsets(bits):
    sizes, table = [0, 0], {}
    for p, part in enumerate(PARTS):
        for i, (_, both, rows, _) in enumerate(steps_of(part, bits)):
            table[p, i] = sizes[both]
            sizes[both] += rows
    return table, sizes


class Links:
    def __init__(self, r, bits):
        self.__dict__.update(r)
        self.bits = bits
        self.dp = lax.axis_index("dp")
        self.half = lax.axis_index("tensor")
        self.bit = [(self.dp // (1 << b)) % 2 for b in range(bits)]
        self.offsets, _ = land_offsets(bits)

    def peer(self, way):
        if way == "y":
            return (self.dp, 1 - self.half)
        return (self.dp + (1 << way) * (1 - 2 * self.bit[way]), self.half)

    def greet(self):
        barrier = pltpu.get_barrier_semaphore()
        ways = ["y"] + list(range(self.bits))
        for way in ways:
            pl.semaphore_signal(barrier, inc=1, device_id=self.peer(way), device_id_type=MESH)
        pl.semaphore_wait(barrier, len(ways))

    def copy(self, src, dst, send, recv, way):
        return pltpu.make_async_remote_copy(
            src_ref=src, dst_ref=dst, send_sem=send, recv_sem=recv,
            device_id=self.peer(way), device_id_type=MESH)

    def load(self, k):
        name, j, n = CHUNKS[k]
        sem = self.load_sem.at[k]
        if name == "g_ff":
            for b in range(6):
                pltpu.make_async_copy(
                    self.w_dn.at[pl.ds(j * 256, 256), pl.ds(b * 128, 128)],
                    self.g_ff.at[j, 0, pl.ds(b * 256, 256)], sem).start()
            for b in range(2):
                pltpu.make_async_copy(
                    self.w_up.at[:, pl.ds(j * 256 + b * 128, 128)],
                    self.g_ff.at[j, 0, pl.ds(1536 + b * D, D)], sem).start()
        elif j < 3:
            for p in range(3):
                pltpu.make_async_copy(
                    self.w_qkv.at[p, :, pl.ds(j * 128, 128)],
                    self.g_at.at[j, 0, pl.ds(p * D, D)], sem).start()
        else:
            for b in range(6):
                pltpu.make_async_copy(
                    self.w_pr.at[:, pl.ds(b * 128, 128)],
                    self.g_at.at[3, 0, pl.ds(b * 384, 384)], sem).start()

    def loaded(self, k):
        name, j, n = CHUNKS[k]
        ref = getattr(self, name).at[j, 0]
        pltpu.make_async_copy(ref, ref, self.load_sem.at[k]).wait()

    def bias(self, stage):
        a = self.copy(self.qvb, self.qvbx, self.b_send.at[0], self.b_recv.at[0], "y")
        b = self.copy(self.upb, self.upbx, self.b_send.at[1], self.b_recv.at[1], "y")
        if stage == 0:
            a.start()
            b.start()
            return
        a.wait()
        b.wait()
        for h, (qv, up) in enumerate(((self.qvb, self.upb), (self.qvbx, self.upbx))):
            for j in range(3):
                for w in range(2):
                    row = 8 * w + h * 3 + j
                    self.qb[row : row + 1, :] = qv[w : w + 1, j * 128 : j * 128 + 128]
            for j in range(6):
                row = h * 6 + j
                self.ub[row : row + 1, :] = up[pl.ds(j * 256, 256)][None, :]

    def gather_copy(self, k, i):
        name, j, n = CHUNKS[k]
        ref = getattr(self, name)
        way, rows = gather_plan(k)[i]
        off = self.bit[0] * (n // 2)
        size = n // 2
        for further in ROUTES[k][:0:-1][: len(ROUTES[k]) - max(i, 1)]:
            size //= 2
            off = off + self.bit[further] * size
        at = pl.ds(pl.multiple_of(off, 16), rows)
        return self.copy(
            ref.at[j, int(i > 0), at], ref.at[j, 1, at],
            self.w_send.at[k, i], self.w_recv.at[k, i], way)

    def gather(self, k, stage):
        copies = len(gather_plan(k))
        if stage < 0:
            for i in range(copies):
                self.gather_copy(k, i).wait_send()
            return
        if stage == 0:
            self.loaded(k)
        else:
            self.gather_copy(k, stage - 1).wait_recv()
        if stage < copies:
            self.gather_copy(k, stage).start()

    def add(self, dst, dst_at, src, src_at, rows):
        size = next(s for s in (256, 192, 144, 128, 112, 96, 80, 64, 48, 32, 16) if rows % s == 0)

        @pl.loop(0, rows // size)
        def _(b):
            to = pl.ds(pl.multiple_of(dst_at + b * size, 16), size)
            of = pl.ds(pl.multiple_of(src_at + b * size, 16), size)
            total = dst[to, :].astype(F32) + src[of, :].astype(F32)
            dst[to, :] = total.astype(BF16)

    def reduce_steps(self, p):
        part = PARTS[p]
        k, first, rows = part[:3]
        name, j, _ = CHUNKS[k]
        ref = getattr(self, name)
        own = ref.at[j, 0]
        at, out, back = first, [], []

        def add(way, src, dst, adds, halves):
            i = len(out)

            def build():
                return self.copy(src(), dst(), self.r_send.at[p, i], self.r_recv.at[p, i], way)

            out.append((way, build, adds, halves))

        def rows_of(r, at, rows):
            return lambda: r.at[pl.ds(pl.multiple_of(at, 16), rows)]

        def both_of(r, at, rows):
            return lambda: r.at[:, pl.ds(pl.multiple_of(at, 16), rows)]

        for way, both, rows, halves in steps_of(part, self.bits):
            o = self.offsets[p, len(out)]
            away = at
            if halves:
                away = at + (1 - self.bit[way]) * rows
                at = at + self.bit[way] * rows
                back.append((way, at, rows))
            if both:
                add(way, both_of(ref.at[j], away, rows), both_of(self.land2, o, rows),
                    [(ref.at[j, h], at, self.land2.at[h], o, rows) for h in range(2)], halves)
            else:
                src = ref.at[j, 1] if way == "y" else own
                add(way, rows_of(src, away, rows), rows_of(self.land, o, rows),
                    [(own, at, self.land, o, rows)], halves)
        for way, at, rows in back[::-1]:
            add(way, rows_of(own, at, rows), rows_of(own, at, rows), [], False)
        return out

    def result_copy(self, p):
        k, first, rows = PARTS[p][:3]
        name, j, _ = CHUNKS[k]
        out = self.o_ff if name == "g_ff" else self.o_at
        at = pl.ds(first, rows)
        return pltpu.make_async_copy(
            getattr(self, name).at[j, 0, at], out.at[j, at], self.out_sem.at[p])

    def reduce(self, p, stage):
        steps = self.reduce_steps(p)
        if stage > 0:
            way, build, adds, halves = steps[stage - 1]
            copy = build()
            copy.wait_recv()
            copy.wait_send()
            if halves:
                pl.semaphore_signal(
                    self.credit.at[p, way], inc=1, device_id=self.peer(way), device_id_type=MESH)
            for one in adds:
                self.add(*one)
        if stage < len(steps):
            way, build, adds, _ = steps[stage]
            if not adds:
                pl.semaphore_wait(self.credit.at[p, way], 1)
            build().start()
        else:
            self.result_copy(p).start()

    def finish(self, p):
        self.result_copy(p).wait()

    def vec_copy(self, s):
        way = (0, "y")[s] if s < 2 else s - 1
        return self.copy(self.vb.at[s], self.vr.at[s], self.v_send.at[s], self.v_recv.at[s], way)

    def vec(self, stage):
        if stage > 0:
            s = stage - 1
            self.vec_copy(s).wait_recv()
            if s == 1:
                self.vb[2, 0:NSUM, :] = self.vb[1, 0:NSUM, :] + self.vr[1, 0:NSUM, :]
                self.vb[2, QVO:QVX, :] = self.vb[1, QVO:QVX, :] + self.vr[1, QVX : QVX + 3, :]
                self.vb[2, QVX:NVEC, :] = jnp.zeros((NVEC - QVX, D), F32)
            else:
                self.vb[stage] = self.vb[s] + self.vr[s]
        if stage < self.bits + 1:
            self.vec_copy(stage).start()

    def vec_end(self):
        for s in range(self.bits + 1):
            self.vec_copy(s).wait_send()
        self.o_vec[...] = self.vb[self.bits + 1]


def link_scratch(bits):
    v, dma = pltpu.VMEM, pltpu.SemaphoreType.DMA
    steps = 2 * bits + 1
    parts = len(PARTS)
    land = land_offsets(bits)[1]
    return dict(
        g_ff=v((6, 2, FF_ROWS, 128), BF16),
        g_at=v((4, 2, AT_ROWS, 128), BF16),
        land2=v((2, land[1], 128), BF16),
        land=v((land[0], 128), BF16),
        qvbx=v((2, 384), F32),
        upbx=v((1536,), F32),
        vb=v((bits + 2, NVEC, D), F32),
        vr=v((bits + 1, NVEC, D), F32),
        load_sem=dma((10,)),
        out_sem=dma((parts,)),
        b_send=dma((2,)),
        b_recv=dma((2,)),
        w_send=dma((10, 4)),
        w_recv=dma((10, 4)),
        r_send=dma((parts, steps)),
        r_recv=dma((parts, steps)),
        credit=pltpu.SemaphoreType.REGULAR((parts, bits)),
        v_send=dma((bits + 1,)),
        v_recv=dma((bits + 1,)),
    )


ROUTES = (('y', 1), ('y', 2), ('y', 2, 1), ('y', 1), ('y', 1, 2), ('y', 1, 2), ('y', 1, 2), ('y', 2, 1), ('y', 2), ('y', 2, 1))
GATHER_ORDER = (6, 7, 9, 8, 2, 0, 1, 4, 5, 3)


def gather_plan(k):
    rows, ways = CHUNKS[k][2] // 2, ROUTES[k]
    n = len(ways)
    steps = [("y", rows >> (n - 1))]
    steps += [(way, rows >> (n - 1 - i)) for i, way in enumerate(ways[1:])]
    return steps + [(0, rows)]


SLACK, STEP, BACKLOG = 0.2, 0.05, 2.455
HOPS = {0: 0.9, "y": 2.2, 1: 2.2, 2: 2.2}
FAR_HOP = 2.7
LINK, CORES, SUMS, MESSAGE, LOADS, ENTRY = 45.5e3, 480e3, 2.4e6, 0.1, 3.0e6, 3.8
LINES = {0: (("c", 1),), "y": (("y", 1),), 1: (("x", 1),), 2: (("z", 1),)}
FAR_LINES = (("z", 1), ("mid", 2))


def compute_pieces():
    out = [("start", 0.5, None)]
    out += [(("qa", t, s), (0.57, 1.45)[s], None) for t in range(3) for s in range(2)]
    out += [("start2", 1.7, None)]
    out += [(("qa", t, s), (0.57, 1.45)[s], 3 + t if s == 0 else None)
            for t in range(3, 6) for s in range(2)]
    out += [("project", 1.6, 9), ("second_norm", 0.8, None), ("turn", 0.6, None)]
    out += [(("feed", u, 0), 1.96, u // 2 if u % 2 == 0 else None) for u in range(12)]
    out += [(("middle_back", i, 0), 1.2, None) for i in range(3)]
    out += [("proj_back", 1.0, None), ("proj_grad", 1.6, None)]
    out += [(("back", u, s), (1.62, 1.4)[s], None) for u in range(6) for s in range(2)]
    out += [(("first_back", i, 0), 0.8, None) for i in range(3)]
    out += [("sums", 0.6, None), ("output", 0.6, None), ("tokens", 0.6, None)]
    after = {("feed", 2 * j + 1, 0): j for j in range(6)}
    after["proj_grad"] = 9
    after.update({("back", 2 * j + 1, 1): 6 + j for j in range(3)})
    return out, after


class Timeline:
    def __init__(self, bits, log=None):
        self.log = log or (lambda *a: None)
        self.now, self.order, self.tasks = ENTRY, [], {}
        self.free = {line: 0.0 for line in ("c", "y", "x", "z", "mid")}
        self.moves, self.adds = {}, {}
        for k in range(10):
            self.moves["w", k] = [(way, rows * 256) for way, rows in gather_plan(k)]
        for p, part in enumerate(PARTS):
            there = steps_of(part, bits)
            self.adds["r", p] = [rows * 256 * (1 + both) for _, both, rows, _ in there]
            self.moves["r", p] = [
                (way, n) for (way, *_), n in zip(there, self.adds["r", p])
            ] + [(way, rows * 256) for way, _, rows, halves in there[::-1] if halves]
        self.moves["v", 0] = [
            (way, NVEC * D * 4) for way in (0, "y") + tuple(range(1, bits))]
        self.left = {
            key: [sum(self.took(*m) + HOPS.get(m[0], FAR_HOP) for m in moves[i:])
                  for i in range(len(moves) + 1)]
            for key, moves in self.moves.items()}

    def took(self, way, nbytes):
        return nbytes / CORES if way == 0 else nbytes / LINK + MESSAGE

    def urgency(self, key):
        if key[0] == "w":
            return 1000 - GATHER_ORDER.index(key[1]) * 10 + self.tasks[key][0]
        weight = PARTS[key[1]][4] if key[0] == "r" else 0
        return self.left[key][self.tasks[key][0]] + weight

    def opens(self, key):
        stage, ready = self.tasks[key]
        if stage < len(self.moves[key]):
            way = self.moves[key][stage][0]
            if way != 0:
                for line, _ in LINES.get(way, FAR_LINES):
                    ready = max(ready, self.free[line] - BACKLOG)
        return ready

    def step(self, key):
        stage, ready = self.tasks[key]
        self.order.append(key + (stage,))
        self.log("op", self.now, key, stage, ready)
        self.now = max(self.now, ready) + STEP
        if 0 < stage <= len(self.adds.get(key, ())):
            self.now += self.adds[key][stage - 1] / SUMS
        if stage == len(self.moves[key]):
            del self.tasks[key]
            return
        way, nbytes = self.moves[key][stage]
        lines = LINES.get(way, FAR_LINES)
        begin = max([self.now] + [self.free[line] for line, _ in lines])
        for line, load in lines:
            self.free[line] = begin + self.took(way, nbytes) * load
            self.log("x", line, begin, self.free[line])
        done = max(self.free[line] for line, _ in lines)
        self.tasks[key] = (stage + 1, done + HOPS.get(way, FAR_HOP))

    def poll(self, slack):
        while True:
            ready = [key for key in self.tasks if self.opens(key) + slack <= self.now]
            if not ready:
                return
            self.step(max(ready, key=self.urgency))

    def wait(self):
        self.now = max(self.now, min(self.opens(key) for key in self.tasks) + 1e-6)
        self.poll(0.0)

    def run(self):
        loaded = ENTRY
        for k in GATHER_ORDER:
            loaded += CHUNKS[k][2] * 256 / LOADS
            self.tasks["w", k] = (0, loaded)
        pieces, after = compute_pieces()
        for piece, took, needs in pieces:
            self.poll(SLACK)
            if needs is not None:
                while ("w", needs) in self.tasks:
                    self.wait()
                self.order.append(("w", needs, -1))
            self.order.append(("c", piece))
            self.log("c", self.now, piece)
            self.now += took
            if piece in after:
                for p, part in enumerate(PARTS):
                    if part[0] == after[piece]:
                        self.tasks["r", p] = (0, self.now)
            if piece == "sums":
                self.tasks["v", 0] = (0, self.now)
        while self.tasks:
            self.wait()
        return self.order, self.now


def timeline(bits, log=None):
    return Timeline(bits, log).run()


def layer_kernel(bits, rows, names, *refs):
    r = dict(zip(names, refs))
    y = Layer(r, rows)
    links = Links(r, bits)
    order, _ = timeline(bits)
    y.io_copy(0).start()
    for k in GATHER_ORDER:
        links.load(k)
    y.io_copy(1).start()
    y.vectors()
    links.greet()
    links.bias(0)

    def link_step(op):
        if op[0] == "w":
            links.gather(op[1], op[2])
        elif op[0] == "r":
            links.reduce(op[1], op[2])
        else:
            links.vec(op[2])

    def attend(t, s):
        if s == 0:
            y.qkv(lax.rem(t, 3), t // 3)
        else:
            y.attend(t)

    def feed(u, s):
        y.feed(u // 2, 1 - lax.rem(u, 2))

    def back(u, s):
        j, h = u // 2, 1 - lax.rem(u, 2)
        if s == 0:
            y.attend_back(h * 3 + j)
        else:
            y.qkv_back(j, h)

    loops = {
        "qa": (attend, 2),
        "feed": (feed, 1),
        "middle_back": (lambda i, s: y.middle_back(i), 1),
        "back": (back, 2),
        "first_back": (lambda i, s: y.first_back(i), 1),
    }

    def proj_grad():
        y.proj_grad(1)
        y.proj_grad(0)

    single = {
        "start": y.start,
        "start2": y.start2,
        "project": y.project,
        "second_norm": y.second_norm,
        "turn": y.turn,
        "proj_back": y.proj_back,
        "proj_grad": proj_grad,
        "sums": lambda: y.sums(links.vb.at[0]),
        "output": y.output,
        "tokens": y.tokens,
    }

    at = 0
    first_pass = True
    while at < len(order):
        op = order[at]
        if op[0] != "c":
            link_step(op)
            at += 1
            continue
        if isinstance(op[1], str):
            if op[1] == "start":
                single["start"]()
                links.bias(1)
            else:
                single[op[1]]()
            at += 1
            continue
        kind = op[1][0]
        body, slots = loops[kind]
        end, last = at, at
        while end < len(order):
            o = order[end]
            if o[0] == "c":
                if isinstance(o[1], str) or o[1][0] != kind:
                    break
                last = end
            end += 1
        before = {}
        pending = []
        for o in order[at : last + 1]:
            if o[0] == "c":
                before[o[1][1], o[1][2]] = pending
                pending = []
            else:
                pending.append(o)
        low = op[1][1]
        high = order[last][1][1] + 1

        @pl.loop(low, high)
        def _(t):
            for s in range(slots):
                for u in range(low, high):
                    if before[u, s]:
                        @pl.when(t == u)
                        def _(ops=before[u, s]):
                            for o in ops:
                                link_step(o)
                body(t, s)

        at = last + 1
    for i in (2, 3):
        y.io_copy(i).wait()
    for p in range(len(PARTS)):
        links.finish(p)
    links.vec_end()


INPUTS = ("h_tok", "mask", "in_mtok", "in_n1g", "in_n1s", "qvb", "in_pb", "ls", "in_n2g", "in_n2s",
          "upb", "in_db", "h_cot", "w_qkv", "w_pr", "w_up", "w_dn")
OUTPUTS = ("h_out", "h_gtok", "o_ff", "o_at", "o_vec")


def finish_kernel(ff, at, vec, o1, o2, p1, p2, wu, wd, wq, wp, mt, g1, s1, qv, pb, ls, g2, s2, ub, db):
    j = pl.program_id(0)
    for b in range(6):
        wd[:, b * 128 : b * 128 + 128] = ff[0, b * 256 : b * 256 + 256, :].astype(F32)
    for b in range(2):
        wu[:, b * 128 : b * 128 + 128] = ff[
            0, 1536 + b * D : 1536 + b * D + D, :].astype(F32)

    @pl.when(j < 3)
    def _():
        for p in range(3):
            wq[p] = at[0, p * D : p * D + D, :].astype(F32)

    @pl.when(j == 3)
    def _():
        for b in range(6):
            wp[:, b * 128 : b * 128 + 128] = at[0, b * 384 : b * 384 + 384, :].astype(F32)

    @pl.when(j == 4)
    def _():
        p1[...] = o1[...]
        p2[...] = o2[...]

    @pl.when(j == 0)
    def _():
        for ref, row in ((mt, MTOK), (g1, N1G), (s1, N1S), (pb, PB), (g2, N2G), (s2, N2S),
                         (db, DB)):
            ref[...] = vec[row, :]
        ls[...] = vec[LS0 : LS1 + 1, :]
        for w in range(2):
            qv[w : w + 1, :] = vec[QVO : QVO + 1, w * 384 : w * 384 + 384]
            ub[pl.ds(w * D, D)] = vec[UPO + w, :]


def local(dp, tokens, patch_mask, mask_token, norm1_gain, norm1_shift, w_qkv, qv_bias, w_proj,
          proj_bias, layer_scales, norm2_gain, norm2_shift, w_up, up_bias, w_down, down_bias,
          cotangent):
    bits = dp.bit_length() - 1
    rows = tokens.shape[0]
    scratch = {**layer_scratch(rows), **link_scratch(bits)}
    vmem, hbm = pl.BlockSpec(memory_space=pltpu.VMEM), pl.BlockSpec(memory_space=pl.ANY)
    shape = jax.ShapeDtypeStruct
    out, gtok, ff, at, vec = pl.pallas_call(
        functools.partial(layer_kernel, bits, rows, INPUTS + OUTPUTS + tuple(scratch)),
        name="layer",
        in_specs=[hbm] + [vmem] * 11 + [hbm] * 5,
        out_specs=[hbm, hbm, hbm, hbm, vmem],
        out_shape=[
            shape((rows, D), BF16),
            shape((rows, D), BF16),
            shape((6, FF_ROWS, 128), BF16),
            shape((4, AT_ROWS, 128), BF16),
            shape((NVEC, D), F32),
        ],
        scratch_shapes=list(scratch.values()),
        compiler_params=pltpu.CompilerParams(
            collective_id=0, has_side_effects=True, vmem_limit_bytes=63 * 2**20),
        cost_estimate=pl.CostEstimate(
            flops=27 * 10**9, bytes_accessed=20 * 10**6, transcendentals=10**7),
    )(
        tokens, patch_mask, mask_token, norm1_gain, norm1_shift, qv_bias, proj_bias,
        layer_scales, norm2_gain, norm2_shift, up_bias, down_bias, cotangent, w_qkv, w_proj,
        w_up, w_down,
    )
    one = shape((D,), F32)
    flat = pl.BlockSpec((D,), lambda j: (0,))
    whole = pl.BlockSpec((rows, D), lambda j: (0, 0))
    out, gtok, wu, wd, wq, wp, mt, g1, s1, qv, pb, ls, g2, s2, ub, db = pl.pallas_call(
        finish_kernel,
        name="finish",
        grid=(6,),
        in_specs=[
            pl.BlockSpec((1, FF_ROWS, 128), lambda j: (j, 0, 0)),
            pl.BlockSpec((1, AT_ROWS, 128), lambda j: (jnp.minimum(j, 3), 0, 0)),
            pl.BlockSpec((NVEC, D), lambda j: (0, 0)),
            whole, whole,
        ],
        out_specs=[
            whole, whole,
            pl.BlockSpec((D, 256), lambda j: (0, j)),
            pl.BlockSpec((256, D), lambda j: (j, 0)),
            pl.BlockSpec((3, D, 128), lambda j: (0, 0, jnp.minimum(j, 2))),
            pl.BlockSpec((384, D), lambda j: (0, 0)),
            flat, flat, flat,
            pl.BlockSpec((2, 384), lambda j: (0, 0)),
            flat,
            pl.BlockSpec((2, D), lambda j: (0, 0)),
            flat, flat,
            pl.BlockSpec((2 * D,), lambda j: (0,)),
            flat,
        ],
        out_shape=[
            shape((rows, D), BF16), shape((rows, D), BF16),
            shape((D, 1536), F32), shape((1536, D), F32), shape((3, D, 384), F32),
            shape((384, D), F32), one, one, one, shape((2, 384), F32), one, shape((2, D), F32),
            one, one, shape((2 * D,), F32), one,
        ],
    )(ff, at, vec, out, gtok)
    return out, gtok, mt, g1, s1, wq, qv, wp, pb, ls, g2, s2, wu, ub, wd, db


def solution(mesh):
    rows2, both = P(("dp", "tensor"), None), P(("dp", "tensor"))
    return jax.shard_map(
        functools.partial(local, mesh.shape["dp"]),
        mesh=mesh,
        in_specs=(
            rows2, both, P(), P(), P(), P(None, None, "tensor"), P(None, "tensor"),
            P("tensor", None), P(), P(), P(), P(), P(None, "tensor"), P("tensor"),
            P("tensor", None), P(), rows2,
        ),
        out_specs=(
            rows2, rows2, P(), P(), P(), P(None, None, "tensor"), P(None, "tensor"),
            P("tensor", None), P(), P(), P(), P(), P(None, "tensor"), P("tensor"),
            P("tensor", None), P(),
        ),
        check_vma=False,
    )
```

```python
import functools

import jax
import jax.numpy as jnp
from jax import lax
from jax.experimental import pallas as pl
from jax.experimental.pallas import tpu as pltpu
from jax.sharding import PartitionSpec as P

MESH = pl.DeviceIdType.MESH
F32 = jnp.float32
BF16 = jnp.bfloat16
L = 197
LP = 208
D = 768
EPS = 1e-06
INV_ROOT2 = 0.7071067811865476
INV_ROOT2PI = 0.3989422804014327

MTOK, N1G, N1S, PB, LS0, LS1, N2G, N2S, DB, QVO, UPO, QVX, UPX = (
    0, 1, 2, 3, 4, 5, 6, 7, 8, 9, 10, 12, 13)
NSUM = 9
NVEC = 16


def dot(a, b):
    return lax.dot_general(a, b, (((1,), (0,)), ((), ())), preferred_element_type=F32)


def dot_nt(a, b):
    return lax.dot_general(a, b, (((1,), (1,)), ((), ())), preferred_element_type=F32)


def fold(x):
    return jnp.sum(x.reshape(x.shape[0] // 8, 8, x.shape[1]), axis=0)


def normed(rows):
    centred = rows - jnp.mean(rows, axis=-1, keepdims=True)
    inverse = lax.rsqrt(jnp.mean(centred * centred, axis=-1, keepdims=True) + EPS)
    return centred * inverse, inverse


def norm_back(grad, gain, scaled, inverse):
    weighted = grad * gain
    inner = (
        weighted
        - jnp.mean(weighted, axis=-1, keepdims=True)
        - scaled * jnp.mean(weighted * scaled, axis=-1, keepdims=True)
    )
    return inverse * inner


def wide(column):
    return jnp.concatenate([column] * (D // 128), axis=1)


BLOCKS = ((0, 48), (48, 48), (96, 48), (144, 48), (192, 16))


VECTORS = ("mtok", "n1g", "n1s", "pb", "n2g", "n2s", "db")
SMALL = VECTORS + ("mask", "qvb", "ls", "upb")


class Layer:
    def __init__(self, r, rows):
        self.__dict__.update(r)
        self.rows = rows
        self.images = rows // L
        self.padded = self.images * LP

    def widen(self, src):
        n = self.rows // 16

        @pl.loop(0, n)
        def _(b):
            at = pl.ds(pl.multiple_of(b * 16, 16), 16)
            self.t32[at, :] = src[at, :].astype(F32)

        left = self.rows - n * 16
        if left:
            self.t32[n * 16 : self.rows, :] = src[n * 16 : self.rows, :].astype(F32)

    def narrow(self, src, dst):
        for i in range(self.images):
            for r, n in BLOCKS:
                n = min(n, L - r)
                self.t32[pl.ds(L * i + r, n), :] = src[pl.ds(LP * i + r, n), :].astype(F32)
        n = self.rows // 16

        @pl.loop(0, n)
        def _(b):
            at = pl.ds(pl.multiple_of(b * 16, 16), 16)
            dst[at, :] = self.t32[at, :].astype(BF16)

        left = self.rows - n * 16
        if left:
            dst[n * 16 : self.rows, :] = self.t32[n * 16 : self.rows, :].astype(BF16)

    def bands(self, i):
        for r, n in BLOCKS:
            yield pl.ds(pl.multiple_of(i * LP + r, 16), n), n

    def acc(self, at, x):
        self.vacc[pl.ds(at * 8, 8), :] += fold(x)

    def small_copy(self, i):
        name = SMALL[i]
        return pltpu.make_async_copy(
            getattr(self, "h_" + name), getattr(self, "in_" + name), self.small_sem.at[i])

    def vectors(self):
        for i in range(len(SMALL)):
            self.small_copy(i).wait()
        for name in VECTORS:
            self.__dict__[name] = self.rows8.at[pl.ds(VECTORS.index(name), 1), :]
            self.rows8[VECTORS.index(name), :] = self.__dict__["in_" + name][...]

    def start(self):
        self.vacc[...] = jnp.zeros_like(self.vacc)
        rows = self.rows
        self.mrow[...] = jnp.zeros_like(self.mrow)
        flags = jnp.where(self.in_mask[...] == 1, 1.0, 0.0).astype(F32)[None, :]
        self.mrow[:, pl.ds(0, rows)] = jnp.broadcast_to(flags, (128, rows))
        self.mcol[...] = jnp.transpose(self.mrow[...])
        self.t32[pl.ds(rows, self.t32.shape[0] - rows), :] = jnp.zeros(
            (self.t32.shape[0] - rows, D), F32)
        self.io_copy(0).wait()
        self.widen(self.tok)
        for i in range(self.images):
            for r, n in BLOCKS:
                at = pl.ds(L * i + r, n)
                to = pl.ds(LP * i + r, n)
                x = self.t32[at, :]
                mk = self.mcol[at, :]
                mx = jnp.where(wide(mk) > 0.5, self.mtok[...], x)
                if r + n > L:
                    keep = lax.broadcasted_iota(jnp.int32, (n, 128), 0) < L - r
                    mk = jnp.where(keep, mk, 0.0)
                    mx = jnp.where(wide(keep), mx, 0.0)
                self.maskp[to, :] = mk
                self.mixed[to, :] = mx
                sc, _ = normed(mx)
                self.n1[to, :] = (sc * self.n1g[...] + self.n1s[...]).astype(BF16)

    def start2(self):
        self.n1t[...] = jnp.transpose(self.n1[...])
        self.io_copy(1).wait()
        self.clear()
        self.widen(self.cot)
        for i in range(self.images):
            for r, n in BLOCKS:
                at = pl.ds(L * i + r, n)
                to = pl.ds(LP * i + r, n)
                go = self.t32[at, :] * wide(self.maskp[to, :])
                self.gout[to, :] = go.astype(BF16)
                self.gb[to, :] = (self.in_ls[1:2, :] * go).astype(BF16)

    def w_pair(self, j, h):
        return jnp.concatenate(
            [self.g_at[j, h, pl.ds(p * D, D), :] for p in range(3)], axis=1)

    def qkv(self, j, h):
        t = h * 3 + j
        proj = dot(self.n1[...], self.w_pair(j, h))
        qb = self.qb[pl.ds(t, 1), :]
        vb = self.qb[pl.ds(8 + t, 1), :]
        self.q[t] = ((proj[:, 0:128] + qb) * 0.125).astype(BF16)
        self.k[t] = proj[:, 128:256].astype(BF16)
        self.v[t] = (proj[:, 256:384] + vb).astype(BF16)

    def two(self, x):
        low = lax.broadcasted_iota(jnp.int32, x.shape, 1) < 64
        zero = jnp.zeros_like(x)
        return jnp.where(low, x, zero), jnp.where(low, zero, x)

    def attend(self, t):
        for i in range(self.images):
            at = pl.ds(i * LP, LP)
            q0, q1 = self.two(self.q[t, at, :])
            k = self.k[t, at, :]
            vt = jnp.transpose(self.v[t, at, :])
            outs = []
            for e, qe in enumerate((q0, q1)):
                s = dot_nt(k, qe)
                tail = s[LP - 16 :]
                keep = lax.broadcasted_iota(jnp.int32, tail.shape, 0) < L - (LP - 16)
                s = jnp.concatenate([s[: LP - 16], jnp.where(keep, tail, -1e30)], axis=0)
                x = jnp.exp(s - jnp.max(s, axis=0, keepdims=True))
                p = (x * (1.0 / jnp.sum(x, axis=0, keepdims=True))).astype(BF16)
                self.pt[(t * self.images + i) * 2 + e] = p
                outs.append(dot(vt[e * 64 : e * 64 + 64, :], p))
            ot = jnp.concatenate(outs, axis=0).astype(BF16)
            self.hot[i, pl.ds(pl.multiple_of(t * 128, 128), 128), :] = ot
            self.ho[t, at, :] = jnp.transpose(ot)

    def w_proj(self):
        return jnp.concatenate(
            [
                jnp.concatenate(
                    [self.g_at[3, h, pl.ds(b * 384, 384), :] for b in range(6)], axis=1)
                for h in range(2)
            ],
            axis=0,
        )

    def project(self):
        o = jnp.concatenate([self.ho[t] for t in range(6)], axis=1)
        self.br1[...] = dot(o, self.w_proj()) + self.pb[...]

    def second_norm(self):
        for i in range(self.images):
            for at, rows in self.bands(i):
                middle = self.mixed[at, :] + self.in_ls[0:1, :] * self.br1[at, :]
                sc, _ = normed(middle)
                self.n2[at, :] = (sc * self.n2g[...] + self.n2s[...]).astype(BF16)

    def clear(self):
        self.br2[...] = jnp.zeros_like(self.br2)
        self.gn2[...] = jnp.zeros_like(self.gn2)

    def turn(self):
        self.n2t[...] = jnp.transpose(self.n2[...])

    def feed(self, j, h):
        wd = jnp.concatenate(
            [self.g_ff[j, h, pl.ds(b * 256, 256), :] for b in range(6)], axis=1)
        wu = jnp.concatenate(
            [self.g_ff[j, h, pl.ds(1536 + b * D, D), :] for b in range(2)], axis=1)
        row = h * 6 + j
        pre = dot(self.n2[...], wu) + self.ub[pl.ds(row, 1), :]
        cdf = 0.5 * (1.0 + lax.erf(pre * INV_ROOT2))
        act = (pre * cdf).astype(BF16)
        slope = cdf + pre * jnp.exp(-0.5 * pre * pre) * INV_ROOT2PI
        gp32 = dot_nt(self.gb[...], wd) * slope
        gp = gp32.astype(BF16)
        self.uba[row] = fold(gp.astype(F32))
        self.br2[...] += dot(act, wd)
        self.gn2[...] += dot_nt(gp, wu)
        gwd = dot(jnp.transpose(act), self.gb[...]).astype(BF16)
        gwu = dot(self.n2t[...], gp).astype(BF16)
        for b in range(6):
            self.g_ff[j, h, pl.ds(b * 256, 256), :] = gwd[:, b * 128 : b * 128 + 128]
        for b in range(2):
            self.g_ff[j, h, pl.ds(1536 + b * D, D), :] = gwu[:, b * 128 : b * 128 + 128]

    def middle_back(self, i):
        ls0, ls1 = self.in_ls[0:1, :], self.in_ls[1:2, :]
        for at, rows in self.bands(i):
            b1 = self.br1[at, :]
            middle = self.mixed[at, :] + ls0 * b1
            sc, inv = normed(middle)
            b2 = self.br2[at, :] + self.db[...]
            self.n2[at, :] = (middle + ls1 * b2).astype(BF16)
            self.br2[at, :] = jnp.zeros((rows, D), F32)
            go = self.gout[at, :].astype(F32)
            self.acc(LS1, go * b2)
            self.acc(DB, self.gb[at, :].astype(F32))
            g = self.gn2[at, :]
            self.acc(N2G, g * sc)
            self.acc(N2S, g)
            gm = go + norm_back(g, self.n2g[...], sc, inv)
            self.acc(LS0, gm * b1)
            gb1 = (ls0 * gm).astype(BF16)
            self.gb[at, :] = gb1
            self.acc(PB, gb1.astype(F32))
            self.gn2[at, :] = gm

    def io_copy(self, i):
        src, dst = ((self.h_tok, self.tok), (self.h_cot, self.cot), (self.tok, self.h_out),
                    (self.cot, self.h_gtok))[i]
        return pltpu.make_async_copy(src, dst, self.io_sem.at[i])

    def output(self):
        self.narrow(self.n2, self.tok)
        self.io_copy(2).start()

    def tokens(self):
        self.narrow(self.br2, self.cot)
        self.io_copy(3).start()

    def proj_back(self):
        gh = dot_nt(self.gb[...], self.w_proj()).astype(BF16)
        for t in range(6):
            self.ho[t] = gh[:, t * 128 : t * 128 + 128]

    def proj_grad(self, h):
        total = sum(
            dot(self.hot[i, pl.ds(h * 384, 384), :], self.gb[pl.ds(i * LP, LP), :])
            for i in range(self.images))
        for b in range(6):
            self.g_at[3, h, pl.ds(b * 384, 384), :] = total[
                :, b * 128 : b * 128 + 128].astype(BF16)

    def attend_back(self, t):
        for i in range(self.images):
            at = pl.ds(i * LP, LP)
            q0, q1 = self.two(self.q[t, at, :])
            d0, d1 = self.two(self.ho[t, at, :])
            k = self.k[t, at, :]
            v = self.v[t, at, :]
            kt = jnp.transpose(k)
            dq, dk, dv = [], 0.0, 0.0
            for e, (qe, de) in enumerate(((q0, d0), (q1, d1))):
                pb = self.pt[(t * self.images + i) * 2 + e]
                p = pb.astype(F32)
                gp = dot_nt(v, de)
                gs = (p * (gp - jnp.sum(gp * p, axis=0, keepdims=True))).astype(BF16)
                dv = dv + dot(pb, de)
                dk = dk + dot(gs, qe)
                dq.append(dot(kt[e * 64 : e * 64 + 64, :], gs))
            dq = jnp.transpose(jnp.concatenate(dq, axis=0)) * 0.125
            self.dqkv[at, 0:128] = dq.astype(BF16)
            self.dqkv[at, 128:256] = dk.astype(BF16)
            self.dqkv[at, 256:384] = dv.astype(BF16)
        self.qa[t] = fold(self.dqkv[:, 0:128].astype(F32))
        self.qa[8 + t] = fold(self.dqkv[:, 256:384].astype(F32))

    def qkv_back(self, j, h):
        self.br2[...] += dot_nt(self.dqkv[...], self.w_pair(j, h))
        grad = dot(self.n1t[...], self.dqkv[...])
        for p in range(3):
            self.g_at[j, h, pl.ds(p * D, D), :] = grad[
                :, p * 128 : p * 128 + 128].astype(BF16)

    def first_back(self, i):
        for at, _ in self.bands(i):
            sc, inv = normed(self.mixed[at, :])
            g = self.br2[at, :]
            self.acc(N1G, g * sc)
            self.acc(N1S, g)
            gx = self.gn2[at, :] + norm_back(g, self.n1g[...], sc, inv)
            mk = wide(self.maskp[at, :]) > 0.5
            self.acc(MTOK, jnp.where(mk, gx, 0.0))
            self.br2[at, :] = jnp.where(mk, 0.0, gx)

    def sums(self, vec):
        vec[...] = jnp.zeros_like(vec)
        for s in range(NSUM):
            vec[s : s + 1, :] = jnp.sum(
                self.vacc[pl.ds(s * 8, 8), :], axis=0, keepdims=True)
        for h, (qv, up) in enumerate(((QVO, UPO), (QVX, UPX))):
            for w in range(2):
                for j in range(3):
                    c = w * 384 + j * 128
                    vec[qv : qv + 1, c : c + 128] = jnp.sum(
                        self.qa[8 * w + h * 3 + j], axis=0, keepdims=True)
            for j in range(6):
                c = j % 3 * 256
                vec[up + j // 3 : up + j // 3 + 1, c : c + 256] = jnp.sum(
                    self.uba[h * 6 + j], axis=0, keepdims=True)


def layer_scratch(rows):
    n = rows // L
    padded = n * LP
    v = pltpu.VMEM
    return dict(
        tok=v((rows, D), BF16),
        cot=v((rows, D), BF16),
        io_sem=pltpu.SemaphoreType.DMA((4,)),
        small_sem=pltpu.SemaphoreType.DMA((len(SMALL),)),
        **{"in_" + name: v((D,), F32) for name in VECTORS},
        in_mask=v((rows,), jnp.int32),
        in_qvb=v((2, 384), F32),
        in_ls=v((2, D), F32),
        in_upb=v((1536,), F32),
        t32=v(((rows + 11 + 15) // 16 * 16 + 0, D), F32),
        mrow=v((128, (rows + 127) // 128 * 128), F32),
        mcol=v(((rows + 127) // 128 * 128, 128), F32),
        maskp=v((padded, 128), F32),
        mixed=v((padded, D), F32),
        gout=v((padded, D), BF16),
        n1=v((padded, D), BF16),
        n1t=v((D, padded), BF16),
        q=v((6, padded, 128), BF16),
        k=v((6, padded, 128), BF16),
        v=v((6, padded, 128), BF16),
        pt=v((6 * n * 2, LP, LP), BF16),
        ho=v((6, padded, 128), BF16),
        hot=v((n, D, LP), BF16),
        br1=v((padded, D), F32),
        n2=v((padded, D), BF16),
        n2t=v((D, padded), BF16),
        gb=v((padded, D), BF16),
        br2=v((padded, D), F32),
        gn2=v((padded, D), F32),
        dqkv=v((padded, 384), BF16),
        rows8=v((8, D), F32),
        vacc=v((NSUM * 8, D), F32),
        qb=v((16, 128), F32),
        ub=v((12, 256), F32),
        qa=v((16, 8, 128), F32),
        uba=v((12, 8, 256), F32),
    )


FF_ROWS, AT_ROWS = 3072, 2304
CHUNKS = tuple([("g_ff", j, FF_ROWS) for j in range(6)] + [("g_at", j, AT_ROWS) for j in range(4)])


Y_FIRST, Z_FIRST = (0, "y", 1, 2, 3), (0, 2, "y", 1, 3)
CUTS = {
    0: ((3, (0, 'y', 'F', 'M', 11), -44), (6, (0, 1, 'y', 'F', 'MM'), -11), (3, (0, 'y', 11, 'F', 'MM'), -8),),
    1: ((1, (0, 'y', 'F', 11, 'MM'), -54), (3, (0, 'y', 'F', 'M', 11), -8), (8, (0, 1, 'y', 'F', 'MM'), -31),),
    2: ((4, (0, 1, 'y', 'F', 'MM'), -23), (8, (0, 'y', 1, 'F', 'MM'), -27),),
    3: ((3, (0, 'y', 11, 'F', 'MM'), 45), (4, (0, 1, 'y', 'F', 'MM'), -3), (3, (0, 'F', 'M', 'y', 11), -6), (2, (0, 'F', 'M', 'y', 11), -60),),
    4: ((9, (0, 1, 'F', 'M', 'y'), -20), (3, (0, 'y', 1, 'F', 'MM'), -39),),
    5: ((7, (0, 'y', 1, 'F', 'MM'), -10), (5, (0, 'y', 1, 'F', 'MM'), 28),),
    9: ((9, (0, 'y', 1, 'F', 'MM'), -26),),
    6: ((4, (0, 'y', 1, 'F', 'M'), -43), (5, (0, 'y', 2, 1, 13), -14),),
    7: ((4, (0, 'y', 1, 'F', 'MM'), 35), (5, (0, 2, 'y', 1, 13), 32),),
    8: ((2, (0, 'F', 'M', 'y', 11), 7), (5, (0, 'y', 1, 'F', 'MM'), 1), (2, (0, 'y', 1, 'F', 'MM'), -18),),
}


def parts_of():
    out = []
    for k, cuts in CUTS.items():
        at = 0
        for units, order, weight in cuts:
            out.append((k, at, units * 256, order, weight))
            at += units * 256
    return tuple(out)


PARTS = parts_of()


def steps_of(part, bits):
    _, _, rows, order, _ = part
    order = list(order) + list(range(4, bits))
    both, role, out = True, "all", []
    for way in order:
        if way == "y":
            both = False
            out.append((way, False, rows, "all", role))
        elif way == "F":
            out.append((way, both, rows, "fold", "fold"))
            role = "inner"
        elif way == "MM" or (way != "M" and way >= 10):
            out.append(("M" if way == "MM" else way - 10, both, rows, "all", role))
        elif rows // 2 % 16 == 0:
            rows //= 2
            out.append((way, both, rows, "half", role))
        else:
            out.append((way, both, rows, "all", role))
    return out


def land_offsets(bits):
    sizes, table = [0, 0], {}
    for p, part in enumerate(PARTS):
        for i, (_, both, rows, *_) in enumerate(steps_of(part, bits)):
            table[p, i] = sizes[both]
            sizes[both] += rows
    return table, sizes


class Links:
    def __init__(self, r, bits):
        self.__dict__.update(r)
        self.bits = bits
        self.dp = lax.axis_index("dp")
        self.half = lax.axis_index("tensor")
        self.bit = [(self.dp // (1 << b)) % 2 for b in range(bits)]
        self.inner = self.bit[2] != self.bit[3]
        self.outer = self.bit[2] == self.bit[3]
        self.offsets, _ = land_offsets(bits)

    def peer(self, way):
        if way == "y":
            return (self.dp, 1 - self.half)
        if way in ("M", "MM"):
            return (self.dp + 4 * (1 - 2 * self.bit[2]) + 8 * (1 - 2 * self.bit[3]), self.half)
        if way in ("F", "U"):
            way = 2
        return (self.dp + (1 << way) * (1 - 2 * self.bit[way]), self.half)

    def greet(self):
        barrier = pltpu.get_barrier_semaphore()
        ways = ["y", "M"] + list(range(self.bits))
        for way in ways:
            pl.semaphore_signal(barrier, inc=1, device_id=self.peer(way), device_id_type=MESH)
        pl.semaphore_wait(barrier, len(ways))

    def copy(self, src, dst, send, recv, way):
        return pltpu.make_async_remote_copy(
            src_ref=src, dst_ref=dst, send_sem=send, recv_sem=recv,
            device_id=self.peer(way), device_id_type=MESH)

    def load(self, k):
        name, j, n = CHUNKS[k]
        sem = self.load_sem.at[k]
        if name == "g_ff":
            for b in range(6):
                pltpu.make_async_copy(
                    self.w_dn.at[pl.ds(j * 256, 256), pl.ds(b * 128, 128)],
                    self.g_ff.at[j, 0, pl.ds(b * 256, 256)], sem).start()
            for b in range(2):
                pltpu.make_async_copy(
                    self.w_up.at[:, pl.ds(j * 256 + b * 128, 128)],
                    self.g_ff.at[j, 0, pl.ds(1536 + b * D, D)], sem).start()
        elif j < 3:
            for p in range(3):
                pltpu.make_async_copy(
                    self.w_qkv.at[p, :, pl.ds(j * 128, 128)],
                    self.g_at.at[j, 0, pl.ds(p * D, D)], sem).start()
        else:
            for b in range(6):
                pltpu.make_async_copy(
                    self.w_pr.at[:, pl.ds(b * 128, 128)],
                    self.g_at.at[3, 0, pl.ds(b * 384, 384)], sem).start()

    def loaded(self, k):
        name, j, n = CHUNKS[k]
        ref = getattr(self, name).at[j, 0]
        pltpu.make_async_copy(ref, ref, self.load_sem.at[k]).wait()

    def bias(self, stage):
        a = self.copy(self.in_qvb, self.qvbx, self.b_send.at[0], self.b_recv.at[0], "y")
        b = self.copy(self.in_upb, self.upbx, self.b_send.at[1], self.b_recv.at[1], "y")
        if stage == 0:
            a.start()
            b.start()
            return
        a.wait()
        b.wait()
        for h, (qv, up) in enumerate(((self.in_qvb, self.in_upb), (self.qvbx, self.upbx))):
            for j in range(3):
                for w in range(2):
                    row = 8 * w + h * 3 + j
                    self.qb[row : row + 1, :] = qv[w : w + 1, j * 128 : j * 128 + 128]
            for j in range(6):
                row = h * 6 + j
                self.ub[row : row + 1, :] = up[pl.ds(j * 256, 256)][None, :]

    def gather_copy(self, k, sub, i):
        name, j, n = CHUNKS[k]
        ref = getattr(self, name)
        ways = ROUTES[k][sub]
        way, rows = gather_plan(k, sub)[i]
        size = n // 4
        off = self.bit[0] * (n // 2) + sub * size
        for further in ways[:0:-1][: len(ways) - max(i, 1)]:
            size //= 2
            off = off + self.bit[further] * size
        at = pl.ds(pl.multiple_of(off, 16), rows)
        return self.copy(
            ref.at[j, int(i > 0), at], ref.at[j, 1, at],
            self.w_send.at[k * 2 + sub, i], self.w_recv.at[k * 2 + sub, i], way)

    def gather(self, k, sub, stage):
        copies = len(gather_plan(k, sub))
        if stage < 0:
            for i in range(copies):
                self.gather_copy(k, sub, i).wait_send()
            return
        if stage > 0:
            self.gather_copy(k, sub, stage - 1).wait_recv()
        if stage < copies:
            self.gather_copy(k, sub, stage).start()

    def add(self, dst, dst_at, src, src_at, rows):
        size = next(s for s in (256, 192, 144, 128, 112, 96, 80, 64, 48, 32, 16) if rows % s == 0)

        @pl.loop(0, rows // size)
        def _(b):
            to = pl.ds(pl.multiple_of(dst_at + b * size, 16), size)
            of = pl.ds(pl.multiple_of(src_at + b * size, 16), size)
            total = dst[to, :].astype(F32) + src[of, :].astype(F32)
            dst[to, :] = total.astype(BF16)

    def when(self, role):
        if role == "all":
            return lambda body: body()
        return pl.when(self.outer if role == "fold" else self.inner)

    def reduce_steps(self, p):
        part = PARTS[p]
        k, first, rows = part[:3]
        name, j, _ = CHUNKS[k]
        ref = getattr(self, name)
        own = ref.at[j, 0]
        at, out, back = first, [], []
        other = {"all": "all", "inner": "inner", "fold": "unfold", "unfold": "fold"}

        def add(way, src, dst, adds, kind, role):
            i = len(out)

            def build():
                return self.copy(src(), dst(), self.r_send.at[p], self.r_recv.at[p, i], way)

            out.append((way, build, adds, kind, role, other[role]))

        def rows_of(r, at, rows):
            return lambda: r.at[pl.ds(pl.multiple_of(at, 16), rows)]

        def both_of(r, at, rows):
            return lambda: r.at[:, pl.ds(pl.multiple_of(at, 16), rows)]

        for way, both, rows, kind, role in steps_of(part, self.bits):
            o = self.offsets[p, len(out)]
            away = at
            if kind == "half":
                b = self.bit[3 if way == "M" else way]
                away = at + (1 - b) * rows
                at = at + b * rows
                back.append((way, at, rows, role))
            elif kind == "fold":
                back.append(("U", at, rows, "unfold"))
            if both:
                add(way, both_of(ref.at[j], away, rows), both_of(self.land2, o, rows),
                    [(ref.at[j, h], at, self.land2.at[h], o, rows) for h in range(2)], kind, role)
            else:
                src = ref.at[j, 1] if way == "y" else own
                add(way, rows_of(src, away, rows), rows_of(self.land, o, rows),
                    [(own, at, self.land, o, rows)], kind, role)
        for way, at, rows, role in back[::-1]:
            add(way, rows_of(own, at, rows), rows_of(own, at, rows), [], "back", role)
        return out

    def credit_of(self, p, way):
        return self.credit.at[p, {"F": 2, "U": 2, "M": 3}.get(way, way)]

    def result_copy(self, p):
        k, first, rows = PARTS[p][:3]
        name, j, _ = CHUNKS[k]
        out = self.o_ff if name == "g_ff" else self.o_at
        at = pl.ds(first, rows)
        return pltpu.make_async_copy(
            getattr(self, name).at[j, 0, at], out.at[j, at], self.out_sem.at[p])

    def reduce(self, p, stage):
        steps = self.reduce_steps(p)
        if stage > 0:
            way, build, adds, kind, sender, receiver = steps[stage - 1]

            def taken():
                build().wait_recv()

            def sent():
                build().wait_send()
                if kind in ("half", "fold"):
                    pl.semaphore_signal(
                        self.credit_of(p, way), inc=1, device_id=self.peer(way),
                        device_id_type=MESH)

            def summed():
                for one in adds:
                    self.add(*one)

            self.when(receiver)(taken)
            self.when(sender)(sent)
            if adds:
                self.when(receiver)(summed)
        if stage < len(steps):
            way, build, adds, kind, sender, receiver = steps[stage]

            def go():
                if kind == "back":
                    pl.semaphore_wait(self.credit_of(p, way), 1)
                build().start()

            self.when(sender)(go)
        else:
            self.result_copy(p).start()

    def finish(self, p):
        self.result_copy(p).wait()

    def vec_copy(self, s):
        way = (0, "y")[s] if s < 2 else s - 1
        return self.copy(self.vb.at[s], self.vr.at[s], self.v_send.at[s], self.v_recv.at[s], way)

    def vec(self, stage):
        if stage > 0:
            s = stage - 1
            self.vec_copy(s).wait_recv()
            if s == 1:
                self.vb[2, 0:NSUM, :] = self.vb[1, 0:NSUM, :] + self.vr[1, 0:NSUM, :]
                self.vb[2, QVO:QVX, :] = self.vb[1, QVO:QVX, :] + self.vr[1, QVX : QVX + 3, :]
                self.vb[2, QVX:NVEC, :] = jnp.zeros((NVEC - QVX, D), F32)
            else:
                self.vb[stage] = self.vb[s] + self.vr[s]
        if stage < self.bits + 1:
            self.vec_copy(stage).start()

    def vec_end(self):
        for s in range(self.bits + 1):
            self.vec_copy(s).wait_send()
        self.vec_out().start()

    def vec_out(self):
        return pltpu.make_async_copy(self.vb.at[self.bits + 1], self.o_vec, self.vec_sem.at[0])


def link_scratch(bits):
    v, dma = pltpu.VMEM, pltpu.SemaphoreType.DMA
    steps = 2 * bits + 1
    parts = len(PARTS)
    land = land_offsets(bits)[1]
    return dict(
        g_ff=v((6, 2, FF_ROWS, 128), BF16),
        g_at=v((4, 2, AT_ROWS, 128), BF16),
        land2=v((2, land[1], 128), BF16),
        land=v((land[0], 128), BF16),
        qvbx=v((2, 384), F32),
        upbx=v((1536,), F32),
        vb=v((bits + 2, NVEC, D), F32),
        vr=v((bits + 1, NVEC, D), F32),
        load_sem=dma((10,)),
        out_sem=dma((parts,)),
        b_send=dma((2,)),
        b_recv=dma((2,)),
        w_send=dma((20, 4)),
        w_recv=dma((20, 4)),
        r_send=dma((parts,)),
        r_recv=dma((parts, steps)),
        credit=pltpu.SemaphoreType.REGULAR((parts, bits)),
        v_send=dma((bits + 1,)),
        vec_sem=dma((1,)),
        v_recv=dma((bits + 1,)),
    )


ROUTES = ((('y', 1, 2), ('y', 2)), (('y', 1, 2), ('y', 2)), (('y', 1, 2), ('y', 1)), (('y', 2, 1), ('y', 1, 2)), (('y', 1, 2), ('y', 2)), (('y',), ('y', 2)), (('y', 2, 1), ('y', 1, 2)), (('y', 2), ('y', 2, 1)), (('y', 1, 2), ('y', 1)), (('y', 2), ('y', 2, 1)))
GATHER_ORDER = (6, 7, 8, 9, 0, 1, 2, 3, 4, 5)


def gather_plan(k, sub):
    rows, ways = CHUNKS[k][2] // 4, ROUTES[k][sub]
    n = len(ways)
    steps = [("y", rows >> (n - 1))]
    steps += [(way, rows >> (n - 1 - i)) for i, way in enumerate(ways[1:])]
    return steps + [(0, rows)]


SLACK, STEP, BACKLOG = 0.2, 0.05, 2.372
HOPS = {0: 0.9, "y": 2.2, 1: 2.2, 2: 2.2, "F": 2.2, "U": 2.2, "M": 2.2}
FAR_HOP = 2.7
LINK, CORES, SUMS, MESSAGE, LOADS, ENTRY = 45.5e3, 480e3, 2.4e6, 0.1, 3.0e6, 3.8
LINES = {
    0: (("c", 1),), "y": (("y", 1),), 1: (("x", 1),), 2: (("zi", 1), ("zo", 1)), "F": (("zi", 1),),
    "U": (("zo", 1),), "M": (("mid", 1),), "MM": (("mid", 1),)}
FAR_LINES = (("zi", 1), ("zo", 1), ("mid", 2))


def compute_pieces():
    out = [("start", 0.5, None)]
    out += [(("qa", t, s), (0.57, 1.45)[s], None) for t in range(3) for s in range(2)]
    out += [("start2", 1.7, None)]
    out += [(("qa", t, s), (0.57, 1.45)[s], 3 + t if s == 0 else None)
            for t in range(3, 6) for s in range(2)]
    out += [("project", 1.6, 9), ("second_norm", 0.8, None), ("turn", 0.6, None)]
    out += [(("feed", u, 0), 1.96, u // 2 if u % 2 == 0 else None) for u in range(12)]
    out += [(("middle_back", i, 0), 1.2, None) for i in range(3)]
    out += [("proj_back", 1.0, None), ("proj_grad", 1.6, None)]
    out += [(("back", u, s), (1.62, 1.4)[s], None) for u in range(6) for s in range(2)]
    out += [(("first_back", i, 0), 0.8, None) for i in range(3)]
    out += [("sums", 0.6, None), ("output", 0.6, None), ("tokens", 0.6, None)]
    after = {("feed", 2 * j + 1, 0): j for j in range(6)}
    after["proj_grad"] = 9
    after.update({("back", 2 * j + 1, 1): 6 + j for j in range(3)})
    return out, after


class Timeline:
    def __init__(self, bits, log=None):
        self.log = log or (lambda *a: None)
        self.now, self.order, self.tasks = ENTRY, [], {}
        self.free = {line: 0.0 for line in ("c", "y", "x", "zi", "zo", "mid")}
        self.moves, self.adds = {}, {}
        for k in range(10):
            self.moves["l", k] = []
            for sub in range(2):
                self.moves["w", k, sub] = [(way, rows * 256) for way, rows in gather_plan(k, sub)]
        for p, part in enumerate(PARTS):
            there = steps_of(part, bits)
            self.adds["r", p] = [rows * 256 * (1 + both) for _, both, rows, *_ in there]
            self.moves["r", p] = [
                (way, n) for (way, *_), n in zip(there, self.adds["r", p])
            ] + [("U" if kind == "fold" else way, rows * 256)
                 for way, _, rows, kind, _ in there[::-1] if kind in ("half", "fold")]
        self.moves["v", 0] = [
            (way, NVEC * D * 4) for way in (0, "y") + tuple(range(1, bits))]
        self.left = {
            key: [sum(self.took(*m) + HOPS.get(m[0], FAR_HOP) for m in moves[i:])
                  for i in range(len(moves) + 1)]
            for key, moves in self.moves.items()}

    def took(self, way, nbytes):
        return nbytes / CORES if way == 0 else nbytes / LINK + MESSAGE

    def urgency(self, key):
        if key[0] == "l":
            return 2000
        if key[0] == "w":
            return 1000 - GATHER_ORDER.index(key[1]) * 10 + self.tasks[key][0]
        weight = PARTS[key[1]][4] if key[0] == "r" else 0
        return self.left[key][self.tasks[key][0]] + weight

    def opens(self, key):
        stage, ready = self.tasks[key]
        if stage < len(self.moves[key]):
            way = self.moves[key][stage][0]
            if way != 0:
                for line, _ in LINES.get(way, FAR_LINES):
                    ready = max(ready, self.free[line] - BACKLOG)
        return ready

    def step(self, key):
        stage, ready = self.tasks[key]
        self.order.append(key + (stage,))
        self.log("op", self.now, key, stage, ready)
        self.now = max(self.now, ready) + STEP
        if 0 < stage <= len(self.adds.get(key, ())):
            self.now += self.adds[key][stage - 1] / SUMS
        if stage == len(self.moves[key]):
            del self.tasks[key]
            if key[0] == "l":
                for sub in range(2):
                    self.tasks["w", key[1], sub] = (0, self.now)
            return
        way, nbytes = self.moves[key][stage]
        lines = LINES.get(way, FAR_LINES)
        begin = max([self.now] + [self.free[line] for line, _ in lines])
        for line, load in lines:
            self.free[line] = begin + self.took(way, nbytes) * load
            self.log("x", line, begin, self.free[line])
        done = max(self.free[line] for line, _ in lines)
        self.tasks[key] = (stage + 1, done + HOPS.get(way, FAR_HOP))

    def poll(self, slack):
        while True:
            ready = [key for key in self.tasks if self.opens(key) + slack <= self.now]
            if not ready:
                return
            self.step(max(ready, key=self.urgency))

    def wait(self):
        self.now = max(self.now, min(self.opens(key) for key in self.tasks) + 1e-6)
        self.poll(0.0)

    def run(self):
        loaded = ENTRY
        for k in GATHER_ORDER:
            loaded += CHUNKS[k][2] * 256 / LOADS
            self.tasks["l", k] = (0, loaded)
        pieces, after = compute_pieces()
        for piece, took, needs in pieces:
            self.poll(SLACK)
            if needs is not None:
                mine = (("l", needs), ("w", needs, 0), ("w", needs, 1))
                while any(key in self.tasks for key in mine):
                    self.wait()
                self.order += [("w", needs, 0, -1), ("w", needs, 1, -1)]
            self.order.append(("c", piece))
            self.log("c", self.now, piece)
            self.now += took
            if piece in after:
                for p, part in enumerate(PARTS):
                    if part[0] == after[piece]:
                        self.tasks["r", p] = (0, self.now)
            if piece == "sums":
                self.tasks["v", 0] = (0, self.now)
        while self.tasks:
            self.wait()
        return self.order, self.now


def timeline(bits, log=None):
    return Timeline(bits, log).run()


def layer_kernel(bits, rows, names, *refs):
    r = dict(zip(names, refs))
    y = Layer(r, rows)
    links = Links(r, bits)
    order, _ = timeline(bits)
    links.load(GATHER_ORDER[0])
    y.io_copy(0).start()
    for i in range(len(SMALL)):
        y.small_copy(i).start()
    for k in GATHER_ORDER[1:]:
        links.load(k)
    y.io_copy(1).start()
    links.greet()
    y.vectors()
    links.bias(0)

    def link_step(op):
        if op[0] == "l":
            links.loaded(op[1])
        elif op[0] == "w":
            links.gather(*op[1:])
        elif op[0] == "r":
            links.reduce(op[1], op[2])
        else:
            links.vec(op[2])

    def attend(t, s):
        if s == 0:
            y.qkv(lax.rem(t, 3), t // 3)
        else:
            y.attend(t)

    def feed(u, s):
        y.feed(u // 2, 1 - lax.rem(u, 2))

    def back(u, s):
        j, h = u // 2, 1 - lax.rem(u, 2)
        if s == 0:
            y.attend_back(h * 3 + j)
        else:
            y.qkv_back(j, h)

    loops = {
        "qa": (attend, 2),
        "feed": (feed, 1),
        "middle_back": (lambda i, s: y.middle_back(i), 1),
        "back": (back, 2),
        "first_back": (lambda i, s: y.first_back(i), 1),
    }

    def proj_grad():
        y.proj_grad(1)
        y.proj_grad(0)

    single = {
        "start": y.start,
        "start2": y.start2,
        "project": y.project,
        "second_norm": y.second_norm,
        "turn": y.turn,
        "proj_back": y.proj_back,
        "proj_grad": proj_grad,
        "sums": lambda: y.sums(links.vb.at[0]),
        "output": y.output,
        "tokens": y.tokens,
    }

    at = 0
    first_pass = True
    while at < len(order):
        op = order[at]
        if op[0] != "c":
            link_step(op)
            at += 1
            continue
        if isinstance(op[1], str):
            if op[1] == "start":
                single["start"]()
                links.bias(1)
            else:
                single[op[1]]()
            at += 1
            continue
        kind = op[1][0]
        body, slots = loops[kind]
        end, last = at, at
        while end < len(order):
            o = order[end]
            if o[0] == "c":
                if isinstance(o[1], str) or o[1][0] != kind:
                    break
                last = end
            end += 1
        before = {}
        pending = []
        for o in order[at : last + 1]:
            if o[0] == "c":
                before[o[1][1], o[1][2]] = pending
                pending = []
            else:
                pending.append(o)
        low = op[1][1]
        high = order[last][1][1] + 1

        @pl.loop(low, high)
        def _(t):
            for s in range(slots):
                for u in range(low, high):
                    if before[u, s]:
                        @pl.when(t == u)
                        def _(ops=before[u, s]):
                            for o in ops:
                                link_step(o)
                body(t, s)

        at = last + 1
    links.vec_end()
    for i in (2, 3):
        y.io_copy(i).wait()
    for p in range(len(PARTS)):
        links.finish(p)
    links.vec_out().wait()


INPUTS = ("h_tok", "h_mask", "h_mtok", "h_n1g", "h_n1s", "h_qvb", "h_pb", "h_ls", "h_n2g", "h_n2s",
          "h_upb", "h_db", "h_cot", "w_qkv", "w_pr", "w_up", "w_dn")
OUTPUTS = ("h_out", "h_gtok", "o_ff", "o_at", "o_vec")


FF_OUT, AT_OUT = 6, 4


def finish_kernel(ff, at, vec, o1, o2, p1, p2, wu, wd, wq, wp, mt, g1, s1, qv, pb, ls, g2, s2, ub, db,
                  ff_in, at_in, vec_in, rows_in, up, down, three, proj, mt_v, g1_v, s1_v, qv_v, pb_v,
                  ls_v, g2_v, s2_v, ub_v, db_v, in_sem, out_sem):
    order = [("at", j) for j in range(AT_OUT)] + [("ff", j) for j in range(FF_OUT)]
    loads = [
        pltpu.make_async_copy(*((ff.at[j], ff_in.at[j]) if kind == "ff" else (at.at[j], at_in.at[j])),
                              in_sem.at[i])
        for i, (kind, j) in enumerate(order)]
    loads += [pltpu.make_async_copy(o, rows_in.at[i], in_sem.at[10 + i])
              for i, o in enumerate((o1, o2))]
    sums = pltpu.make_async_copy(vec, vec_in, in_sem.at[12])
    stores = []
    for load in loads[:4] + [sums] + loads[4:]:
        load.start()

    def send(src, dst):
        copy = pltpu.make_async_copy(src, dst, out_sem.at[len(stores)])
        copy.start()
        stores.append(copy)

    for i, ((kind, j), load) in enumerate(zip(order, loads)):
        load.wait()
        if kind == "ff":
            for b in range(6):
                down[j, :, b * 128 : b * 128 + 128] = ff_in[j, pl.ds(b * 256, 256), :].astype(F32)
            send(down.at[j], wd.at[pl.ds(j * 256, 256), :])
            for b in range(2):
                up[j, :, b * 128 : b * 128 + 128] = ff_in[j, pl.ds(1536 + b * D, D), :].astype(F32)
            send(up.at[j], wu.at[:, pl.ds(j * 256, 256)])
        elif j < 3:
            for p in range(3):
                three[j, p] = at_in[j, pl.ds(p * D, D), :].astype(F32)
            send(three.at[j], wq.at[:, :, pl.ds(j * 128, 128)])
        else:
            for b in range(6):
                proj[:, b * 128 : b * 128 + 128] = at_in[j, pl.ds(b * 384, 384), :].astype(F32)
            send(proj, wp)
        if i == 4:
            sums.wait()
            for ref, row in ((mt_v, MTOK), (g1_v, N1G), (s1_v, N1S), (pb_v, PB), (g2_v, N2G),
                             (s2_v, N2S), (db_v, DB)):
                ref[...] = vec_in[row, :]
            ls_v[...] = vec_in[LS0 : LS1 + 1, :]
            for w in range(2):
                qv_v[w : w + 1, :] = vec_in[QVO : QVO + 1, w * 384 : w * 384 + 384]
                ub_v[pl.ds(w * D, D)] = vec_in[UPO + w, :]
            for pair in ((mt_v, mt), (g1_v, g1), (s1_v, s1), (qv_v, qv), (pb_v, pb), (ls_v, ls),
                         (g2_v, g2), (s2_v, s2), (ub_v, ub), (db_v, db)):
                send(*pair)
    for i, p in enumerate((p1, p2)):
        loads[10 + i].wait()
        send(rows_in.at[i], p)
    for store in stores:
        store.wait()


def local(dp, tokens, patch_mask, mask_token, norm1_gain, norm1_shift, w_qkv, qv_bias, w_proj,
          proj_bias, layer_scales, norm2_gain, norm2_shift, w_up, up_bias, w_down, down_bias,
          cotangent):
    bits = dp.bit_length() - 1
    rows = tokens.shape[0]
    scratch = {**layer_scratch(rows), **link_scratch(bits)}
    hbm = pl.BlockSpec(memory_space=pl.ANY)
    shape = jax.ShapeDtypeStruct
    out, gtok, ff, at, vec = pl.pallas_call(
        functools.partial(layer_kernel, bits, rows, INPUTS + OUTPUTS + tuple(scratch)),
        name="layer",
        in_specs=[hbm] * 17,
        out_specs=[hbm] * 5,
        out_shape=[
            shape((rows, D), BF16),
            shape((rows, D), BF16),
            shape((6, FF_ROWS, 128), BF16),
            shape((4, AT_ROWS, 128), BF16),
            shape((NVEC, D), F32),
        ],
        scratch_shapes=list(scratch.values()),
        compiler_params=pltpu.CompilerParams(
            collective_id=0, has_side_effects=True, vmem_limit_bytes=63 * 2**20),
        cost_estimate=pl.CostEstimate(
            flops=27 * 10**9, bytes_accessed=20 * 10**6, transcendentals=10**7),
    )(
        tokens, patch_mask, mask_token, norm1_gain, norm1_shift, qv_bias, proj_bias,
        layer_scales, norm2_gain, norm2_shift, up_bias, down_bias, cotangent, w_qkv, w_proj,
        w_up, w_down,
    )
    one, flat = shape((D,), F32), pltpu.VMEM((D,), F32)
    out, gtok, wu, wd, wq, wp, mt, g1, s1, qv, pb, ls, g2, s2, ub, db = pl.pallas_call(
        finish_kernel,
        name="finish",
        in_specs=[hbm] * 5,
        out_specs=[hbm] * 16,
        out_shape=[
            shape((rows, D), BF16), shape((rows, D), BF16),
            shape((D, 1536), F32), shape((1536, D), F32), shape((3, D, 384), F32),
            shape((384, D), F32), one, one, one, shape((2, 384), F32), one, shape((2, D), F32),
            one, one, shape((2 * D,), F32), one,
        ],
        scratch_shapes=[
            pltpu.VMEM((6, FF_ROWS, 128), BF16), pltpu.VMEM((4, AT_ROWS, 128), BF16),
            pltpu.VMEM((NVEC, D), F32), pltpu.VMEM((2, rows, D), BF16),
            pltpu.VMEM((6, D, 256), F32), pltpu.VMEM((6, 256, D), F32),
            pltpu.VMEM((3, 3, D, 128), F32), pltpu.VMEM((384, D), F32),
            flat, flat, flat, pltpu.VMEM((2, 384), F32), flat, pltpu.VMEM((2, D), F32), flat, flat,
            pltpu.VMEM((2 * D,), F32), flat,
            pltpu.SemaphoreType.DMA((13,)), pltpu.SemaphoreType.DMA((28,)),
        ],
        compiler_params=pltpu.CompilerParams(vmem_limit_bytes=62 * 2**20),
    )(ff, at, vec, out, gtok)
    return out, gtok, mt, g1, s1, wq, qv, wp, pb, ls, g2, s2, wu, ub, wd, db


def solution(mesh):
    rows2, both = P(("dp", "tensor"), None), P(("dp", "tensor"))
    return jax.shard_map(
        functools.partial(local, mesh.shape["dp"]),
        mesh=mesh,
        in_specs=(
            rows2, both, P(), P(), P(), P(None, None, "tensor"), P(None, "tensor"),
            P("tensor", None), P(), P(), P(), P(), P(None, "tensor"), P("tensor"),
            P("tensor", None), P(), rows2,
        ),
        out_specs=(
            rows2, rows2, P(), P(), P(), P(None, None, "tensor"), P(None, "tensor"),
            P("tensor", None), P(), P(), P(), P(), P(None, "tensor"), P("tensor"),
            P("tensor", None), P(),
        ),
        check_vma=False,
    )
```

```python
import functools

import jax
import jax.numpy as jnp
from jax import lax
from jax.experimental import pallas as pl
from jax.experimental.pallas import tpu as pltpu
from jax.sharding import PartitionSpec as P

MESH = pl.DeviceIdType.MESH
F32 = jnp.float32
BF16 = jnp.bfloat16
L = 197
LP = 208
D = 768
EPS = 1e-06
INV_ROOT2 = 0.7071067811865476
INV_ROOT2PI = 0.3989422804014327

MTOK, N1G, N1S, PB, LS0, LS1, N2G, N2S, DB, QVO, UPO, QVX, UPX = (
    0, 1, 2, 3, 4, 5, 6, 7, 8, 9, 10, 12, 13)
NSUM = 9
NVEC = 16


def dot(a, b):
    return lax.dot_general(a, b, (((1,), (0,)), ((), ())), preferred_element_type=F32)


def dot_nt(a, b):
    return lax.dot_general(a, b, (((1,), (1,)), ((), ())), preferred_element_type=F32)


def fold(x):
    return jnp.sum(x.reshape(x.shape[0] // 8, 8, x.shape[1]), axis=0)


def normed(rows):
    centred = rows - jnp.mean(rows, axis=-1, keepdims=True)
    inverse = lax.rsqrt(jnp.mean(centred * centred, axis=-1, keepdims=True) + EPS)
    return centred * inverse, inverse


def norm_back(grad, gain, scaled, inverse):
    weighted = grad * gain
    inner = (
        weighted
        - jnp.mean(weighted, axis=-1, keepdims=True)
        - scaled * jnp.mean(weighted * scaled, axis=-1, keepdims=True)
    )
    return inverse * inner


def wide(column):
    return jnp.concatenate([column] * (D // 128), axis=1)


BLOCKS = ((0, 48), (48, 48), (96, 48), (144, 48), (192, 16))


VECTORS = ("mtok", "n1g", "n1s", "pb", "n2g", "n2s", "db")
SMALL = VECTORS + ("mask", "qvb", "ls", "upb")


class Layer:
    def __init__(self, r, rows):
        self.__dict__.update(r)
        self.rows = rows
        self.images = rows // L
        self.padded = self.images * LP

    def widen(self, src):
        n = self.rows // 16

        @pl.loop(0, n)
        def _(b):
            at = pl.ds(pl.multiple_of(b * 16, 16), 16)
            self.t32[at, :] = src[at, :].astype(F32)

        left = self.rows - n * 16
        if left:
            self.t32[n * 16 : self.rows, :] = src[n * 16 : self.rows, :].astype(F32)

    def narrow(self, src, dst):
        for i in range(self.images):
            for r, n in BLOCKS:
                n = min(n, L - r)
                self.t32[pl.ds(L * i + r, n), :] = src[pl.ds(LP * i + r, n), :].astype(F32)
        n = self.rows // 16

        @pl.loop(0, n)
        def _(b):
            at = pl.ds(pl.multiple_of(b * 16, 16), 16)
            dst[at, :] = self.t32[at, :].astype(BF16)

        left = self.rows - n * 16
        if left:
            dst[n * 16 : self.rows, :] = self.t32[n * 16 : self.rows, :].astype(BF16)

    def bands(self, i):
        for r, n in BLOCKS:
            yield pl.ds(pl.multiple_of(i * LP + r, 16), n), n

    def acc(self, at, x):
        self.vacc[pl.ds(at * 8, 8), :] += fold(x)

    def small_copy(self, i):
        name = SMALL[i]
        return pltpu.make_async_copy(
            getattr(self, "h_" + name), getattr(self, "in_" + name), self.small_sem.at[i])

    def vectors(self):
        for i in range(len(SMALL)):
            self.small_copy(i).wait()
        for name in VECTORS:
            self.__dict__[name] = self.rows8.at[pl.ds(VECTORS.index(name), 1), :]
            self.rows8[VECTORS.index(name), :] = self.__dict__["in_" + name][...]

    def start(self):
        self.vacc[...] = jnp.zeros_like(self.vacc)
        rows = self.rows
        self.mrow[...] = jnp.zeros_like(self.mrow)
        flags = jnp.where(self.in_mask[...] == 1, 1.0, 0.0).astype(F32)[None, :]
        self.mrow[:, pl.ds(0, rows)] = jnp.broadcast_to(flags, (128, rows))
        self.mcol[...] = jnp.transpose(self.mrow[...])
        self.t32[pl.ds(rows, self.t32.shape[0] - rows), :] = jnp.zeros(
            (self.t32.shape[0] - rows, D), F32)
        self.io_copy(0).wait()
        self.widen(self.tok)
        for i in range(self.images):
            for r, n in BLOCKS:
                at = pl.ds(L * i + r, n)
                to = pl.ds(LP * i + r, n)
                x = self.t32[at, :]
                mk = self.mcol[at, :]
                mx = jnp.where(wide(mk) > 0.5, self.mtok[...], x)
                if r + n > L:
                    keep = lax.broadcasted_iota(jnp.int32, (n, 128), 0) < L - r
                    mk = jnp.where(keep, mk, 0.0)
                    mx = jnp.where(wide(keep), mx, 0.0)
                self.maskp[to, :] = mk
                self.mixed[to, :] = mx
                sc, _ = normed(mx)
                self.n1[to, :] = (sc * self.n1g[...] + self.n1s[...]).astype(BF16)

    def turn1(self):
        self.n1t[...] = jnp.transpose(self.n1[...])

    def spread(self):
        self.io_copy(1).wait()
        self.widen(self.cot)
        for i in range(self.images):
            for r, n in BLOCKS:
                at = pl.ds(L * i + r, n)
                to = pl.ds(LP * i + r, n)
                go = self.t32[at, :] * wide(self.maskp[to, :])
                self.gout[to, :] = go.astype(BF16)
                self.gb[to, :] = (self.in_ls[1:2, :] * go).astype(BF16)

    def w_pair(self, j, h):
        return jnp.concatenate(
            [self.g_at[j, h, pl.ds(p * D, D), :] for p in range(3)], axis=1)

    def qkv(self, j, h):
        t = h * 3 + j
        proj = dot(self.n1[...], self.w_pair(j, h))
        qb = self.qb[pl.ds(t, 1), :]
        vb = self.qb[pl.ds(8 + t, 1), :]
        self.q[t] = ((proj[:, 0:128] + qb) * 0.125).astype(BF16)
        self.k[t] = proj[:, 128:256].astype(BF16)
        self.v[t] = (proj[:, 256:384] + vb).astype(BF16)

    def two(self, x):
        low = lax.broadcasted_iota(jnp.int32, x.shape, 1) < 64
        zero = jnp.zeros_like(x)
        return jnp.where(low, x, zero), jnp.where(low, zero, x)

    def softmax(self, s):
        tail = s[LP - 16 :]
        keep = lax.broadcasted_iota(jnp.int32, tail.shape, 0) < L - (LP - 16)
        s = jnp.concatenate([s[: LP - 16], jnp.where(keep, tail, -1e30)], axis=0)
        x = jnp.exp(s - jnp.max(s, axis=0, keepdims=True))
        return (x * (1.0 / jnp.sum(x, axis=0, keepdims=True))).astype(BF16)

    def attend(self, t):
        n = self.images
        rows = [pl.ds(i * LP, LP) for i in range(n)]
        scores = []
        for at in rows:
            k = self.k[t, at, :]
            scores.append([dot_nt(k, q) for q in self.two(self.q[t, at, :])])
        probs = [[self.softmax(s) for s in pair] for pair in scores]
        for i, at in enumerate(rows):
            vt = jnp.transpose(self.v[t, at, :])
            outs = []
            for e in range(2):
                self.pt[(t * n + i) * 2 + e] = probs[i][e]
                outs.append(dot(vt[e * 64 : e * 64 + 64, :], probs[i][e]))
            ot = jnp.concatenate(outs, axis=0).astype(BF16)
            self.hot[i, pl.ds(pl.multiple_of(t * 128, 128), 128), :] = ot
            self.ho[t, at, :] = jnp.transpose(ot)

    def w_proj(self):
        return jnp.concatenate(
            [
                jnp.concatenate(
                    [self.g_at[3, h, pl.ds(b * 384, 384), :] for b in range(6)], axis=1)
                for h in range(2)
            ],
            axis=0,
        )

    def project(self):
        o = jnp.concatenate([self.ho[t] for t in range(6)], axis=1)
        self.br1[...] = dot(o, self.w_proj()) + self.pb[...]

    def second_norm(self):
        for i in range(self.images):
            for at, rows in self.bands(i):
                middle = self.mixed[at, :] + self.in_ls[0:1, :] * self.br1[at, :]
                sc, _ = normed(middle)
                self.n2[at, :] = (sc * self.n2g[...] + self.n2s[...]).astype(BF16)

    def clear(self):
        self.br2[...] = jnp.zeros_like(self.br2)
        self.gn2[...] = jnp.zeros_like(self.gn2)

    def turn(self):
        self.n2t[...] = jnp.transpose(self.n2[...])

    def feed(self, j, h):
        wd = jnp.concatenate(
            [self.g_ff[j, h, pl.ds(b * 256, 256), :] for b in range(6)], axis=1)
        wu = jnp.concatenate(
            [self.g_ff[j, h, pl.ds(1536 + b * D, D), :] for b in range(2)], axis=1)
        row = h * 6 + j
        pre = dot(self.n2[...], wu) + self.ub[pl.ds(row, 1), :]
        ga = dot_nt(self.gb[...], wd)
        cdf = 0.5 * (1.0 + lax.erf(pre * INV_ROOT2))
        act = (pre * cdf).astype(BF16)
        gp = (ga * (cdf + pre * jnp.exp(-0.5 * pre * pre) * INV_ROOT2PI)).astype(BF16)
        self.br2[...] += dot(act, wd)
        gwd = dot(jnp.transpose(act), self.gb[...]).astype(BF16)
        self.gn2[...] += dot_nt(gp, wu)
        gwu = dot(self.n2t[...], gp).astype(BF16)
        self.uba[row] = fold(gp.astype(F32))
        for b in range(6):
            self.g_ff[j, h, pl.ds(b * 256, 256), :] = gwd[:, b * 128 : b * 128 + 128]
        for b in range(2):
            self.g_ff[j, h, pl.ds(1536 + b * D, D), :] = gwu[:, b * 128 : b * 128 + 128]

    def middle_back(self, i):
        ls0, ls1 = self.in_ls[0:1, :], self.in_ls[1:2, :]
        for at, rows in self.bands(i):
            b1 = self.br1[at, :]
            middle = self.mixed[at, :] + ls0 * b1
            sc, inv = normed(middle)
            b2 = self.br2[at, :] + self.db[...]
            self.n2[at, :] = (middle + ls1 * b2).astype(BF16)
            self.br2[at, :] = jnp.zeros((rows, D), F32)
            go = self.gout[at, :].astype(F32)
            self.acc(LS1, go * b2)
            self.acc(DB, self.gb[at, :].astype(F32))
            g = self.gn2[at, :]
            self.acc(N2G, g * sc)
            self.acc(N2S, g)
            gm = go + norm_back(g, self.n2g[...], sc, inv)
            self.acc(LS0, gm * b1)
            gb1 = (ls0 * gm).astype(BF16)
            self.gb[at, :] = gb1
            self.acc(PB, gb1.astype(F32))
            self.gn2[at, :] = gm

    def io_copy(self, i):
        src, dst = ((self.h_tok, self.tok), (self.h_cot, self.cot), (self.tok, self.h_out),
                    (self.cot, self.h_gtok))[i]
        return pltpu.make_async_copy(src, dst, self.io_sem.at[i])

    def output(self):
        self.narrow(self.n2, self.tok)
        self.io_copy(2).start()

    def tokens(self):
        self.narrow(self.br2, self.cot)
        self.io_copy(3).start()

    def proj_back(self):
        gh = dot_nt(self.gb[...], self.w_proj()).astype(BF16)
        for t in range(6):
            self.ho[t] = gh[:, t * 128 : t * 128 + 128]

    def proj_grad(self, h):
        total = sum(
            dot(self.hot[i, pl.ds(h * 384, 384), :], self.gb[pl.ds(i * LP, LP), :])
            for i in range(self.images))
        for b in range(6):
            self.g_at[3, h, pl.ds(b * 384, 384), :] = total[
                :, b * 128 : b * 128 + 128].astype(BF16)

    def attend_back(self, t):
        n = self.images
        rows = [pl.ds(i * LP, LP) for i in range(n)]
        grads = []
        for at in rows:
            v = self.v[t, at, :]
            grads.append([dot_nt(v, d) for d in self.two(self.ho[t, at, :])])
        scores = []
        for i in range(n):
            pair = []
            for e in range(2):
                p, gp = self.pt[(t * n + i) * 2 + e].astype(F32), grads[i][e]
                pair.append((p * (gp - jnp.sum(gp * p, axis=0, keepdims=True))).astype(BF16))
            scores.append(pair)
        for i, at in enumerate(rows):
            q, d = self.two(self.q[t, at, :]), self.two(self.ho[t, at, :])
            kt = jnp.transpose(self.k[t, at, :])
            gs = scores[i]
            dv = dot(self.pt[(t * n + i) * 2], d[0]) + dot(self.pt[(t * n + i) * 2 + 1], d[1])
            dk = dot(gs[0], q[0]) + dot(gs[1], q[1])
            dq = [dot(kt[e * 64 : e * 64 + 64, :], gs[e]) for e in range(2)]
            dq = jnp.transpose(jnp.concatenate(dq, axis=0)) * 0.125
            self.dqkv[at, 0:128] = dq.astype(BF16)
            self.dqkv[at, 128:256] = dk.astype(BF16)
            self.dqkv[at, 256:384] = dv.astype(BF16)
        self.qa[t] = fold(self.dqkv[:, 0:128].astype(F32))
        self.qa[8 + t] = fold(self.dqkv[:, 256:384].astype(F32))

    def qkv_back(self, j, h):
        self.br2[...] += dot_nt(self.dqkv[...], self.w_pair(j, h))
        grad = dot(self.n1t[...], self.dqkv[...])
        for p in range(3):
            self.g_at[j, h, pl.ds(p * D, D), :] = grad[
                :, p * 128 : p * 128 + 128].astype(BF16)

    def first_back(self, i):
        for at, _ in self.bands(i):
            sc, inv = normed(self.mixed[at, :])
            g = self.br2[at, :]
            self.acc(N1G, g * sc)
            self.acc(N1S, g)
            gx = self.gn2[at, :] + norm_back(g, self.n1g[...], sc, inv)
            mk = wide(self.maskp[at, :]) > 0.5
            self.acc(MTOK, jnp.where(mk, gx, 0.0))
            self.br2[at, :] = jnp.where(mk, 0.0, gx)

    def sums(self, vec):
        vec[...] = jnp.zeros_like(vec)
        for s in range(NSUM):
            vec[s : s + 1, :] = jnp.sum(
                self.vacc[pl.ds(s * 8, 8), :], axis=0, keepdims=True)
        for h, (qv, up) in enumerate(((QVO, UPO), (QVX, UPX))):
            for w in range(2):
                for j in range(3):
                    c = w * 384 + j * 128
                    vec[qv : qv + 1, c : c + 128] = jnp.sum(
                        self.qa[8 * w + h * 3 + j], axis=0, keepdims=True)
            for j in range(6):
                c = j % 3 * 256
                vec[up + j // 3 : up + j // 3 + 1, c : c + 256] = jnp.sum(
                    self.uba[h * 6 + j], axis=0, keepdims=True)


def layer_scratch(rows):
    n = rows // L
    padded = n * LP
    v = pltpu.VMEM
    return dict(
        tok=v((rows, D), BF16),
        cot=v((rows, D), BF16),
        io_sem=pltpu.SemaphoreType.DMA((4,)),
        small_sem=pltpu.SemaphoreType.DMA((len(SMALL),)),
        **{"in_" + name: v((D,), F32) for name in VECTORS},
        in_mask=v((rows,), jnp.int32),
        in_qvb=v((2, 384), F32),
        in_ls=v((2, D), F32),
        in_upb=v((1536,), F32),
        t32=v(((rows + 11 + 15) // 16 * 16 + 0, D), F32),
        mrow=v((128, (rows + 127) // 128 * 128), F32),
        mcol=v(((rows + 127) // 128 * 128, 128), F32),
        maskp=v((padded, 128), F32),
        mixed=v((padded, D), F32),
        gout=v((padded, D), BF16),
        n1=v((padded, D), BF16),
        n1t=v((D, padded), BF16),
        q=v((6, padded, 128), BF16),
        k=v((6, padded, 128), BF16),
        v=v((6, padded, 128), BF16),
        pt=v((6 * n * 2, LP, LP), BF16),
        ho=v((6, padded, 128), BF16),
        hot=v((n, D, LP), BF16),
        br1=v((padded, D), F32),
        n2=v((padded, D), BF16),
        n2t=v((D, padded), BF16),
        gb=v((padded, D), BF16),
        br2=v((padded, D), F32),
        gn2=v((padded, D), F32),
        dqkv=v((padded, 384), BF16),
        rows8=v((8, D), F32),
        vacc=v((NSUM * 8, D), F32),
        qb=v((16, 128), F32),
        ub=v((12, 256), F32),
        qa=v((16, 8, 128), F32),
        uba=v((12, 8, 256), F32),
    )


FF_ROWS, AT_ROWS = 3072, 2304
CHUNKS = tuple([("g_ff", j, FF_ROWS) for j in range(6)] + [("g_at", j, AT_ROWS) for j in range(4)])


Y_FIRST, Z_FIRST = (0, "y", 1, 2, 3), (0, 2, "y", 1, 3)
CUTS = {
    0: ((6, (0, 1, 'y', 'F', 'M'), -33), (6, (0, 'y', 1, 'F', 'MM'), -41),),
    1: ((3, (0, 1, 'y', 'F', 'M'), 28), (4, (0, 3, 2, 'y', 11), -25), (2, (0, 'y', 11, 'F', 'MM'), -56), (3, (0, 'y', 'F', 'M', 11), 10),),
    2: ((8, (0, 1, 'y', 'F', 'MM'), 46), (4, (0, 'y', 1, 'F', 'M'), -10),),
    3: ((3, (0, 'y', 'F', 'M', 11), 33), (3, (0, 'y', 1, 'F', 'MM'), -21), (6, (0, 1, 'y', 'F', 'MM'), -20),),
    4: ((7, (0, 2, 'y', 1, 13), -30), (5, (0, 'y', 1, 'F', 'MM'), -30),),
    5: ((4, (0, 'y', 'F', 'M', 1), 54), (8, (0, 1, 'y', 'F', 'MM'), 31),),
    9: ((7, (0, 'y', 1, 'F', 'M'), 55), (2, (0, 'y', 2, 3, 1), 15),),
    6: ((1, (0, 1, 'F', 'y', 'MM'), -25), (4, (0, 'y', 1, 'F', 'MM'), 46), (4, (0, 'y', 1, 'F', 'MM'), -27),),
    7: ((4, (0, 'y', 1, 'F', 'MM'), -1), (5, (0, 'y', 1, 'F', 'MM'), -10),),
    8: ((1, (0, 'y', 'F', 'M', 11), 12), (3, (0, 'y', 'F', 'M', 11), 43), (3, (0, 'y', 1, 'F', 'MM'), 5), (2, (0, 'y', 1, 'F', 'M'), 20),),
}


def parts_of():
    out = []
    for k, cuts in CUTS.items():
        at = 0
        for units, order, weight in cuts:
            out.append((k, at, units * 256, order, weight))
            at += units * 256
    return tuple(out)


PARTS = parts_of()


def steps_of(part, bits):
    _, _, rows, order, _ = part
    order = list(order) + list(range(4, bits))
    both, role, out = True, "all", []
    for way in order:
        if way == "y":
            both = False
            out.append((way, False, rows, "all", role))
        elif way == "F":
            out.append((way, both, rows, "fold", "fold"))
            role = "inner"
        elif way == "MM" or (way != "M" and way >= 10):
            out.append(("M" if way == "MM" else way - 10, both, rows, "all", role))
        elif rows // 2 % 16 == 0:
            rows //= 2
            out.append((way, both, rows, "half", role))
        else:
            out.append((way, both, rows, "all", role))
    return out


def land_offsets(bits):
    sizes, table = [0, 0], {}
    for p, part in enumerate(PARTS):
        for i, (_, both, rows, *_) in enumerate(steps_of(part, bits)):
            table[p, i] = sizes[both]
            sizes[both] += rows
    return table, sizes


class Links:
    def __init__(self, r, bits):
        self.__dict__.update(r)
        self.bits = bits
        self.dp = lax.axis_index("dp")
        self.half = lax.axis_index("tensor")
        self.bit = [(self.dp // (1 << b)) % 2 for b in range(bits)]
        self.inner = self.bit[2] != self.bit[3]
        self.outer = self.bit[2] == self.bit[3]
        self.offsets, _ = land_offsets(bits)

    def peer(self, way):
        if way == "y":
            return (self.dp, 1 - self.half)
        if way in ("M", "MM"):
            return (self.dp + 4 * (1 - 2 * self.bit[2]) + 8 * (1 - 2 * self.bit[3]), self.half)
        if way in ("F", "U"):
            way = 2
        return (self.dp + (1 << way) * (1 - 2 * self.bit[way]), self.half)

    def greet(self):
        barrier = pltpu.get_barrier_semaphore()
        ways = ["y", "M"] + list(range(self.bits))
        for way in ways:
            pl.semaphore_signal(barrier, inc=1, device_id=self.peer(way), device_id_type=MESH)
        pl.semaphore_wait(barrier, len(ways))

    def copy(self, src, dst, send, recv, way):
        return pltpu.make_async_remote_copy(
            src_ref=src, dst_ref=dst, send_sem=send, recv_sem=recv,
            device_id=self.peer(way), device_id_type=MESH)

    def load(self, k):
        name, j, n = CHUNKS[k]
        sem = self.load_sem.at[k]
        if name == "g_ff":
            for b in range(6):
                pltpu.make_async_copy(
                    self.w_dn.at[pl.ds(j * 256, 256), pl.ds(b * 128, 128)],
                    self.g_ff.at[j, 0, pl.ds(b * 256, 256)], sem).start()
            for b in range(2):
                pltpu.make_async_copy(
                    self.w_up.at[:, pl.ds(j * 256 + b * 128, 128)],
                    self.g_ff.at[j, 0, pl.ds(1536 + b * D, D)], sem).start()
        elif j < 3:
            for p in range(3):
                pltpu.make_async_copy(
                    self.w_qkv.at[p, :, pl.ds(j * 128, 128)],
                    self.g_at.at[j, 0, pl.ds(p * D, D)], sem).start()
        else:
            for b in range(6):
                pltpu.make_async_copy(
                    self.w_pr.at[:, pl.ds(b * 128, 128)],
                    self.g_at.at[3, 0, pl.ds(b * 384, 384)], sem).start()

    def loaded(self, k):
        name, j, n = CHUNKS[k]
        ref = getattr(self, name).at[j, 0]
        pltpu.make_async_copy(ref, ref, self.load_sem.at[k]).wait()

    def bias(self, stage):
        a = self.copy(self.in_qvb, self.qvbx, self.b_send.at[0], self.b_recv.at[0], "y")
        b = self.copy(self.in_upb, self.upbx, self.b_send.at[1], self.b_recv.at[1], "y")
        if stage == 0:
            a.start()
            b.start()
            return
        a.wait()
        b.wait()
        for h, (qv, up) in enumerate(((self.in_qvb, self.in_upb), (self.qvbx, self.upbx))):
            for j in range(3):
                for w in range(2):
                    row = 8 * w + h * 3 + j
                    self.qb[row : row + 1, :] = qv[w : w + 1, j * 128 : j * 128 + 128]
            for j in range(6):
                row = h * 6 + j
                self.ub[row : row + 1, :] = up[pl.ds(j * 256, 256)][None, :]

    def gather_copy(self, k, sub, i):
        name, j, n = CHUNKS[k]
        ref = getattr(self, name)
        ways = ROUTES[k][sub]
        way, rows = gather_plan(k, sub)[i]
        size = n // 4
        off = self.bit[0] * (n // 2) + sub * size
        for further in ways[:0:-1][: len(ways) - max(i, 1)]:
            size //= 2
            off = off + self.bit[further] * size
        at = pl.ds(pl.multiple_of(off, 16), rows)
        return self.copy(
            ref.at[j, int(i > 0), at], ref.at[j, 1, at],
            self.w_send.at[k * 2 + sub, i], self.w_recv.at[k * 2 + sub, i], way)

    def gather(self, k, sub, stage):
        copies = len(gather_plan(k, sub))
        if stage < 0:
            for i in range(copies):
                self.gather_copy(k, sub, i).wait_send()
            return
        if stage > 0:
            self.gather_copy(k, sub, stage - 1).wait_recv()
        if stage < copies:
            self.gather_copy(k, sub, stage).start()

    def add(self, dst, dst_at, src, src_at, rows):
        size = next(s for s in (256, 192, 144, 128, 112, 96, 80, 64, 48, 32, 16) if rows % s == 0)

        @pl.loop(0, rows // size)
        def _(b):
            to = pl.ds(pl.multiple_of(dst_at + b * size, 16), size)
            of = pl.ds(pl.multiple_of(src_at + b * size, 16), size)
            total = dst[to, :].astype(F32) + src[of, :].astype(F32)
            dst[to, :] = total.astype(BF16)

    def when(self, role):
        if role == "all":
            return lambda body: body()
        return pl.when(self.outer if role == "fold" else self.inner)

    def reduce_steps(self, p):
        part = PARTS[p]
        k, first, rows = part[:3]
        name, j, _ = CHUNKS[k]
        ref = getattr(self, name)
        own = ref.at[j, 0]
        at, out, back = first, [], []
        other = {"all": "all", "inner": "inner", "fold": "unfold", "unfold": "fold"}

        def add(way, src, dst, adds, kind, role):
            i = len(out)

            def build():
                return self.copy(src(), dst(), self.r_send.at[p], self.r_recv.at[p, i], way)

            out.append((way, build, adds, kind, role, other[role]))

        def rows_of(r, at, rows):
            return lambda: r.at[pl.ds(pl.multiple_of(at, 16), rows)]

        def both_of(r, at, rows):
            return lambda: r.at[:, pl.ds(pl.multiple_of(at, 16), rows)]

        for way, both, rows, kind, role in steps_of(part, self.bits):
            o = self.offsets[p, len(out)]
            away = at
            if kind == "half":
                b = self.bit[3 if way == "M" else way]
                away = at + (1 - b) * rows
                at = at + b * rows
                back.append((way, at, rows, role))
            elif kind == "fold":
                back.append(("U", at, rows, "unfold"))
            if both:
                add(way, both_of(ref.at[j], away, rows), both_of(self.land2, o, rows),
                    [(ref.at[j, h], at, self.land2.at[h], o, rows) for h in range(2)], kind, role)
            else:
                src = ref.at[j, 1] if way == "y" else own
                add(way, rows_of(src, away, rows), rows_of(self.land, o, rows),
                    [(own, at, self.land, o, rows)], kind, role)
        for way, at, rows, role in back[::-1]:
            add(way, rows_of(own, at, rows), rows_of(own, at, rows), [], "back", role)
        return out

    def credit_of(self, p, way):
        return self.credit.at[p, {"F": 2, "U": 2, "M": 3}.get(way, way)]

    def result_copy(self, p):
        k, first, rows = PARTS[p][:3]
        name, j, _ = CHUNKS[k]
        out = self.o_ff if name == "g_ff" else self.o_at
        at = pl.ds(first, rows)
        return pltpu.make_async_copy(
            getattr(self, name).at[j, 0, at], out.at[j, at], self.out_sem.at[p])

    def reduce(self, p, stage):
        steps = self.reduce_steps(p)
        if stage > 0:
            way, build, adds, kind, sender, receiver = steps[stage - 1]

            def taken():
                build().wait_recv()

            def sent():
                build().wait_send()
                if kind in ("half", "fold"):
                    pl.semaphore_signal(
                        self.credit_of(p, way), inc=1, device_id=self.peer(way),
                        device_id_type=MESH)

            def summed():
                for one in adds:
                    self.add(*one)

            self.when(receiver)(taken)
            self.when(sender)(sent)
            if adds:
                self.when(receiver)(summed)
        if stage < len(steps):
            way, build, adds, kind, sender, receiver = steps[stage]

            def go():
                if kind == "back":
                    pl.semaphore_wait(self.credit_of(p, way), 1)
                build().start()

            self.when(sender)(go)
        else:
            self.result_copy(p).start()

    def finish(self, p):
        self.result_copy(p).wait()

    def vec_copy(self, s):
        way = (0, "y")[s] if s < 2 else s - 1
        return self.copy(self.vb.at[s], self.vr.at[s], self.v_send.at[s], self.v_recv.at[s], way)

    def vec(self, stage):
        if stage > 0:
            s = stage - 1
            self.vec_copy(s).wait_recv()
            if s == 1:
                self.vb[2, 0:NSUM, :] = self.vb[1, 0:NSUM, :] + self.vr[1, 0:NSUM, :]
                self.vb[2, QVO:QVX, :] = self.vb[1, QVO:QVX, :] + self.vr[1, QVX : QVX + 3, :]
                self.vb[2, QVX:NVEC, :] = jnp.zeros((NVEC - QVX, D), F32)
            else:
                self.vb[stage] = self.vb[s] + self.vr[s]
        if stage < self.bits + 1:
            self.vec_copy(stage).start()

    def vec_end(self):
        for s in range(self.bits + 1):
            self.vec_copy(s).wait_send()
        self.vec_out().start()

    def vec_out(self):
        return pltpu.make_async_copy(self.vb.at[self.bits + 1], self.o_vec, self.vec_sem.at[0])


def link_scratch(bits):
    v, dma = pltpu.VMEM, pltpu.SemaphoreType.DMA
    steps = 2 * bits + 1
    parts = len(PARTS)
    land = land_offsets(bits)[1]
    return dict(
        g_ff=v((6, 2, FF_ROWS, 128), BF16),
        g_at=v((4, 2, AT_ROWS, 128), BF16),
        land2=v((2, land[1], 128), BF16),
        land=v((land[0], 128), BF16),
        qvbx=v((2, 384), F32),
        upbx=v((1536,), F32),
        vb=v((bits + 2, NVEC, D), F32),
        vr=v((bits + 1, NVEC, D), F32),
        load_sem=dma((10,)),
        out_sem=dma((parts,)),
        b_send=dma((2,)),
        b_recv=dma((2,)),
        w_send=dma((20, 4)),
        w_recv=dma((20, 4)),
        r_send=dma((parts,)),
        r_recv=dma((parts, steps)),
        credit=pltpu.SemaphoreType.REGULAR((parts, bits)),
        v_send=dma((bits + 1,)),
        vec_sem=dma((1,)),
        v_recv=dma((bits + 1,)),
    )


ROUTES = ((('y', 1, 2), ('y', 1)), (('y', 2), ('y', 1, 2)), (('y', 2, 1), ('y', 1)), (('y', 1, 2), ('y', 2)), (('y', 2), ('y', 1, 2)), (('y', 2), ('y', 2)), (('y', 1, 2), ('y', 2, 1)), (('y', 1, 2), ('y', 1)), (('y', 1, 2), ('y', 1, 2)), (('y', 1), ('y', 2)))
GATHER_ORDER = (8, 6, 7, 9, 0, 1, 2, 3, 4, 5)


def gather_plan(k, sub):
    rows, ways = CHUNKS[k][2] // 4, ROUTES[k][sub]
    n = len(ways)
    steps = [("y", rows >> (n - 1))]
    steps += [(way, rows >> (n - 1 - i)) for i, way in enumerate(ways[1:])]
    return steps + [(0, rows)]


SLACK, STEP, BACKLOG = 0.2, 0.05, 4.338
HOPS = {0: 0.9, "y": 2.2, 1: 2.2, 2: 2.2, "F": 2.2, "U": 2.2, "M": 2.2}
FAR_HOP = 2.7
LINK, CORES, SUMS, MESSAGE, LOADS, ENTRY = 46.0e3, 480e3, 2.4e6, 0.09, 3.0e6, 3.8
LINES = {
    0: (("c", 1),), "y": (("y", 1),), 1: (("x", 1),), 2: (("zi", 1), ("zo", 1)), "F": (("zi", 1),),
    "U": (("zo", 1),), "M": (("mid", 1),), "MM": (("mid", 1),)}
FAR_LINES = (("zi", 1), ("zo", 1), ("mid", 2))


def compute_pieces():
    out = [("start", 0.5, None)]
    out += [(("qa", t, s), (0.57, 0.8)[s], None) for t in range(3) for s in range(2)]
    out += [("spread", 0.9, None), ("clear", 0.4, None), ("turn1", 0.4, None)]
    out += [(("qa", t, s), (0.57, 0.8)[s], 3 + t if s == 0 else None)
            for t in range(3, 6) for s in range(2)]
    out += [("project", 1.2, 9), ("second_norm", 0.8, None), ("turn", 0.5, None)]
    out += [(("feed", u, 0), 1.88, u // 2 if u % 2 == 0 else None) for u in range(12)]
    out += [(("middle_back", i, 0), 1.33, None) for i in range(3)]
    out += [("proj_back", 1.0, None), ("proj_grad", 1.5, None)]
    out += [(("back", u, s), (0.9, 1.25)[s], None) for u in range(6) for s in range(2)]
    out += [(("first_back", i, 0), 0.8, None) for i in range(3)]
    out += [("sums", 0.6, None), ("output", 0.6, None), ("tokens", 0.6, None)]
    after = {("feed", 2 * j + 1, 0): j for j in range(6)}
    after["proj_grad"] = 9
    after.update({("back", 2 * j + 1, 1): 6 + j for j in range(3)})
    return out, after


class Timeline:
    def __init__(self, bits, log=None):
        self.log = log or (lambda *a: None)
        self.now, self.order, self.tasks = ENTRY, [], {}
        self.free = {line: 0.0 for line in ("c", "y", "x", "zi", "zo", "mid")}
        self.moves, self.adds = {}, {}
        for k in range(10):
            self.moves["l", k] = []
            for sub in range(2):
                self.moves["w", k, sub] = [(way, rows * 256) for way, rows in gather_plan(k, sub)]
        for p, part in enumerate(PARTS):
            there = steps_of(part, bits)
            self.adds["r", p] = [rows * 256 * (1 + both) for _, both, rows, *_ in there]
            self.moves["r", p] = [
                (way, n) for (way, *_), n in zip(there, self.adds["r", p])
            ] + [("U" if kind == "fold" else way, rows * 256)
                 for way, _, rows, kind, _ in there[::-1] if kind in ("half", "fold")]
        self.moves["v", 0] = [
            (way, NVEC * D * 4) for way in (0, "y") + tuple(range(1, bits))]
        self.left = {
            key: [sum(self.took(*m) + HOPS.get(m[0], FAR_HOP) for m in moves[i:])
                  for i in range(len(moves) + 1)]
            for key, moves in self.moves.items()}

    def took(self, way, nbytes):
        return nbytes / CORES if way == 0 else nbytes / LINK + MESSAGE

    def urgency(self, key):
        if key[0] == "l":
            return 2000
        if key[0] == "w":
            return 1000 - GATHER_ORDER.index(key[1]) * 10 + self.tasks[key][0]
        weight = PARTS[key[1]][4] if key[0] == "r" else 0
        return self.left[key][self.tasks[key][0]] + weight

    def opens(self, key):
        stage, ready = self.tasks[key]
        if stage < len(self.moves[key]):
            way = self.moves[key][stage][0]
            if way != 0:
                for line, _ in LINES.get(way, FAR_LINES):
                    ready = max(ready, self.free[line] - BACKLOG)
        return ready

    def step(self, key):
        stage, ready = self.tasks[key]
        self.order.append(key + (stage,))
        self.log("op", self.now, key, stage, ready)
        self.now = max(self.now, ready) + STEP
        if 0 < stage <= len(self.adds.get(key, ())):
            self.now += self.adds[key][stage - 1] / SUMS
        if stage == len(self.moves[key]):
            del self.tasks[key]
            if key[0] == "l":
                for sub in range(2):
                    self.tasks["w", key[1], sub] = (0, self.now - SLACK)
            return
        way, nbytes = self.moves[key][stage]
        lines = LINES.get(way, FAR_LINES)
        begin = max([self.now] + [self.free[line] for line, _ in lines])
        for line, load in lines:
            self.free[line] = begin + self.took(way, nbytes) * load
            self.log("x", line, begin, self.free[line])
        done = max(self.free[line] for line, _ in lines)
        self.tasks[key] = (stage + 1, done + HOPS.get(way, FAR_HOP))

    def poll(self, slack):
        while True:
            ready = [key for key in self.tasks if self.opens(key) + slack <= self.now]
            if not ready:
                return
            self.step(max(ready, key=self.urgency))

    def wait(self):
        self.now = max(self.now, min(self.opens(key) for key in self.tasks) + 1e-6)
        self.poll(0.0)

    def run(self):
        loaded = 0.0
        for k in GATHER_ORDER:
            loaded += CHUNKS[k][2] * 256 / LOADS
            self.tasks["l", k] = (0, max(ENTRY, 2.5 + loaded) - SLACK)
        pieces, after = compute_pieces()
        for piece, took, needs in pieces:
            self.poll(SLACK)
            if needs is not None:
                mine = (("l", needs), ("w", needs, 0), ("w", needs, 1))
                while any(key in self.tasks for key in mine):
                    self.wait()
                self.order += [("w", needs, 0, -1), ("w", needs, 1, -1)]
            self.order.append(("c", piece))
            self.log("c", self.now, piece)
            self.now += took
            if piece in after:
                for p, part in enumerate(PARTS):
                    if part[0] == after[piece]:
                        self.tasks["r", p] = (0, self.now)
            if piece == "sums":
                self.tasks["v", 0] = (0, self.now)
        while self.tasks:
            self.wait()
        return self.order, self.now


def timeline(bits, log=None):
    return Timeline(bits, log).run()


def layer_kernel(bits, rows, names, *refs):
    r = dict(zip(names, refs))
    y = Layer(r, rows)
    links = Links(r, bits)
    order, _ = timeline(bits)
    links.load(GATHER_ORDER[0])
    y.io_copy(0).start()
    for i in range(len(SMALL)):
        y.small_copy(i).start()
    for k in GATHER_ORDER[1:]:
        links.load(k)
    y.io_copy(1).start()
    links.greet()
    y.vectors()
    links.bias(0)

    def link_step(op):
        if op[0] == "l":
            links.loaded(op[1])
        elif op[0] == "w":
            links.gather(*op[1:])
        elif op[0] == "r":
            links.reduce(op[1], op[2])
        else:
            links.vec(op[2])

    def attend(t, s):
        if s == 0:
            y.qkv(lax.rem(t, 3), t // 3)
        else:
            y.attend(t)

    def feed(u, s):
        y.feed(u // 2, 1 - lax.rem(u, 2))

    def back(u, s):
        j, h = u // 2, 1 - lax.rem(u, 2)
        if s == 0:
            y.attend_back(h * 3 + j)
        else:
            y.qkv_back(j, h)

    loops = {
        "qa": (attend, 2),
        "feed": (feed, 1),
        "middle_back": (lambda i, s: y.middle_back(i), 1),
        "back": (back, 2),
        "first_back": (lambda i, s: y.first_back(i), 1),
    }

    def proj_grad():
        y.proj_grad(1)
        y.proj_grad(0)

    single = {
        "start": y.start,
        "spread": y.spread,
        "clear": y.clear,
        "turn1": y.turn1,
        "project": y.project,
        "second_norm": y.second_norm,
        "turn": y.turn,
        "proj_back": y.proj_back,
        "proj_grad": proj_grad,
        "sums": lambda: y.sums(links.vb.at[0]),
        "output": y.output,
        "tokens": y.tokens,
    }

    at = 0
    first_pass = True
    while at < len(order):
        op = order[at]
        if op[0] != "c":
            link_step(op)
            at += 1
            continue
        if isinstance(op[1], str):
            if op[1] == "start":
                single["start"]()
                links.bias(1)
            else:
                single[op[1]]()
            at += 1
            continue
        kind = op[1][0]
        body, slots = loops[kind]
        end, last = at, at
        while end < len(order):
            o = order[end]
            if o[0] == "c":
                if isinstance(o[1], str) or o[1][0] != kind:
                    break
                last = end
            end += 1
        before = {}
        pending = []
        for o in order[at : last + 1]:
            if o[0] == "c":
                before[o[1][1], o[1][2]] = pending
                pending = []
            else:
                pending.append(o)
        low = op[1][1]
        high = order[last][1][1] + 1

        @pl.loop(low, high)
        def _(t):
            for s in range(slots):
                for u in range(low, high):
                    if before[u, s]:
                        @pl.when(t == u)
                        def _(ops=before[u, s]):
                            for o in ops:
                                link_step(o)
                body(t, s)

        at = last + 1
    links.vec_end()
    for i in (2, 3):
        y.io_copy(i).wait()
    for p in range(len(PARTS)):
        links.finish(p)
    links.vec_out().wait()


INPUTS = ("h_tok", "h_mask", "h_mtok", "h_n1g", "h_n1s", "h_qvb", "h_pb", "h_ls", "h_n2g", "h_n2s",
          "h_upb", "h_db", "h_cot", "w_qkv", "w_pr", "w_up", "w_dn")
OUTPUTS = ("h_out", "h_gtok", "o_ff", "o_at", "o_vec")


FF_OUT, AT_OUT = 6, 4


def finish_kernel(ff, at, vec, o1, o2, p1, p2, wu, wd, wq, wp, mt, g1, s1, qv, pb, ls, g2, s2, ub, db,
                  ff_in, at_in, vec_in, rows_in, up, down, three, proj, mt_v, g1_v, s1_v, qv_v, pb_v,
                  ls_v, g2_v, s2_v, ub_v, db_v, in_sem, out_sem):
    order = [("at", j) for j in range(AT_OUT)] + [("ff", j) for j in range(FF_OUT)]
    loads = [
        pltpu.make_async_copy(*((ff.at[j], ff_in.at[j]) if kind == "ff" else (at.at[j], at_in.at[j])),
                              in_sem.at[i])
        for i, (kind, j) in enumerate(order)]
    loads += [pltpu.make_async_copy(o, rows_in.at[i], in_sem.at[10 + i])
              for i, o in enumerate((o1, o2))]
    sums = pltpu.make_async_copy(vec, vec_in, in_sem.at[12])
    stores = []
    for load in loads[:4] + [sums] + loads[4:]:
        load.start()

    def send(src, dst):
        copy = pltpu.make_async_copy(src, dst, out_sem.at[len(stores)])
        copy.start()
        stores.append(copy)

    for i, ((kind, j), load) in enumerate(zip(order, loads)):
        load.wait()
        if kind == "ff":
            for b in range(6):
                down[j, :, b * 128 : b * 128 + 128] = ff_in[j, pl.ds(b * 256, 256), :].astype(F32)
            send(down.at[j], wd.at[pl.ds(j * 256, 256), :])
            for b in range(2):
                up[j, :, b * 128 : b * 128 + 128] = ff_in[j, pl.ds(1536 + b * D, D), :].astype(F32)
            send(up.at[j], wu.at[:, pl.ds(j * 256, 256)])
        elif j < 3:
            for p in range(3):
                three[j, p] = at_in[j, pl.ds(p * D, D), :].astype(F32)
            send(three.at[j], wq.at[:, :, pl.ds(j * 128, 128)])
        else:
            for b in range(6):
                proj[:, b * 128 : b * 128 + 128] = at_in[j, pl.ds(b * 384, 384), :].astype(F32)
            send(proj, wp)
        if i == 4:
            sums.wait()
            for ref, row in ((mt_v, MTOK), (g1_v, N1G), (s1_v, N1S), (pb_v, PB), (g2_v, N2G),
                             (s2_v, N2S), (db_v, DB)):
                ref[...] = vec_in[row, :]
            ls_v[...] = vec_in[LS0 : LS1 + 1, :]
            for w in range(2):
                qv_v[w : w + 1, :] = vec_in[QVO : QVO + 1, w * 384 : w * 384 + 384]
                ub_v[pl.ds(w * D, D)] = vec_in[UPO + w, :]
            for pair in ((mt_v, mt), (g1_v, g1), (s1_v, s1), (qv_v, qv), (pb_v, pb), (ls_v, ls),
                         (g2_v, g2), (s2_v, s2), (ub_v, ub), (db_v, db)):
                send(*pair)
    for i, p in enumerate((p1, p2)):
        loads[10 + i].wait()
        send(rows_in.at[i], p)
    for store in stores:
        store.wait()


def local(dp, tokens, patch_mask, mask_token, norm1_gain, norm1_shift, w_qkv, qv_bias, w_proj,
          proj_bias, layer_scales, norm2_gain, norm2_shift, w_up, up_bias, w_down, down_bias,
          cotangent):
    bits = dp.bit_length() - 1
    rows = tokens.shape[0]
    scratch = {**layer_scratch(rows), **link_scratch(bits)}
    hbm = pl.BlockSpec(memory_space=pl.ANY)
    shape = jax.ShapeDtypeStruct
    out, gtok, ff, at, vec = pl.pallas_call(
        functools.partial(layer_kernel, bits, rows, INPUTS + OUTPUTS + tuple(scratch)),
        name="layer",
        in_specs=[hbm] * 17,
        out_specs=[hbm] * 5,
        out_shape=[
            shape((rows, D), BF16),
            shape((rows, D), BF16),
            shape((6, FF_ROWS, 128), BF16),
            shape((4, AT_ROWS, 128), BF16),
            shape((NVEC, D), F32),
        ],
        scratch_shapes=list(scratch.values()),
        compiler_params=pltpu.CompilerParams(
            collective_id=0, has_side_effects=True, vmem_limit_bytes=63 * 2**20),
        cost_estimate=pl.CostEstimate(
            flops=27 * 10**9, bytes_accessed=20 * 10**6, transcendentals=10**7),
    )(
        tokens, patch_mask, mask_token, norm1_gain, norm1_shift, qv_bias, proj_bias,
        layer_scales, norm2_gain, norm2_shift, up_bias, down_bias, cotangent, w_qkv, w_proj,
        w_up, w_down,
    )
    one, flat = shape((D,), F32), pltpu.VMEM((D,), F32)
    out, gtok, wu, wd, wq, wp, mt, g1, s1, qv, pb, ls, g2, s2, ub, db = pl.pallas_call(
        finish_kernel,
        name="finish",
        in_specs=[hbm] * 5,
        out_specs=[hbm] * 16,
        out_shape=[
            shape((rows, D), BF16), shape((rows, D), BF16),
            shape((D, 1536), F32), shape((1536, D), F32), shape((3, D, 384), F32),
            shape((384, D), F32), one, one, one, shape((2, 384), F32), one, shape((2, D), F32),
            one, one, shape((2 * D,), F32), one,
        ],
        scratch_shapes=[
            pltpu.VMEM((6, FF_ROWS, 128), BF16), pltpu.VMEM((4, AT_ROWS, 128), BF16),
            pltpu.VMEM((NVEC, D), F32), pltpu.VMEM((2, rows, D), BF16),
            pltpu.VMEM((6, D, 256), F32), pltpu.VMEM((6, 256, D), F32),
            pltpu.VMEM((3, 3, D, 128), F32), pltpu.VMEM((384, D), F32),
            flat, flat, flat, pltpu.VMEM((2, 384), F32), flat, pltpu.VMEM((2, D), F32), flat, flat,
            pltpu.VMEM((2 * D,), F32), flat,
            pltpu.SemaphoreType.DMA((13,)), pltpu.SemaphoreType.DMA((28,)),
        ],
        compiler_params=pltpu.CompilerParams(vmem_limit_bytes=62 * 2**20),
    )(ff, at, vec, out, gtok)
    return out, gtok, mt, g1, s1, wq, qv, wp, pb, ls, g2, s2, wu, ub, wd, db


def solution(mesh):
    rows2, both = P(("dp", "tensor"), None), P(("dp", "tensor"))
    return jax.shard_map(
        functools.partial(local, mesh.shape["dp"]),
        mesh=mesh,
        in_specs=(
            rows2, both, P(), P(), P(), P(None, None, "tensor"), P(None, "tensor"),
            P("tensor", None), P(), P(), P(), P(), P(None, "tensor"), P("tensor"),
            P("tensor", None), P(), rows2,
        ),
        out_specs=(
            rows2, rows2, P(), P(), P(), P(None, None, "tensor"), P(None, "tensor"),
            P("tensor", None), P(), P(), P(), P(), P(None, "tensor"), P("tensor"),
            P("tensor", None), P(),
        ),
        check_vma=False,
    )
```

```python
import functools

import jax
import jax.numpy as jnp
from jax import lax
from jax.experimental import pallas as pl
from jax.experimental.pallas import tpu as pltpu
from jax.sharding import PartitionSpec as P

MESH = pl.DeviceIdType.MESH
F32 = jnp.float32
BF16 = jnp.bfloat16
L = 197
LP = 208
D = 768
EPS = 1e-06
INV_ROOT2 = 0.7071067811865476
INV_ROOT2PI = 0.3989422804014327

MTOK, N1G, N1S, PB, LS0, LS1, N2G, N2S, DB, QVO, UPO, QVX, UPX = (
    0, 1, 2, 3, 4, 5, 6, 7, 8, 9, 10, 12, 13)
NSUM = 9
NVEC = 16


def dot(a, b):
    return lax.dot_general(a, b, (((1,), (0,)), ((), ())), preferred_element_type=F32)


def dot_nt(a, b):
    return lax.dot_general(a, b, (((1,), (1,)), ((), ())), preferred_element_type=F32)


def fold(x):
    return jnp.sum(x.reshape(x.shape[0] // 8, 8, x.shape[1]), axis=0)


def normed(rows):
    centred = rows - jnp.mean(rows, axis=-1, keepdims=True)
    inverse = lax.rsqrt(jnp.mean(centred * centred, axis=-1, keepdims=True) + EPS)
    return centred * inverse, inverse


def norm_back(grad, gain, scaled, inverse):
    weighted = grad * gain
    inner = (
        weighted
        - jnp.mean(weighted, axis=-1, keepdims=True)
        - scaled * jnp.mean(weighted * scaled, axis=-1, keepdims=True)
    )
    return inverse * inner


def wide(column):
    return jnp.concatenate([column] * (D // 128), axis=1)


BLOCKS = ((0, 48), (48, 48), (96, 48), (144, 48), (192, 16))


VECTORS = ("mtok", "n1g", "n1s", "pb", "n2g", "n2s", "db")
SMALL = VECTORS + ("mask", "qvb", "ls", "upb")


class Layer:
    def __init__(self, r, rows):
        self.__dict__.update(r)
        self.rows = rows
        self.images = rows // L
        self.padded = self.images * LP

    def widen(self, src):
        n = self.rows // 16

        @pl.loop(0, n)
        def _(b):
            at = pl.ds(pl.multiple_of(b * 16, 16), 16)
            self.t32[at, :] = src[at, :].astype(F32)

        left = self.rows - n * 16
        if left:
            self.t32[n * 16 : self.rows, :] = src[n * 16 : self.rows, :].astype(F32)

    def narrow(self, src, dst):
        for i in range(self.images):
            for r, n in BLOCKS:
                n = min(n, L - r)
                self.t32[pl.ds(L * i + r, n), :] = src[pl.ds(LP * i + r, n), :].astype(F32)
        n = self.rows // 16

        @pl.loop(0, n)
        def _(b):
            at = pl.ds(pl.multiple_of(b * 16, 16), 16)
            dst[at, :] = self.t32[at, :].astype(BF16)

        left = self.rows - n * 16
        if left:
            dst[n * 16 : self.rows, :] = self.t32[n * 16 : self.rows, :].astype(BF16)

    def bands(self, i):
        for r, n in BLOCKS:
            yield pl.ds(pl.multiple_of(i * LP + r, 16), n), n

    def acc(self, at, x):
        self.vacc[pl.ds(at * 8, 8), :] += fold(x)

    def small_copy(self, i):
        name = SMALL[i]
        return pltpu.make_async_copy(
            getattr(self, "h_" + name), getattr(self, "in_" + name), self.small_sem.at[i])

    def vectors(self):
        for i in range(len(SMALL)):
            self.small_copy(i).wait()
        for name in VECTORS:
            self.__dict__[name] = self.rows8.at[pl.ds(VECTORS.index(name), 1), :]
            self.rows8[VECTORS.index(name), :] = self.__dict__["in_" + name][...]

    def start(self):
        self.vacc[...] = jnp.zeros_like(self.vacc)
        rows = self.rows
        self.mrow[...] = jnp.zeros_like(self.mrow)
        flags = jnp.where(self.in_mask[...] == 1, 1.0, 0.0).astype(F32)[None, :]
        self.mrow[:, pl.ds(0, rows)] = jnp.broadcast_to(flags, (128, rows))
        self.mcol[...] = jnp.transpose(self.mrow[...])
        self.t32[pl.ds(rows, self.t32.shape[0] - rows), :] = jnp.zeros(
            (self.t32.shape[0] - rows, D), F32)
        self.io_copy(0).wait()
        self.widen(self.tok)
        for i in range(self.images):
            for r, n in BLOCKS:
                at = pl.ds(L * i + r, n)
                to = pl.ds(LP * i + r, n)
                x = self.t32[at, :]
                mk = self.mcol[at, :]
                mx = jnp.where(wide(mk) > 0.5, self.mtok[...], x)
                if r + n > L:
                    keep = lax.broadcasted_iota(jnp.int32, (n, 128), 0) < L - r
                    mk = jnp.where(keep, mk, 0.0)
                    mx = jnp.where(wide(keep), mx, 0.0)
                self.maskp[to, :] = mk
                self.mixed[to, :] = mx
                sc, _ = normed(mx)
                self.n1[to, :] = (sc * self.n1g[...] + self.n1s[...]).astype(BF16)

    def turn1(self):
        self.n1t[...] = jnp.transpose(self.n1[...])

    def spread(self):
        self.io_copy(1).wait()
        self.widen(self.cot)
        for i in range(self.images):
            for r, n in BLOCKS:
                at = pl.ds(L * i + r, n)
                to = pl.ds(LP * i + r, n)
                go = self.t32[at, :] * wide(self.maskp[to, :])
                self.gout[to, :] = go.astype(BF16)
                self.gb[to, :] = (self.in_ls[1:2, :] * go).astype(BF16)

    def w_pair(self, j, h):
        return jnp.concatenate(
            [self.g_at[j, h, pl.ds(p * D, D), :] for p in range(3)], axis=1)

    def qkv(self, j, h):
        t = h * 3 + j
        proj = dot(self.n1[...], self.w_pair(j, h))
        qb = self.qb[pl.ds(t, 1), :]
        vb = self.qb[pl.ds(8 + t, 1), :]
        self.q[t] = ((proj[:, 0:128] + qb) * 0.125).astype(BF16)
        self.k[t] = proj[:, 128:256].astype(BF16)
        self.v[t] = (proj[:, 256:384] + vb).astype(BF16)

    def two(self, x):
        low = lax.broadcasted_iota(jnp.int32, x.shape, 1) < 64
        zero = jnp.zeros_like(x)
        return jnp.where(low, x, zero), jnp.where(low, zero, x)

    def softmax(self, s):
        tail = s[LP - 16 :]
        keep = lax.broadcasted_iota(jnp.int32, tail.shape, 0) < L - (LP - 16)
        s = jnp.concatenate([s[: LP - 16], jnp.where(keep, tail, -1e30)], axis=0)
        x = jnp.exp(s - jnp.max(s, axis=0, keepdims=True))
        return (x * (1.0 / jnp.sum(x, axis=0, keepdims=True))).astype(BF16)

    def attend(self, t):
        n = self.images
        rows = [pl.ds(i * LP, LP) for i in range(n)]
        scores = []
        for at in rows:
            k = self.k[t, at, :]
            scores.append([dot_nt(k, q) for q in self.two(self.q[t, at, :])])
        probs = [[self.softmax(s) for s in pair] for pair in scores]
        for i, at in enumerate(rows):
            vt = jnp.transpose(self.v[t, at, :])
            outs = []
            for e in range(2):
                self.pt[(t * n + i) * 2 + e] = probs[i][e]
                outs.append(dot(vt[e * 64 : e * 64 + 64, :], probs[i][e]))
            ot = jnp.concatenate(outs, axis=0).astype(BF16)
            self.hot[i, pl.ds(pl.multiple_of(t * 128, 128), 128), :] = ot
            self.ho[t, at, :] = jnp.transpose(ot)

    def w_proj(self):
        return jnp.concatenate(
            [
                jnp.concatenate(
                    [self.g_at[3, h, pl.ds(b * 384, 384), :] for b in range(6)], axis=1)
                for h in range(2)
            ],
            axis=0,
        )

    def project(self):
        o = jnp.concatenate([self.ho[t] for t in range(6)], axis=1)
        self.br1[...] = dot(o, self.w_proj()) + self.pb[...]

    def second_norm(self):
        for i in range(self.images):
            for at, rows in self.bands(i):
                middle = self.mixed[at, :] + self.in_ls[0:1, :] * self.br1[at, :]
                sc, _ = normed(middle)
                self.n2[at, :] = (sc * self.n2g[...] + self.n2s[...]).astype(BF16)

    def clear(self):
        self.br2[...] = jnp.zeros_like(self.br2)
        self.gn2[...] = jnp.zeros_like(self.gn2)

    def turn(self):
        self.n2t[...] = jnp.transpose(self.n2[...])

    def feed(self, j, h):
        wd = jnp.concatenate(
            [self.g_ff[j, h, pl.ds(b * 256, 256), :] for b in range(6)], axis=1)
        wu = jnp.concatenate(
            [self.g_ff[j, h, pl.ds(1536 + b * D, D), :] for b in range(2)], axis=1)
        row = h * 6 + j
        pre = dot(self.n2[...], wu) + self.ub[pl.ds(row, 1), :]
        ga = dot_nt(self.gb[...], wd)
        cdf = 0.5 * (1.0 + lax.erf(pre * INV_ROOT2))
        act = (pre * cdf).astype(BF16)
        gp = (ga * (cdf + pre * jnp.exp(-0.5 * pre * pre) * INV_ROOT2PI)).astype(BF16)
        self.br2[...] += dot(act, wd)
        gwd = dot(jnp.transpose(act), self.gb[...]).astype(BF16)
        self.gn2[...] += dot_nt(gp, wu)
        gwu = dot(self.n2t[...], gp).astype(BF16)
        self.uba[row] = fold(gp.astype(F32))
        for b in range(6):
            self.g_ff[j, h, pl.ds(b * 256, 256), :] = gwd[:, b * 128 : b * 128 + 128]
        for b in range(2):
            self.g_ff[j, h, pl.ds(1536 + b * D, D), :] = gwu[:, b * 128 : b * 128 + 128]

    def middle_back(self, i):
        ls0, ls1 = self.in_ls[0:1, :], self.in_ls[1:2, :]
        for at, rows in self.bands(i):
            b1 = self.br1[at, :]
            middle = self.mixed[at, :] + ls0 * b1
            sc, inv = normed(middle)
            b2 = self.br2[at, :] + self.db[...]
            self.n2[at, :] = (middle + ls1 * b2).astype(BF16)
            self.br2[at, :] = jnp.zeros((rows, D), F32)
            go = self.gout[at, :].astype(F32)
            self.acc(LS1, go * b2)
            self.acc(DB, self.gb[at, :].astype(F32))
            g = self.gn2[at, :]
            self.acc(N2G, g * sc)
            self.acc(N2S, g)
            gm = go + norm_back(g, self.n2g[...], sc, inv)
            self.acc(LS0, gm * b1)
            gb1 = (ls0 * gm).astype(BF16)
            self.gb[at, :] = gb1
            self.acc(PB, gb1.astype(F32))
            self.gn2[at, :] = gm

    def io_copy(self, i):
        src, dst = ((self.h_tok, self.tok), (self.h_cot, self.cot), (self.tok, self.h_out),
                    (self.cot, self.h_gtok))[i]
        return pltpu.make_async_copy(src, dst, self.io_sem.at[i])

    def output(self):
        self.narrow(self.n2, self.tok)
        self.io_copy(2).start()

    def tokens(self):
        self.narrow(self.br2, self.cot)
        self.io_copy(3).start()

    def proj_back(self):
        gh = dot_nt(self.gb[...], self.w_proj()).astype(BF16)
        for t in range(6):
            self.ho[t] = gh[:, t * 128 : t * 128 + 128]

    def proj_grad(self, h):
        total = sum(
            dot(self.hot[i, pl.ds(h * 384, 384), :], self.gb[pl.ds(i * LP, LP), :])
            for i in range(self.images))
        for b in range(6):
            self.g_at[3, h, pl.ds(b * 384, 384), :] = total[
                :, b * 128 : b * 128 + 128].astype(BF16)

    def attend_back(self, t):
        n = self.images
        rows = [pl.ds(i * LP, LP) for i in range(n)]
        grads = []
        for at in rows:
            v = self.v[t, at, :]
            grads.append([dot_nt(v, d) for d in self.two(self.ho[t, at, :])])
        scores = []
        for i in range(n):
            pair = []
            for e in range(2):
                p, gp = self.pt[(t * n + i) * 2 + e].astype(F32), grads[i][e]
                pair.append((p * (gp - jnp.sum(gp * p, axis=0, keepdims=True))).astype(BF16))
            scores.append(pair)
        for i, at in enumerate(rows):
            q, d = self.two(self.q[t, at, :]), self.two(self.ho[t, at, :])
            kt = jnp.transpose(self.k[t, at, :])
            gs = scores[i]
            dv = dot(self.pt[(t * n + i) * 2], d[0]) + dot(self.pt[(t * n + i) * 2 + 1], d[1])
            dk = dot(gs[0], q[0]) + dot(gs[1], q[1])
            dq = [dot(kt[e * 64 : e * 64 + 64, :], gs[e]) for e in range(2)]
            dq = jnp.transpose(jnp.concatenate(dq, axis=0)) * 0.125
            self.dqkv[at, 0:128] = dq.astype(BF16)
            self.dqkv[at, 128:256] = dk.astype(BF16)
            self.dqkv[at, 256:384] = dv.astype(BF16)
        self.qa[t] = fold(self.dqkv[:, 0:128].astype(F32))
        self.qa[8 + t] = fold(self.dqkv[:, 256:384].astype(F32))

    def qkv_back(self, j, h):
        self.br2[...] += dot_nt(self.dqkv[...], self.w_pair(j, h))
        grad = dot(self.n1t[...], self.dqkv[...])
        for p in range(3):
            self.g_at[j, h, pl.ds(p * D, D), :] = grad[
                :, p * 128 : p * 128 + 128].astype(BF16)

    def first_back(self, i):
        for at, _ in self.bands(i):
            sc, inv = normed(self.mixed[at, :])
            g = self.br2[at, :]
            self.acc(N1G, g * sc)
            self.acc(N1S, g)
            gx = self.gn2[at, :] + norm_back(g, self.n1g[...], sc, inv)
            mk = wide(self.maskp[at, :]) > 0.5
            self.acc(MTOK, jnp.where(mk, gx, 0.0))
            self.br2[at, :] = jnp.where(mk, 0.0, gx)

    def sums(self, vec):
        vec[...] = jnp.zeros_like(vec)
        for s in range(NSUM):
            vec[s : s + 1, :] = jnp.sum(
                self.vacc[pl.ds(s * 8, 8), :], axis=0, keepdims=True)
        for h, (qv, up) in enumerate(((QVO, UPO), (QVX, UPX))):
            for w in range(2):
                for j in range(3):
                    c = w * 384 + j * 128
                    vec[qv : qv + 1, c : c + 128] = jnp.sum(
                        self.qa[8 * w + h * 3 + j], axis=0, keepdims=True)
            for j in range(6):
                c = j % 3 * 256
                vec[up + j // 3 : up + j // 3 + 1, c : c + 256] = jnp.sum(
                    self.uba[h * 6 + j], axis=0, keepdims=True)


def layer_scratch(rows):
    n = rows // L
    padded = n * LP
    v = pltpu.VMEM
    return dict(
        tok=v((rows, D), BF16),
        cot=v((rows, D), BF16),
        io_sem=pltpu.SemaphoreType.DMA((4,)),
        small_sem=pltpu.SemaphoreType.DMA((len(SMALL),)),
        **{"in_" + name: v((D,), F32) for name in VECTORS},
        in_mask=v((rows,), jnp.int32),
        in_qvb=v((2, 384), F32),
        in_ls=v((2, D), F32),
        in_upb=v((1536,), F32),
        t32=v(((rows + 11 + 15) // 16 * 16 + 0, D), F32),
        mrow=v((128, (rows + 127) // 128 * 128), F32),
        mcol=v(((rows + 127) // 128 * 128, 128), F32),
        maskp=v((padded, 128), F32),
        mixed=v((padded, D), F32),
        gout=v((padded, D), BF16),
        n1=v((padded, D), BF16),
        n1t=v((D, padded), BF16),
        q=v((6, padded, 128), BF16),
        k=v((6, padded, 128), BF16),
        v=v((6, padded, 128), BF16),
        pt=v((6 * n * 2, LP, LP), BF16),
        ho=v((6, padded, 128), BF16),
        hot=v((n, D, LP), BF16),
        br1=v((padded, D), F32),
        n2=v((padded, D), BF16),
        n2t=v((D, padded), BF16),
        gb=v((padded, D), BF16),
        br2=v((padded, D), F32),
        gn2=v((padded, D), F32),
        dqkv=v((padded, 384), BF16),
        rows8=v((8, D), F32),
        vacc=v((NSUM * 8, D), F32),
        qb=v((16, 128), F32),
        ub=v((12, 256), F32),
        qa=v((16, 8, 128), F32),
        uba=v((12, 8, 256), F32),
    )


FF_ROWS, AT_ROWS = 3072, 2304
CHUNKS = tuple([("g_ff", j, FF_ROWS) for j in range(6)] + [("g_at", j, AT_ROWS) for j in range(4)])


Y_FIRST, Z_FIRST = (0, "y", 1, 2, 3), (0, 2, "y", 1, 3)
CUTS = {
    0: ((5, (0, 'y', 'F', 'M', 11), 49), (7, (0, 1, 'y', 'F', 'MM'), 2),),
    1: ((3, (0, 'y', 11, 'F', 'MM'), -58), (5, (0, 'y', 2, 1, 13), 58), (4, (0, 1, 'y', 'F', 'MM'), -28),),
    2: ((4, (0, 'y', 1, 'F', 'MM'), -60), (8, (0, 1, 'y', 'F', 'MM'), -33),),
    3: ((8, (0, 2, 'y', 1, 13), 40), (4, (0, 'y', 'F', 'M', 11), -60),),
    4: ((3, (0, 1, 'F', 'MM', 'y'), -7), (9, (0, 'y', 1, 'F', 'MM'), -13),),
    5: ((3, (0, 1, 'y', 'F', 'MM'), 26), (7, (0, 1, 'y', 'F', 'MM'), -37), (2, (0, 'y', 2, 11, 13), -46),),
    9: ((9, (0, 'y', 1, 'F', 'MM'), -5),),
    6: ((3, (0, 1, 'F', 'M', 'y'), -25), (6, (0, 'y', 1, 'F', 'MM'), 37),),
    7: ((1, (0, 'F', 'M', 'y', 1), -40), (1, (0, 'y', 'F', 'M', 11), 21), (4, (0, 'y', 'F', 'M', 11), -2), (3, (0, 'y', 1, 'F', 'MM'), 17),),
    8: ((1, (0, 'y', 1, 'F', 'M'), -29), (3, (0, 'y', 1, 'F', 'MM'), -60), (2, (0, 'y', 1, 'F', 'MM'), 38), (1, (0, 'y', 1, 'F', 'MM'), 3), (2, (0, 'y', 1, 'F', 'MM'), 1),),
}


def parts_of():
    out = []
    for k, cuts in CUTS.items():
        at = 0
        for units, order, weight in cuts:
            out.append((k, at, units * 256, order, weight))
            at += units * 256
    return tuple(out)


PARTS = parts_of()


def steps_of(part, bits):
    _, _, rows, order, _ = part
    order = list(order) + list(range(4, bits))
    both, role, out = True, "all", []
    for way in order:
        if way == "y":
            both = False
            out.append((way, False, rows, "all", role))
        elif way == "F":
            out.append((way, both, rows, "fold", "fold"))
            role = "inner"
        elif way == "MM" or (way != "M" and way >= 10):
            out.append(("M" if way == "MM" else way - 10, both, rows, "all", role))
        elif rows // 2 % 16 == 0:
            rows //= 2
            out.append((way, both, rows, "half", role))
        else:
            out.append((way, both, rows, "all", role))
    return out


def land_offsets(bits):
    sizes, table = [0, 0], {}
    for p, part in enumerate(PARTS):
        for i, (_, both, rows, *_) in enumerate(steps_of(part, bits)):
            table[p, i] = sizes[both]
            sizes[both] += rows
    return table, sizes


class Links:
    def __init__(self, r, bits):
        self.__dict__.update(r)
        self.bits = bits
        self.dp = lax.axis_index("dp")
        self.half = lax.axis_index("tensor")
        self.bit = [(self.dp // (1 << b)) % 2 for b in range(bits)]
        self.inner = self.bit[2] != self.bit[3]
        self.outer = self.bit[2] == self.bit[3]
        self.offsets, _ = land_offsets(bits)

    def peer(self, way):
        if way == "y":
            return (self.dp, 1 - self.half)
        if way in ("M", "MM"):
            return (self.dp + 4 * (1 - 2 * self.bit[2]) + 8 * (1 - 2 * self.bit[3]), self.half)
        if way in ("F", "U"):
            way = 2
        return (self.dp + (1 << way) * (1 - 2 * self.bit[way]), self.half)

    def greet(self):
        barrier = pltpu.get_barrier_semaphore()
        ways = ["y", "M"] + list(range(self.bits))
        for way in ways:
            pl.semaphore_signal(barrier, inc=1, device_id=self.peer(way), device_id_type=MESH)
        pl.semaphore_wait(barrier, len(ways))

    def copy(self, src, dst, send, recv, way):
        return pltpu.make_async_remote_copy(
            src_ref=src, dst_ref=dst, send_sem=send, recv_sem=recv,
            device_id=self.peer(way), device_id_type=MESH)

    def load(self, k):
        name, j, n = CHUNKS[k]
        sem = self.load_sem.at[k]
        if name == "g_ff":
            for b in range(6):
                pltpu.make_async_copy(
                    self.w_dn.at[pl.ds(j * 256, 256), pl.ds(b * 128, 128)],
                    self.g_ff.at[j, 0, pl.ds(b * 256, 256)], sem).start()
            for b in range(2):
                pltpu.make_async_copy(
                    self.w_up.at[:, pl.ds(j * 256 + b * 128, 128)],
                    self.g_ff.at[j, 0, pl.ds(1536 + b * D, D)], sem).start()
        elif j < 3:
            for p in range(3):
                pltpu.make_async_copy(
                    self.w_qkv.at[p, :, pl.ds(j * 128, 128)],
                    self.g_at.at[j, 0, pl.ds(p * D, D)], sem).start()
        else:
            for b in range(6):
                pltpu.make_async_copy(
                    self.w_pr.at[:, pl.ds(b * 128, 128)],
                    self.g_at.at[3, 0, pl.ds(b * 384, 384)], sem).start()

    def loaded(self, k):
        name, j, n = CHUNKS[k]
        ref = getattr(self, name).at[j, 0]
        pltpu.make_async_copy(ref, ref, self.load_sem.at[k]).wait()

    def bias(self, stage):
        a = self.copy(self.in_qvb, self.qvbx, self.b_send.at[0], self.b_recv.at[0], "y")
        b = self.copy(self.in_upb, self.upbx, self.b_send.at[1], self.b_recv.at[1], "y")
        if stage == 0:
            a.start()
            b.start()
            return
        a.wait()
        b.wait()
        for h, (qv, up) in enumerate(((self.in_qvb, self.in_upb), (self.qvbx, self.upbx))):
            for j in range(3):
                for w in range(2):
                    row = 8 * w + h * 3 + j
                    self.qb[row : row + 1, :] = qv[w : w + 1, j * 128 : j * 128 + 128]
            for j in range(6):
                row = h * 6 + j
                self.ub[row : row + 1, :] = up[pl.ds(j * 256, 256)][None, :]

    def gather_copy(self, k, sub, i):
        name, j, n = CHUNKS[k]
        ref = getattr(self, name)
        ways = ROUTES[k][sub]
        way, rows = gather_plan(k, sub)[i]
        size = n // 4
        off = self.bit[0] * (n // 2) + sub * size
        for further in ways[:0:-1][: len(ways) - max(i, 1)]:
            size //= 2
            off = off + self.bit[further] * size
        at = pl.ds(pl.multiple_of(off, 16), rows)
        return self.copy(
            ref.at[j, int(i > 0), at], ref.at[j, 1, at],
            self.w_send.at[k * 2 + sub, i], self.w_recv.at[k * 2 + sub, i], way)

    def gather(self, k, sub, stage):
        copies = len(gather_plan(k, sub))
        if stage < 0:
            for i in range(copies):
                self.gather_copy(k, sub, i).wait_send()
            return
        if stage > 0:
            self.gather_copy(k, sub, stage - 1).wait_recv()
        if stage < copies:
            self.gather_copy(k, sub, stage).start()

    def add(self, dst, dst_at, src, src_at, rows):
        size = next(s for s in (256, 192, 144, 128, 112, 96, 80, 64, 48, 32, 16) if rows % s == 0)

        @pl.loop(0, rows // size)
        def _(b):
            to = pl.ds(pl.multiple_of(dst_at + b * size, 16), size)
            of = pl.ds(pl.multiple_of(src_at + b * size, 16), size)
            dst[to, :] = dst[to, :] + src[of, :]

    def when(self, role):
        if role == "all":
            return lambda body: body()
        return pl.when(self.outer if role == "fold" else self.inner)

    def reduce_steps(self, p):
        part = PARTS[p]
        k, first, rows = part[:3]
        name, j, _ = CHUNKS[k]
        ref = getattr(self, name)
        own = ref.at[j, 0]
        at, out, back = first, [], []
        other = {"all": "all", "inner": "inner", "fold": "unfold", "unfold": "fold"}

        def add(way, src, dst, adds, kind, role):
            i = len(out)

            def build():
                return self.copy(src(), dst(), self.r_send.at[p], self.r_recv.at[p, i], way)

            out.append((way, build, adds, kind, role, other[role]))

        def rows_of(r, at, rows):
            return lambda: r.at[pl.ds(pl.multiple_of(at, 16), rows)]

        def both_of(r, at, rows):
            return lambda: r.at[:, pl.ds(pl.multiple_of(at, 16), rows)]

        for way, both, rows, kind, role in steps_of(part, self.bits):
            o = self.offsets[p, len(out)]
            away = at
            if kind == "half":
                b = self.bit[3 if way == "M" else way]
                away = at + (1 - b) * rows
                at = at + b * rows
                back.append((way, at, rows, role))
            elif kind == "fold":
                back.append(("U", at, rows, "unfold"))
            if both:
                add(way, both_of(ref.at[j], away, rows), both_of(self.land2, o, rows),
                    [(ref.at[j, h], at, self.land2.at[h], o, rows) for h in range(2)], kind, role)
            else:
                src = ref.at[j, 1] if way == "y" else own
                add(way, rows_of(src, away, rows), rows_of(self.land, o, rows),
                    [(own, at, self.land, o, rows)], kind, role)
        for way, at, rows, role in back[::-1]:
            add(way, rows_of(own, at, rows), rows_of(own, at, rows), [], "back", role)
        return out

    def credit_of(self, p, way):
        return self.credit.at[p, {"F": 2, "U": 2, "M": 3}.get(way, way)]

    def result_copy(self, p):
        k, first, rows = PARTS[p][:3]
        name, j, _ = CHUNKS[k]
        out = self.o_ff if name == "g_ff" else self.o_at
        at = pl.ds(first, rows)
        return pltpu.make_async_copy(
            getattr(self, name).at[j, 0, at], out.at[j, at], self.out_sem.at[p])

    def reduce(self, p, stage):
        steps = self.reduce_steps(p)
        if stage > 0:
            way, build, adds, kind, sender, receiver = steps[stage - 1]

            def taken():
                build().wait_recv()

            def sent():
                build().wait_send()
                if kind in ("half", "fold"):
                    pl.semaphore_signal(
                        self.credit_of(p, way), inc=1, device_id=self.peer(way),
                        device_id_type=MESH)

            def summed():
                for one in adds:
                    self.add(*one)

            self.when(receiver)(taken)
            self.when(sender)(sent)
            if adds:
                self.when(receiver)(summed)
        if stage < len(steps):
            way, build, adds, kind, sender, receiver = steps[stage]

            def go():
                if kind == "back":
                    pl.semaphore_wait(self.credit_of(p, way), 1)
                build().start()

            self.when(sender)(go)
        else:
            self.result_copy(p).start()

    def finish(self, p):
        self.result_copy(p).wait()

    def vec_copy(self, s):
        way = (0, "y")[s] if s < 2 else s - 1
        return self.copy(self.vb.at[s], self.vr.at[s], self.v_send.at[s], self.v_recv.at[s], way)

    def vec(self, stage):
        if stage > 0:
            s = stage - 1
            self.vec_copy(s).wait_recv()
            if s == 1:
                self.vb[2, 0:NSUM, :] = self.vb[1, 0:NSUM, :] + self.vr[1, 0:NSUM, :]
                self.vb[2, QVO:QVX, :] = self.vb[1, QVO:QVX, :] + self.vr[1, QVX : QVX + 3, :]
                self.vb[2, QVX:NVEC, :] = jnp.zeros((NVEC - QVX, D), F32)
            else:
                self.vb[stage] = self.vb[s] + self.vr[s]
        if stage < self.bits + 1:
            self.vec_copy(stage).start()

    def vec_end(self):
        for s in range(self.bits + 1):
            self.vec_copy(s).wait_send()
        self.vec_out().start()

    def vec_out(self):
        return pltpu.make_async_copy(self.vb.at[self.bits + 1], self.o_vec, self.vec_sem.at[0])


def link_scratch(bits):
    v, dma = pltpu.VMEM, pltpu.SemaphoreType.DMA
    steps = 2 * bits + 1
    parts = len(PARTS)
    land = land_offsets(bits)[1]
    return dict(
        g_ff=v((6, 2, FF_ROWS, 128), BF16),
        g_at=v((4, 2, AT_ROWS, 128), BF16),
        land2=v((2, land[1], 128), BF16),
        land=v((land[0], 128), BF16),
        qvbx=v((2, 384), F32),
        upbx=v((1536,), F32),
        vb=v((bits + 2, NVEC, D), F32),
        vr=v((bits + 1, NVEC, D), F32),
        load_sem=dma((10,)),
        out_sem=dma((parts,)),
        b_send=dma((2,)),
        b_recv=dma((2,)),
        w_send=dma((20, 4)),
        w_recv=dma((20, 4)),
        r_send=dma((parts,)),
        r_recv=dma((parts, steps)),
        credit=pltpu.SemaphoreType.REGULAR((parts, bits)),
        v_send=dma((bits + 1,)),
        vec_sem=dma((1,)),
        v_recv=dma((bits + 1,)),
    )


ROUTES = ((('y', 1, 2), ('y', 2, 1)), (('y', 2, 1), ('y', 1, 2)), (('y', 2), ('y', 2)), (('y', 1, 2), ('y', 2)), (('y', 2), ('y',)), (('y', 2), ('y', 2)), (('y', 2, 1), ('y', 1, 2)), (('y', 2, 1), ('y', 1, 2)), (('y', 1, 2), ('y', 1)), (('y', 1), ('y', 2)))
GATHER_ORDER = (6, 7, 8, 0, 9, 1, 2, 3, 4, 5)


def gather_plan(k, sub):
    rows, ways = CHUNKS[k][2] // 4, ROUTES[k][sub]
    n = len(ways)
    steps = [("y", rows >> (n - 1))]
    steps += [(way, rows >> (n - 1 - i)) for i, way in enumerate(ways[1:])]
    return steps + [(0, rows)]


SLACK, STEP, BACKLOG = 0.2, 0.08, 2.417
HOPS = {0: 0.9, "y": 2.2, 1: 2.2, 2: 2.2, "F": 2.2, "U": 2.2, "M": 2.2}
FAR_HOP = 2.7
LINK, CORES, SUMS, MESSAGE, LOADS, ENTRY = 47.0e3, 480e3, 2.4e6, 0.01, 3.0e6, 3.8
LINES = {
    0: (("c", 1),), "y": (("y", 1),), 1: (("x", 1),), 2: (("zi", 1), ("zo", 1)), "F": (("zi", 1),),
    "U": (("zo", 1),), "M": (("mid", 1),), "MM": (("mid", 1),)}
FAR_LINES = (("zi", 1), ("zo", 1), ("mid", 2))


def compute_pieces():
    out = [("start", 0.5, None)]
    out += [(("qa", t, s), (0.57, 0.8)[s], None) for t in range(3) for s in range(2)]
    out += [("spread", 0.9, None), ("clear", 0.4, None), ("turn1", 0.4, None)]
    out += [(("qa", t, s), (0.57, 0.8)[s], 3 + t if s == 0 else None)
            for t in range(3, 6) for s in range(2)]
    out += [("project", 1.2, 9), ("second_norm", 0.8, None), ("turn", 0.5, None)]
    out += [(("feed", u, 0), 1.88, u // 2 if u % 2 == 0 else None) for u in range(12)]
    out += [(("middle_back", i, 0), 1.33, None) for i in range(3)]
    out += [("proj_back", 1.0, None), ("proj_grad", 1.5, None)]
    out += [(("back", u, s), (0.9, 1.25)[s], None) for u in range(6) for s in range(2)]
    out += [(("first_back", i, 0), 0.8, None) for i in range(3)]
    out += [("sums", 0.6, None), ("output", 0.6, None), ("tokens", 0.6, None)]
    after = {("feed", 2 * j + 1, 0): j for j in range(6)}
    after["proj_grad"] = 9
    after.update({("back", 2 * j + 1, 1): 6 + j for j in range(3)})
    return out, after


class Timeline:
    def __init__(self, bits, log=None):
        self.log = log or (lambda *a: None)
        self.now, self.order, self.tasks = ENTRY, [], {}
        self.free = {line: 0.0 for line in ("c", "y", "x", "zi", "zo", "mid")}
        self.moves, self.adds = {}, {}
        for k in range(10):
            self.moves["l", k] = []
            for sub in range(2):
                self.moves["w", k, sub] = [(way, rows * 256) for way, rows in gather_plan(k, sub)]
        for p, part in enumerate(PARTS):
            there = steps_of(part, bits)
            self.adds["r", p] = [rows * 256 * (1 + both) for _, both, rows, *_ in there]
            self.moves["r", p] = [
                (way, n) for (way, *_), n in zip(there, self.adds["r", p])
            ] + [("U" if kind == "fold" else way, rows * 256)
                 for way, _, rows, kind, _ in there[::-1] if kind in ("half", "fold")]
        self.moves["v", 0] = [
            (way, NVEC * D * 4) for way in (0, "y") + tuple(range(1, bits))]
        self.left = {
            key: [sum(self.took(*m) + HOPS.get(m[0], FAR_HOP) for m in moves[i:])
                  for i in range(len(moves) + 1)]
            for key, moves in self.moves.items()}

    def took(self, way, nbytes):
        return nbytes / CORES if way == 0 else nbytes / LINK + MESSAGE

    def urgency(self, key):
        if key[0] == "l":
            return 2000
        if key[0] == "w":
            return 1000 - GATHER_ORDER.index(key[1]) * 10 + self.tasks[key][0]
        weight = PARTS[key[1]][4] if key[0] == "r" else 0
        return self.left[key][self.tasks[key][0]] + weight

    def opens(self, key):
        stage, ready = self.tasks[key]
        if stage < len(self.moves[key]):
            way = self.moves[key][stage][0]
            if way != 0:
                for line, _ in LINES.get(way, FAR_LINES):
                    ready = max(ready, self.free[line] - BACKLOG)
        return ready

    def step(self, key):
        stage, ready = self.tasks[key]
        self.order.append(key + (stage,))
        self.log("op", self.now, key, stage, ready)
        self.now = max(self.now, ready) + STEP
        if 0 < stage <= len(self.adds.get(key, ())):
            self.now += self.adds[key][stage - 1] / SUMS
        if stage == len(self.moves[key]):
            del self.tasks[key]
            if key[0] == "l":
                for sub in range(2):
                    self.tasks["w", key[1], sub] = (0, self.now - SLACK)
            return
        way, nbytes = self.moves[key][stage]
        lines = LINES.get(way, FAR_LINES)
        begin = max([self.now] + [self.free[line] for line, _ in lines])
        for line, load in lines:
            self.free[line] = begin + self.took(way, nbytes) * load
            self.log("x", line, begin, self.free[line])
        done = max(self.free[line] for line, _ in lines)
        self.tasks[key] = (stage + 1, done + HOPS.get(way, FAR_HOP))

    def poll(self, slack):
        while True:
            ready = [key for key in self.tasks if self.opens(key) + slack <= self.now]
            if not ready:
                return
            self.step(max(ready, key=self.urgency))

    def wait(self):
        self.now = max(self.now, min(self.opens(key) for key in self.tasks) + 1e-6)
        self.poll(0.0)

    def run(self):
        loaded = 0.0
        for k in GATHER_ORDER:
            loaded += CHUNKS[k][2] * 256 / LOADS
            self.tasks["l", k] = (0, max(ENTRY, 2.5 + loaded) - SLACK)
        pieces, after = compute_pieces()
        for piece, took, needs in pieces:
            self.poll(SLACK)
            if needs is not None:
                mine = (("l", needs), ("w", needs, 0), ("w", needs, 1))
                while any(key in self.tasks for key in mine):
                    self.wait()
                self.order += [("w", needs, 0, -1), ("w", needs, 1, -1)]
            self.order.append(("c", piece))
            self.log("c", self.now, piece)
            self.now += took
            if piece in after:
                for p, part in enumerate(PARTS):
                    if part[0] == after[piece]:
                        self.tasks["r", p] = (0, self.now)
            if piece == "sums":
                self.tasks["v", 0] = (0, self.now)
        while self.tasks:
            self.wait()
        return self.order, self.now


def timeline(bits, log=None):
    return Timeline(bits, log).run()


def layer_kernel(bits, rows, names, *refs):
    r = dict(zip(names, refs))
    y = Layer(r, rows)
    links = Links(r, bits)
    order, _ = timeline(bits)
    links.load(GATHER_ORDER[0])
    y.io_copy(0).start()
    for i in range(len(SMALL)):
        y.small_copy(i).start()
    for k in GATHER_ORDER[1:]:
        links.load(k)
    y.io_copy(1).start()
    links.greet()
    y.vectors()
    links.bias(0)

    def link_step(op):
        if op[0] == "l":
            links.loaded(op[1])
        elif op[0] == "w":
            links.gather(*op[1:])
        elif op[0] == "r":
            links.reduce(op[1], op[2])
        else:
            links.vec(op[2])

    def attend(t, s):
        if s == 0:
            y.qkv(lax.rem(t, 3), t // 3)
        else:
            y.attend(t)

    def feed(u, s):
        y.feed(u // 2, 1 - lax.rem(u, 2))

    def back(u, s):
        j, h = u // 2, 1 - lax.rem(u, 2)
        if s == 0:
            y.attend_back(h * 3 + j)
        else:
            y.qkv_back(j, h)

    loops = {
        "qa": (attend, 2),
        "feed": (feed, 1),
        "middle_back": (lambda i, s: y.middle_back(i), 1),
        "back": (back, 2),
        "first_back": (lambda i, s: y.first_back(i), 1),
    }

    def proj_grad():
        y.proj_grad(1)
        y.proj_grad(0)

    single = {
        "start": y.start,
        "spread": y.spread,
        "clear": y.clear,
        "turn1": y.turn1,
        "project": y.project,
        "second_norm": y.second_norm,
        "turn": y.turn,
        "proj_back": y.proj_back,
        "proj_grad": proj_grad,
        "sums": lambda: y.sums(links.vb.at[0]),
        "output": y.output,
        "tokens": y.tokens,
    }

    at = 0
    first_pass = True
    while at < len(order):
        op = order[at]
        if op[0] != "c":
            link_step(op)
            at += 1
            continue
        if isinstance(op[1], str):
            if op[1] == "start":
                single["start"]()
                links.bias(1)
            else:
                single[op[1]]()
            at += 1
            continue
        kind = op[1][0]
        body, slots = loops[kind]
        end, last = at, at
        while end < len(order):
            o = order[end]
            if o[0] == "c":
                if isinstance(o[1], str) or o[1][0] != kind:
                    break
                last = end
            end += 1
        before = {}
        pending = []
        for o in order[at : last + 1]:
            if o[0] == "c":
                before[o[1][1], o[1][2]] = pending
                pending = []
            else:
                pending.append(o)
        low = op[1][1]
        high = order[last][1][1] + 1

        @pl.loop(low, high)
        def _(t):
            for s in range(slots):
                for u in range(low, high):
                    if before[u, s]:
                        @pl.when(t == u)
                        def _(ops=before[u, s]):
                            for o in ops:
                                link_step(o)
                body(t, s)

        at = last + 1
    links.vec_end()
    for i in (2, 3):
        y.io_copy(i).wait()
    for p in range(len(PARTS)):
        links.finish(p)
    links.vec_out().wait()


INPUTS = ("h_tok", "h_mask", "h_mtok", "h_n1g", "h_n1s", "h_qvb", "h_pb", "h_ls", "h_n2g", "h_n2s",
          "h_upb", "h_db", "h_cot", "w_qkv", "w_pr", "w_up", "w_dn")
OUTPUTS = ("h_out", "h_gtok", "o_ff", "o_at", "o_vec")


FF_OUT, AT_OUT = 6, 4


def finish_kernel(ff, at, vec, o1, o2, p1, p2, wu, wd, wq, wp, mt, g1, s1, qv, pb, ls, g2, s2, ub, db,
                  ff_in, at_in, vec_in, rows_in, up, down, three, proj, mt_v, g1_v, s1_v, qv_v, pb_v,
                  ls_v, g2_v, s2_v, ub_v, db_v, in_sem, out_sem):
    order = [("at", j) for j in range(AT_OUT)] + [("ff", j) for j in range(FF_OUT)]
    loads = [
        pltpu.make_async_copy(*((ff.at[j], ff_in.at[j]) if kind == "ff" else (at.at[j], at_in.at[j])),
                              in_sem.at[i])
        for i, (kind, j) in enumerate(order)]
    loads += [pltpu.make_async_copy(o, rows_in.at[i], in_sem.at[10 + i])
              for i, o in enumerate((o1, o2))]
    sums = pltpu.make_async_copy(vec, vec_in, in_sem.at[12])
    stores = []
    for load in loads[:4] + [sums] + loads[4:]:
        load.start()

    def send(src, dst):
        copy = pltpu.make_async_copy(src, dst, out_sem.at[len(stores)])
        copy.start()
        stores.append(copy)

    for i, ((kind, j), load) in enumerate(zip(order, loads)):
        load.wait()
        if kind == "ff":
            for b in range(6):
                down[j, :, b * 128 : b * 128 + 128] = ff_in[j, pl.ds(b * 256, 256), :].astype(F32)
            send(down.at[j], wd.at[pl.ds(j * 256, 256), :])
            for b in range(2):
                up[j, :, b * 128 : b * 128 + 128] = ff_in[j, pl.ds(1536 + b * D, D), :].astype(F32)
            send(up.at[j], wu.at[:, pl.ds(j * 256, 256)])
        elif j < 3:
            for p in range(3):
                three[j, p] = at_in[j, pl.ds(p * D, D), :].astype(F32)
            send(three.at[j], wq.at[:, :, pl.ds(j * 128, 128)])
        else:
            for b in range(6):
                proj[:, b * 128 : b * 128 + 128] = at_in[j, pl.ds(b * 384, 384), :].astype(F32)
            send(proj, wp)
        if i == 4:
            sums.wait()
            for ref, row in ((mt_v, MTOK), (g1_v, N1G), (s1_v, N1S), (pb_v, PB), (g2_v, N2G),
                             (s2_v, N2S), (db_v, DB)):
                ref[...] = vec_in[row, :]
            ls_v[...] = vec_in[LS0 : LS1 + 1, :]
            for w in range(2):
                qv_v[w : w + 1, :] = vec_in[QVO : QVO + 1, w * 384 : w * 384 + 384]
                ub_v[pl.ds(w * D, D)] = vec_in[UPO + w, :]
            for pair in ((mt_v, mt), (g1_v, g1), (s1_v, s1), (qv_v, qv), (pb_v, pb), (ls_v, ls),
                         (g2_v, g2), (s2_v, s2), (ub_v, ub), (db_v, db)):
                send(*pair)
    for i, p in enumerate((p1, p2)):
        loads[10 + i].wait()
        send(rows_in.at[i], p)
    for store in stores:
        store.wait()


def local(dp, tokens, patch_mask, mask_token, norm1_gain, norm1_shift, w_qkv, qv_bias, w_proj,
          proj_bias, layer_scales, norm2_gain, norm2_shift, w_up, up_bias, w_down, down_bias,
          cotangent):
    bits = dp.bit_length() - 1
    rows = tokens.shape[0]
    scratch = {**layer_scratch(rows), **link_scratch(bits)}
    hbm = pl.BlockSpec(memory_space=pl.ANY)
    shape = jax.ShapeDtypeStruct
    out, gtok, ff, at, vec = pl.pallas_call(
        functools.partial(layer_kernel, bits, rows, INPUTS + OUTPUTS + tuple(scratch)),
        name="layer",
        in_specs=[hbm] * 17,
        out_specs=[hbm] * 5,
        out_shape=[
            shape((rows, D), BF16),
            shape((rows, D), BF16),
            shape((6, FF_ROWS, 128), BF16),
            shape((4, AT_ROWS, 128), BF16),
            shape((NVEC, D), F32),
        ],
        scratch_shapes=list(scratch.values()),
        compiler_params=pltpu.CompilerParams(
            collective_id=0, has_side_effects=True, vmem_limit_bytes=63 * 2**20),
        cost_estimate=pl.CostEstimate(
            flops=27 * 10**9, bytes_accessed=20 * 10**6, transcendentals=10**7),
    )(
        tokens, patch_mask, mask_token, norm1_gain, norm1_shift, qv_bias, proj_bias,
        layer_scales, norm2_gain, norm2_shift, up_bias, down_bias, cotangent, w_qkv, w_proj,
        w_up, w_down,
    )
    one, flat = shape((D,), F32), pltpu.VMEM((D,), F32)
    out, gtok, wu, wd, wq, wp, mt, g1, s1, qv, pb, ls, g2, s2, ub, db = pl.pallas_call(
        finish_kernel,
        name="finish",
        in_specs=[hbm] * 5,
        out_specs=[hbm] * 16,
        out_shape=[
            shape((rows, D), BF16), shape((rows, D), BF16),
            shape((D, 1536), F32), shape((1536, D), F32), shape((3, D, 384), F32),
            shape((384, D), F32), one, one, one, shape((2, 384), F32), one, shape((2, D), F32),
            one, one, shape((2 * D,), F32), one,
        ],
        scratch_shapes=[
            pltpu.VMEM((6, FF_ROWS, 128), BF16), pltpu.VMEM((4, AT_ROWS, 128), BF16),
            pltpu.VMEM((NVEC, D), F32), pltpu.VMEM((2, rows, D), BF16),
            pltpu.VMEM((6, D, 256), F32), pltpu.VMEM((6, 256, D), F32),
            pltpu.VMEM((3, 3, D, 128), F32), pltpu.VMEM((384, D), F32),
            flat, flat, flat, pltpu.VMEM((2, 384), F32), flat, pltpu.VMEM((2, D), F32), flat, flat,
            pltpu.VMEM((2 * D,), F32), flat,
            pltpu.SemaphoreType.DMA((13,)), pltpu.SemaphoreType.DMA((28,)),
        ],
        compiler_params=pltpu.CompilerParams(vmem_limit_bytes=62 * 2**20),
    )(ff, at, vec, out, gtok)
    return out, gtok, mt, g1, s1, wq, qv, wp, pb, ls, g2, s2, wu, ub, wd, db


def solution(mesh):
    rows2, both = P(("dp", "tensor"), None), P(("dp", "tensor"))
    return jax.shard_map(
        functools.partial(local, mesh.shape["dp"]),
        mesh=mesh,
        in_specs=(
            rows2, both, P(), P(), P(), P(None, None, "tensor"), P(None, "tensor"),
            P("tensor", None), P(), P(), P(), P(), P(None, "tensor"), P("tensor"),
            P("tensor", None), P(), rows2,
        ),
        out_specs=(
            rows2, rows2, P(), P(), P(), P(None, None, "tensor"), P(None, "tensor"),
            P("tensor", None), P(), P(), P(), P(), P(None, "tensor"), P("tensor"),
            P("tensor", None), P(),
        ),
        check_vma=False,
    )
```
